512 devices in a mesh: frame: 32 (over z, core), head: 16 (over x, y).
Axes of the slice: x: 4, y: 4, z: 16, core: 2. Of those that a mesh axis runs over, the one named last changes fastest.
Arguments:
- queries: bfloat16 [16384, 4096], P('frame', 'head'), may hold values from -6 to 6
- key_rows: bfloat16 [16384, 4096], P('frame', 'head'), may hold values from -6 to 6
- values: bfloat16 [16384, 4096], P('frame', 'head'), may hold values from -6 to 6
- gate_init: float32 [32, 128, 128], P('head'), may hold values from -0.5 to 0.5
- up_init: float32 [32, 128, 128], P('head'), may hold values from -0.5 to 0.5
- down_init: float32 [32, 128, 128], P('head'), may hold values from -0.5 to 0.5
- step_size: float32 [32], P('head'), may hold values from 0.1 to 1
- head_scale: float32 [32], P('head'), may hold values from 0.25 to 4
- out_gain: float32 [4096], P('head'), may hold values from 0.5 to 1.5
Outputs:
- layer_out: bfloat16 [16384, 4096], P('frame', 'head')
The draws below stay inside these ranges and needn't reach their ends.
All inputs are finite; a program needn't handle non-finite values.
Results may differ from the reference program's by a relative error of at most 0.012.
The reference program's roundings to bfloat16 on the way (of `probs`, `attended`, `query_norm` and `fast_out`) count: a program that leaves them out, or rounds other values in their place, can miss the bound.
Values may be sent and summed in bfloat16 or wider, within the bound.
No kernel may reach another device: no remote copies, remote signals or barrier semaphores. Data moves between devices by JAX's collectives and lax.ppermute only.
A program may use at most 64 MiB of HBM per device.

```python
import math
import jax
import jax.numpy as jnp
from jax import lax

DH = 128
FWH = 128
FT = 512
NS_ITERS = 5
GROUPS = 2
HEADS = 32
TOKENS = 16384
N_FRAME = 32


def drawn_pair(key):
    base = jax.random.fold_in(key, 4111)
    width = HEADS * DH
    shape = (TOKENS, width)
    query_draw = jnp.clip(jax.random.normal(jax.random.fold_in(base, 1), shape, jnp.float32), -4.0, 4.0)
    key_draw = jnp.clip(jax.random.normal(jax.random.fold_in(base, 2), shape, jnp.float32), -4.0, 4.0)
    return (query_draw, key_draw)


def draw_queries(key, part):
    return drawn_pair(key)[0].astype(jnp.bfloat16)


def draw_key_rows(key, part):
    return drawn_pair(key)[1].astype(jnp.bfloat16)


def block_levels(key, dims, pieces, low, high):
    loudness = 1.0
    for axis_at, shards_of in pieces:
        steps = jax.random.uniform(jax.random.fold_in(jax.random.fold_in(key, 6), axis_at), (shards_of,), jnp.float32, low / len(pieces), high / len(pieces))
        loudness = loudness * jnp.repeat(jnp.exp(steps), dims[axis_at] // shards_of).reshape((-1,) + (1,) * (len(dims) - 1 - axis_at))
    return loudness


def centred(rng, dims, scale, limit, split=(), kind=jnp.bfloat16):
    values = scale * jax.random.normal(rng, dims, jnp.float32)
    if split:
        values = values * block_levels(rng, dims, split, -0.22, 0.18)
    return jnp.clip(values, -limit, limit).astype(kind)


def setup_inputs(seed: int = 0) -> dict:
    splits = jax.random.split(jax.random.key(seed), 10)
    queries = draw_queries(jax.random.fold_in(splits[9], 71), 0)
    key_rows = draw_key_rows(jax.random.fold_in(splits[9], 71), 0)
    values = centred(splits[2], (TOKENS, HEADS * DH), 1.0, 6.0, ((0, 32), (1, 16)))
    gate_init = centred(splits[3], (HEADS, DH, FWH), DH ** -0.5, 0.5, ((0, 16),), jnp.float32)
    up_init = centred(splits[4], (HEADS, DH, FWH), DH ** -0.5, 0.5, ((0, 16),), jnp.float32)
    down_init = centred(splits[5], (HEADS, FWH, DH), FWH ** -0.5, 0.5, ((0, 16),), jnp.float32)
    step_size = jnp.clip(jnp.exp(math.log(1.0) - 2.3025851 * jax.random.uniform(splits[6], (HEADS,), jnp.float32) ** block_levels(splits[6], (HEADS,), ((0, 16),), -0.2, 0.2)), 0.1, 1.0)
    head_scale = jnp.clip(jnp.exp(math.log(4.0) - 2.7725887 * jax.random.uniform(splits[7], (HEADS,), jnp.float32) ** block_levels(splits[7], (HEADS,), ((0, 16),), -0.2, 0.2)), 0.25, 4.0)
    out_gain = jnp.clip(1.0 + 0.1 * jax.random.normal(splits[8], (HEADS * DH,), jnp.float32), 0.5, 1.5)
    return {"queries": queries, "key_rows": key_rows, "values": values, "gate_init": gate_init, "up_init": up_init, "down_init": down_init, "step_size": step_size, "head_scale": head_scale, "out_gain": out_gain}


quintic_terms = (3.4445, -4.775, 2.0315)
highest = lax.Precision.HIGHEST

def rms_scale(rows_in, epsilon):
    mean_square = lax.optimization_barrier(jnp.mean(rows_in * rows_in, axis=-1, keepdims=True))
    return rows_in * lax.rsqrt(mean_square + epsilon)

def newton_schulz(gradient):
    flipped = gradient.shape[1] > gradient.shape[2]
    matrix = jnp.swapaxes(gradient, 1, 2) if flipped else gradient
    frobenius = jnp.sqrt(lax.optimization_barrier(jnp.sum(matrix * matrix, axis=(1, 2), keepdims=True)))
    matrix = matrix / (frobenius + 1e-07)
    for repeat_no in range(NS_ITERS):
        square = jnp.einsum('hij,hkj->hik', matrix, matrix, precision=highest)
        quartic = jnp.einsum('hij,hjk->hik', square, square, precision=highest)
        mixing = quintic_terms[1] * square + quintic_terms[2] * quartic
        matrix = quintic_terms[0] * matrix + jnp.einsum('hij,hjk->hik', mixing, matrix, precision=highest)
    return jnp.swapaxes(matrix, 1, 2) if flipped else matrix

def column_norms(weight):
    return jnp.sqrt(lax.optimization_barrier(jnp.sum(weight * weight, axis=1, keepdims=True)))

def fast_grads(weights, key_part, value_part):
    gate_w, up_w, down_w = weights
    key_f = key_part.astype(jnp.float32)
    value_f = value_part.astype(jnp.float32)
    gate = jnp.einsum('nhd,hdf->nhf', key_f, gate_w, precision=highest)
    upward = jnp.einsum('nhd,hdf->nhf', key_f, up_w, precision=highest)
    sigma = jax.nn.sigmoid(gate)
    active = gate * sigma
    hidden = active * upward
    back_hidden = -jnp.einsum('nhd,hfd->nhf', value_f, down_w, precision=highest)
    grad_down = -jnp.einsum('nhf,nhd->hfd', hidden, value_f, precision=highest)
    back_gate = back_hidden * upward * sigma * (1.0 + gate * (1.0 - sigma))
    back_up = back_hidden * active
    grad_gate = jnp.einsum('nhd,nhf->hdf', key_f, back_gate, precision=highest)
    grad_up = jnp.einsum('nhd,nhf->hdf', key_f, back_up, precision=highest)
    return (grad_gate, grad_up, grad_down)

def renewed(weights, gradients, step_size, targets):
    result = []
    for weight, gradient, target in zip(weights, gradients, targets):
        moved = weight - step_size[:, None, None] * newton_schulz(gradient)
        length = jnp.sqrt(lax.optimization_barrier(jnp.sum(moved * moved, axis=1, keepdims=True)))
        result.append(moved * (target / (length + 1e-06)))
    return tuple(result)

def fast_apply(weights, query_part, head_scale):
    gate_w, up_w, down_w = weights
    query_f = query_part.astype(jnp.float32)
    gate = jnp.einsum('nhd,hdf->nhf', query_f, gate_w, precision=highest)
    upward = jnp.einsum('nhd,hdf->nhf', query_f, up_w, precision=highest)
    hidden = jax.nn.silu(gate) * upward
    output = jnp.einsum('nhf,hfd->nhd', hidden, down_w, precision=highest)
    return (output * head_scale[None, :, None]).astype(jnp.bfloat16)

def reference(queries, key_rows, values, gate_init, up_init, down_init, step_size, head_scale, out_gain):
    frames = N_FRAME
    heads = HEADS
    grid_q = queries.reshape(frames, FT, heads, DH).transpose(0, 2, 1, 3)
    grid_k = key_rows.reshape(frames, FT, heads, DH).transpose(0, 2, 1, 3)
    grid_v = values.reshape(frames, FT, heads, DH).transpose(0, 2, 1, 3)
    score_scale = 1.0 / math.sqrt(DH)
    column = lax.broadcasted_iota(jnp.int32, (1, 2 * FT), 1)

    def one_pair(index):
        frame_no = index // heads
        head_no = index % heads
        prev_no = jnp.maximum(frame_no - 1, 0)
        query_part = grid_q[frame_no, head_no].astype(jnp.float32)
        key_all = jnp.concatenate([grid_k[prev_no, head_no], grid_k[frame_no, head_no]], axis=0).astype(jnp.float32)
        value_all = jnp.concatenate([grid_v[prev_no, head_no], grid_v[frame_no, head_no]], axis=0).astype(jnp.float32)
        scores = jnp.einsum('qd,kd->qk', query_part, key_all) * score_scale
        masked = jnp.logical_and(frame_no == 0, column < FT)
        scores = jnp.where(masked, -1e+30, scores)
        probs = jax.nn.softmax(scores, axis=-1).astype(jnp.bfloat16)
        probs = lax.optimization_barrier(probs).astype(jnp.float32)
        mixed = jnp.einsum('qk,kd->qd', probs, value_all)
        return rms_scale(mixed, 1e-06).astype(jnp.bfloat16)
    attended = lax.map(one_pair, jnp.arange(frames * heads, dtype=jnp.int32))
    attended = attended.reshape(frames, heads, FT, DH).transpose(0, 2, 1, 3).reshape(TOKENS, heads, DH)
    query_norm = rms_scale(queries.astype(jnp.float32).reshape(TOKENS, heads, DH), 1e-06).astype(jnp.bfloat16)
    value_grid = values.reshape(TOKENS, heads, DH)
    seg_len = TOKENS // GROUPS

    def per_head(packed):
        key_h, query_h, value_h, gate_w, up_w, down_w, step_h, scale_h = packed
        weights = (gate_w[None], up_w[None], down_w[None])
        targets = tuple((column_norms(weight) for weight in weights))
        outputs = []
        for segment in range(GROUPS):
            lower = segment * seg_len
            upper = lower + seg_len
            gradients = fast_grads(weights, key_h[lower:upper][:, None], value_h[lower:upper][:, None])
            weights = renewed(weights, gradients, step_h[None], targets)
            outputs.append(fast_apply(weights, query_h[lower:upper][:, None], scale_h[None])[:, 0])
        return jnp.concatenate(outputs, axis=0)
    fast_out = lax.map(per_head, (attended.transpose(1, 0, 2), query_norm.transpose(1, 0, 2), value_grid.transpose(1, 0, 2), gate_init, up_init, down_init, step_size, head_scale))
    fast_out = fast_out.transpose(1, 0, 2).reshape(TOKENS, heads * DH)
    combined = attended.reshape(TOKENS, heads * DH).astype(jnp.float32) + fast_out.astype(jnp.float32)
    total = lax.optimization_barrier(jnp.mean(combined * combined, axis=1, keepdims=True))
    return (combined * lax.rsqrt(total + 1e-05) * out_gain[None, :]).astype(jnp.bfloat16)
```

```python
import math

import jax
import jax.numpy as jnp
from jax import lax
from jax.experimental import pallas as pl
from jax.experimental.pallas import tpu as pltpu
from jax.sharding import PartitionSpec as P

NS_ITERS = 5
quintic_terms = (3.4445, -4.775, 2.0315)
f32, bf16 = jnp.float32, jnp.bfloat16
WIRE = f32

inside = (((1,), (0,)), ((), ()))
across = (((1,), (1,)), ((), ()))


def dot(a, b, dims):
    return lax.dot_general(a, b, dims, preferred_element_type=f32)


def parts_of(matrix):
    high = matrix.astype(bf16)
    low = (matrix - high.astype(f32)).astype(bf16)
    return high, low


def rows2(high, low):
    return jnp.concatenate([jnp.concatenate([high, high], 1), jnp.concatenate([low, low], 1)], 0)


def cols2(high, low):
    both = jnp.concatenate([high, low], 1)
    return jnp.concatenate([both, both], 0)


def folded(wide):
    half = wide.shape[1] // 2
    return wide[:, :half] + wide[:, half:]


def newton_schulz(gradients):
    matrices = []
    for gradient in gradients:
        total = jnp.sum(jnp.sum(gradient * gradient, axis=1, keepdims=True), axis=0, keepdims=True)
        matrices.append(gradient / (jnp.sqrt(total) + 1e-07))
    for _ in range(NS_ITERS):
        split = [parts_of(matrix) for matrix in matrices]
        squares = [
            folded(dot(jnp.concatenate(pair, 1), rows2(*pair), across)) for pair in split
        ]
        halves = [parts_of(square) for square in squares]
        quartics = [
            folded(dot(jnp.concatenate(pair, 1), cols2(*pair), inside)) for pair in halves
        ]
        mixings = [
            parts_of(quintic_terms[1] * square + quintic_terms[2] * quartic)
            for square, quartic in zip(squares, quartics)
        ]
        products = [
            folded(dot(jnp.concatenate(pair, 1), cols2(*other), inside))
            for pair, other in zip(mixings, split)
        ]
        matrices = [
            quintic_terms[0] * matrix + product for matrix, product in zip(matrices, products)
        ]
    return matrices


def renewed(weights, gradients, initial, steps):
    result = []
    for no, (weight, ortho, first) in enumerate(zip(weights, newton_schulz(gradients), initial)):
        axis = 1 if no % 3 == 2 else 0
        moved = weight - steps[no // 3] * ortho
        target = jnp.sqrt(jnp.sum(first * first, axis=axis, keepdims=True))
        length = jnp.sqrt(jnp.sum(moved * moved, axis=axis, keepdims=True))
        result.append(moved * (target / (length + 1e-06)))
    return result


def gate_and_up(rows, gate_w, up_w):
    gate_parts, up_parts = parts_of(gate_w), parts_of(up_w)
    stacked = jnp.concatenate(
        [jnp.concatenate([gate_parts[i], up_parts[i]], 1) for i in range(2)], 0
    )
    both = dot(jnp.concatenate([rows, rows], 1), stacked, inside)
    dim = gate_w.shape[1]
    return both[:, :dim], both[:, dim:]


def fast_grads(weights, key, value):
    gate_w, up_w, down_t = weights
    gate, upward = gate_and_up(key, gate_w, up_w)
    sigma = 1.0 / (1.0 + jnp.exp(-gate))
    active = gate * sigma
    hidden = active * upward
    back = dot(jnp.concatenate([value, value], 1), jnp.concatenate(parts_of(down_t), 0), inside)
    back_gate = back * upward * sigma * (1.0 + gate * (1.0 - sigma))
    back_up = back * active
    gate_parts, up_parts, hidden_parts = parts_of(back_gate), parts_of(back_up), parts_of(hidden)
    key_t, value_t = key.T, value.T
    dim = key.shape[1]
    both = dot(key_t, jnp.concatenate([gate_parts[0], up_parts[0]], 1), inside)
    both = both + dot(key_t, jnp.concatenate([gate_parts[1], up_parts[1]], 1), inside)
    down = folded(dot(value_t, jnp.concatenate(hidden_parts, 1), inside))
    return -both[:, :dim], -both[:, dim:], -down


def initial_of(gate_ref, up_ref, down_ref):
    weights = []
    for head_no in range(gate_ref.shape[0]):
        weights += [gate_ref[head_no], up_ref[head_no], down_ref[head_no].T]
    return weights


def store_matrices(ref, first, matrices):
    for no, matrix in enumerate(matrices):
        rows = matrix.shape[0]
        ref[(first + no) * rows : (first + no + 1) * rows, :] = matrix.astype(ref.dtype)


def load_matrices(ref, dim):
    return [
        ref[no * dim : (no + 1) * dim, :].astype(f32) for no in range(ref.shape[0] // dim)
    ]


def attend_kernel(
    flags, q_ref, kp_ref, k_ref, vp_ref, v_ref, gate_ref, up_ref, down_ref, att_ref, grad_ref
):
    heads, dim = gate_ref.shape[0], gate_ref.shape[1]
    frame_len = q_ref.shape[0]
    rows = 128
    scale = math.log2(math.e) / math.sqrt(dim)
    bias = jnp.where(flags[0] == 0, -1e30, 0.0).astype(f32)
    weights = initial_of(gate_ref, up_ref, down_ref)
    for head_no in range(heads):
        cols = slice(head_no * dim, (head_no + 1) * dim)
        for block in range(frame_len // rows):
            here = slice(block * rows, (block + 1) * rows)
            query = q_ref[here, cols]
            before = dot(query, kp_ref[:, cols], across) + bias
            within = dot(query, k_ref[:, cols], across)
            top = jnp.maximum(
                jnp.max(before, axis=1, keepdims=True), jnp.max(within, axis=1, keepdims=True)
            )
            before = jnp.exp2((before - top) * scale)
            within = jnp.exp2((within - top) * scale)
            total = jnp.sum(before, axis=1, keepdims=True) + jnp.sum(within, axis=1, keepdims=True)
            share = 1.0 / total
            mixed = dot((before * share).astype(bf16), vp_ref[:, cols], inside)
            mixed = mixed + dot((within * share).astype(bf16), v_ref[:, cols], inside)
            square = jnp.mean(mixed * mixed, axis=1, keepdims=True)
            att_ref[here, cols] = (mixed * lax.rsqrt(square + 1e-06)).astype(bf16)
        grads = fast_grads(
            weights[3 * head_no : 3 * head_no + 3], att_ref[:, cols], v_ref[:, cols]
        )
        store_matrices(grad_ref, 3 * head_no, grads)


def second_kernel(
    step_ref, total_ref, att_ref, v_ref, gate_ref, up_ref, down_ref, weight_ref, grad_ref
):
    heads, dim = gate_ref.shape[0], gate_ref.shape[1]
    initial = initial_of(gate_ref, up_ref, down_ref)
    steps = [step_ref[head_no] for head_no in range(heads)]
    weights = renewed(initial, load_matrices(total_ref, dim), initial, steps)
    store_matrices(weight_ref, 0, weights)
    for head_no in range(heads):
        cols = slice(head_no * dim, (head_no + 1) * dim)
        grads = fast_grads(
            weights[3 * head_no : 3 * head_no + 3], att_ref[:, cols], v_ref[:, cols]
        )
        store_matrices(grad_ref, 3 * head_no, grads)


def apply_kernel(
    flags,
    step_ref,
    scale_ref,
    total_ref,
    weight_ref,
    att_ref,
    q_ref,
    gate_ref,
    up_ref,
    down_ref,
    comb_ref,
    square_ref,
):
    heads, dim = gate_ref.shape[0], gate_ref.shape[1]
    initial = initial_of(gate_ref, up_ref, down_ref)
    steps = [step_ref[head_no] for head_no in range(heads)]
    earlier = load_matrices(weight_ref, dim)
    weights = renewed(earlier, load_matrices(total_ref, dim), initial, steps)
    late = flags[1] != 0
    weights = [jnp.where(late, new, old) for new, old in zip(weights, earlier)]
    for head_no in range(heads):
        cols = slice(head_no * dim, (head_no + 1) * dim)
        gate_w, up_w, down_t = weights[3 * head_no : 3 * head_no + 3]
        query = q_ref[:, cols].astype(f32)
        square = jnp.mean(query * query, axis=1, keepdims=True)
        query = (query * lax.rsqrt(square + 1e-06)).astype(bf16)
        gate, upward = gate_and_up(query, gate_w, up_w)
        hidden = gate / (1.0 + jnp.exp(-gate)) * upward
        output = folded(
            dot(jnp.concatenate(parts_of(hidden), 1), rows2(*parts_of(down_t)), across)
        )
        fast_out = (output * scale_ref[head_no]).astype(bf16)
        comb_ref[:, cols] = att_ref[:, cols].astype(f32) + fast_out.astype(f32)
    combined = comb_ref[...]
    square = combined * combined
    ones = jnp.ones((8, square.shape[1]), bf16)
    high, low = parts_of(square)
    square_ref[...] = dot(ones, high, across) + dot(ones, low, across)


def final_kernel(square_ref, comb_ref, gain_ref, out_ref, *, features):
    ones = jnp.ones((square_ref.shape[0], 128), bf16)
    squares = square_ref[...]
    high, low = parts_of(squares)
    first = (((0,), (0,)), ((), ()))
    total = dot(high, ones, first) + dot(low, ones, first)
    scale = lax.rsqrt(total / features + 1e-05)
    for no in range(comb_ref.shape[1] // 128):
        cols = slice(no * 128, (no + 1) * 128)
        out_ref[:, cols] = (comb_ref[:, cols] * scale * gain_ref[:, cols]).astype(bf16)


def call(kernel, outs, *args, smem=0, flops=0):
    spec = pl.BlockSpec(memory_space=pltpu.VMEM)
    scalar = pl.BlockSpec(memory_space=pltpu.SMEM)
    shapes = [jax.ShapeDtypeStruct(*out) for out in outs]
    return pl.pallas_call(
        kernel,
        out_shape=shapes,
        in_specs=[scalar] * smem + [spec] * (len(args) - smem),
        out_specs=[spec] * len(shapes),
        compiler_params=pltpu.CompilerParams(vmem_limit_bytes=40 * 2**20),
    )(*args)


def exchange(array, groups):
    return lax.all_to_all(
        array, "frame", split_axis=0, concat_axis=0, tiled=True, axis_index_groups=groups
    )


def shards(
    queries, key_rows, values, gate_init, up_init, down_init, step_size, head_scale, out_gain
):
    frame_len, width = queries.shape
    heads, dim = gate_init.shape[0], gate_init.shape[1]
    frames = lax.axis_size("frame")
    position = lax.axis_index("frame")
    near = frames // 4
    near_groups = [list(range(near * i, near * i + near)) for i in range(4)]
    far_groups = [list(range(i, frames, near)) for i in range(near)]
    rows = 3 * heads * dim
    piece = rows // near
    flags = jnp.stack([position, position // (frames // 2)]).astype(jnp.int32)

    route = [(i, i + 1) for i in range(frames - 1)]
    keys_prev = lax.ppermute(key_rows, "frame", route)
    values_prev = lax.ppermute(values, "frame", route)
    attended, grads = call(
        attend_kernel,
        [((frame_len, width), bf16), ((rows, dim), WIRE)],
        flags,
        queries,
        keys_prev,
        key_rows,
        values_prev,
        values,
        gate_init,
        up_init,
        down_init,
        smem=1,
    )

    def near_sum(grads):
        return jnp.sum(exchange(grads, near_groups).reshape(near, piece, dim).astype(f32), axis=0)

    def spread(part):
        part = part.astype(WIRE)
        return exchange(
            jnp.broadcast_to(part[None], (near, piece, dim)).reshape(rows, dim), near_groups
        )

    part = near_sum(grads).astype(WIRE)
    parts = exchange(
        jnp.broadcast_to(part[None], (4, piece, dim)).reshape(4 * piece, dim), far_groups
    ).reshape(4, piece, dim)
    total = spread(parts[0].astype(f32) + parts[1].astype(f32))
    weights, grads = call(
        second_kernel,
        [((rows, dim), f32), ((rows, dim), WIRE)],
        step_size,
        total,
        attended,
        values,
        gate_init,
        up_init,
        down_init,
        smem=1,
    )
    part = near_sum(grads).astype(WIRE)
    other = lax.ppermute(part, "frame", [(i, i ^ near) for i in range(frames)])
    total = spread(part.astype(f32) + other.astype(f32))
    combined, square = call(
        apply_kernel,
        [((frame_len, width), f32), ((8, frame_len), f32)],
        flags,
        step_size,
        head_scale,
        total,
        weights,
        attended,
        queries,
        gate_init,
        up_init,
        down_init,
        smem=3,
    )
    columns = lax.axis_size("head")
    squares = lax.all_to_all(
        jnp.broadcast_to(square[:1], (columns, frame_len)),
        "head",
        split_axis=0,
        concat_axis=0,
        tiled=True,
    )
    (out,) = call(
        lambda *refs: final_kernel(*refs, features=width * columns),
        [((frame_len, width), bf16)],
        squares,
        combined,
        out_gain[None, :],
    )
    return out


def solution(mesh):
    in_specs = (
        P("frame", "head"),
        P("frame", "head"),
        P("frame", "head"),
        P("head", None, None),
        P("head", None, None),
        P("head", None, None),
        P("head"),
        P("head"),
        P("head"),
    )
    out_specs = P("frame", "head")
    return jax.shard_map(shards, mesh=mesh, in_specs=in_specs, out_specs=out_specs, check_vma=False)
```

```python
import math

import jax
import jax.numpy as jnp
from jax import lax
from jax.experimental import pallas as pl
from jax.experimental.pallas import tpu as pltpu
from jax.sharding import PartitionSpec as P

NS_ITERS = 5
quintic_terms = (3.4445, -4.775, 2.0315)
f32, bf16 = jnp.float32, jnp.bfloat16
WIRE = f32
ROWS = 128

inside = (((1,), (0,)), ((), ()))
across = (((1,), (1,)), ((), ()))


def dot(a, b, dims):
    return lax.dot_general(a, b, dims, preferred_element_type=f32)


def parts_of(matrix):
    high = matrix.astype(bf16)
    low = (matrix - high.astype(f32)).astype(bf16)
    return high, low


def rows2(high, low):
    return jnp.concatenate([jnp.concatenate([high, high], 1), jnp.concatenate([low, low], 1)], 0)


def cols2(high, low):
    both = jnp.concatenate([high, low], 1)
    return jnp.concatenate([both, both], 0)


def folded(wide):
    half = wide.shape[1] // 2
    return wide[:, :half] + wide[:, half:]


def newton_schulz(gradients):
    matrices = []
    for gradient in gradients:
        total = jnp.sum(jnp.sum(gradient * gradient, axis=1, keepdims=True), axis=0, keepdims=True)
        matrices.append(gradient / (jnp.sqrt(total) + 1e-07))
    for _ in range(NS_ITERS):
        split = [parts_of(matrix) for matrix in matrices]
        squares = [
            folded(dot(jnp.concatenate(pair, 1), rows2(*pair), across)) for pair in split
        ]
        halves = [parts_of(square) for square in squares]
        quartics = [
            folded(dot(jnp.concatenate(pair, 1), cols2(*pair), inside)) for pair in halves
        ]
        mixings = [
            parts_of(quintic_terms[1] * square + quintic_terms[2] * quartic)
            for square, quartic in zip(squares, quartics)
        ]
        products = [
            folded(dot(jnp.concatenate(pair, 1), cols2(*other), inside))
            for pair, other in zip(mixings, split)
        ]
        matrices = [
            quintic_terms[0] * matrix + product for matrix, product in zip(matrices, products)
        ]
    return matrices


def renewed(weights, gradients, initial, steps):
    result = []
    for no, (weight, ortho, first) in enumerate(zip(weights, newton_schulz(gradients), initial)):
        axis = 1 if no % 3 == 2 else 0
        moved = weight - steps[no // 3] * ortho
        target = jnp.sqrt(jnp.sum(first * first, axis=axis, keepdims=True))
        length = jnp.sqrt(jnp.sum(moved * moved, axis=axis, keepdims=True))
        result.append(moved * (target / (length + 1e-06)))
    return result


def gate_and_up(rows, gate_w, up_w):
    gate_parts, up_parts = parts_of(gate_w), parts_of(up_w)
    stacked = jnp.concatenate(
        [jnp.concatenate([gate_parts[i], up_parts[i]], 1) for i in range(2)], 0
    )
    both = dot(jnp.concatenate([rows, rows], 1), stacked, inside)
    dim = gate_w.shape[1]
    return both[:, :dim], both[:, dim:]


def fast_grads(weights, key, value):
    gate_w, up_w, down_t = weights
    gate, upward = gate_and_up(key, gate_w, up_w)
    sigma = 1.0 / (1.0 + jnp.exp(-gate))
    active = gate * sigma
    hidden = active * upward
    back = dot(jnp.concatenate([value, value], 1), jnp.concatenate(parts_of(down_t), 0), inside)
    back_gate = back * upward * sigma * (1.0 + gate * (1.0 - sigma))
    back_up = back * active
    gate_parts, up_parts, hidden_parts = parts_of(back_gate), parts_of(back_up), parts_of(hidden)
    key_t, value_t = key.T, value.T
    dim = key.shape[1]
    both = dot(key_t, jnp.concatenate([gate_parts[0], up_parts[0]], 1), inside)
    both = both + dot(key_t, jnp.concatenate([gate_parts[1], up_parts[1]], 1), inside)
    down = folded(dot(value_t, jnp.concatenate(hidden_parts, 1), inside))
    return -both[:, :dim], -both[:, dim:], -down


def initial_of(weights_ref):
    heads = weights_ref.shape[0] // 3
    dim = weights_ref.shape[1]
    weights = []
    for head_no in range(heads):
        weights += [weights_ref[head_no], weights_ref[heads + head_no]]
        weights.append(weights_ref[2 * heads + head_no].T)
    return weights


def store_matrices(ref, first, matrices):
    for no, matrix in enumerate(matrices):
        rows = matrix.shape[0]
        ref[(first + no) * rows : (first + no + 1) * rows, :] = matrix.astype(ref.dtype)


def load_matrices(ref, dim):
    return [
        ref[no * dim : (no + 1) * dim, :].astype(f32) for no in range(ref.shape[0] // dim)
    ]


def within_kernel(q_ref, kv_ref, prob_ref, stat_ref):
    frame_len, width = q_ref.shape
    dim = 128
    heads = width // dim
    scale = math.log2(math.e) / math.sqrt(dim)
    for head_no in range(heads):
        cols = slice(head_no * dim, (head_no + 1) * dim)
        for block in range(frame_len // ROWS):
            here = slice(block * ROWS, (block + 1) * ROWS)
            place = slice(head_no * frame_len + block * ROWS, head_no * frame_len + (block + 1) * ROWS)
            within = dot(q_ref[here, cols], kv_ref[0:frame_len, cols], across)
            top = jnp.max(within, axis=1, keepdims=True)
            within = jnp.exp2((within - top) * scale)
            total = jnp.sum(within, axis=1, keepdims=True)
            prob_ref[place, :] = within
            stat_ref[place, 0:128] = jnp.broadcast_to(top, (ROWS, 128))
            stat_ref[place, 128:256] = jnp.broadcast_to(total, (ROWS, 128))


def attend_kernel(
    scalars, q_ref, past_ref, kv_ref, weights_ref, prob_ref, stat_ref, att_ref, grad_ref
):
    dim = weights_ref.shape[1]
    heads = weights_ref.shape[0] // 3
    frame_len = q_ref.shape[0]
    scale = math.log2(math.e) / math.sqrt(dim)
    bias = jnp.where(scalars[0] == 0, -1e30, 0.0).astype(f32)
    weights = initial_of(weights_ref)
    for head_no in range(heads):
        cols = slice(head_no * dim, (head_no + 1) * dim)
        for block in range(frame_len // ROWS):
            here = slice(block * ROWS, (block + 1) * ROWS)
            place = slice(head_no * frame_len + block * ROWS, head_no * frame_len + (block + 1) * ROWS)
            before = dot(q_ref[here, cols], past_ref[0:frame_len, cols], across) + bias
            top_within = stat_ref[place, 0:1]
            top = jnp.maximum(jnp.max(before, axis=1, keepdims=True), top_within)
            before = jnp.exp2((before - top) * scale)
            shrink = jnp.exp2((top_within - top) * scale)
            total = jnp.sum(before, axis=1, keepdims=True) + stat_ref[place, 128:129] * shrink
            share = 1.0 / total
            mixed = dot((before * share).astype(bf16), past_ref[frame_len:, cols], inside)
            within = (prob_ref[place, :] * (shrink * share)).astype(bf16)
            mixed = mixed + dot(within, kv_ref[frame_len:, cols], inside)
            square = jnp.mean(mixed * mixed, axis=1, keepdims=True)
            att_ref[here, cols] = (mixed * lax.rsqrt(square + 1e-06)).astype(bf16)
        grads = fast_grads(
            weights[3 * head_no : 3 * head_no + 3], att_ref[:, cols], kv_ref[frame_len:, cols]
        )
        store_matrices(grad_ref, 3 * head_no, grads)


def second_kernel(scalars, total_ref, att_ref, kv_ref, weights_ref, weight_ref, grad_ref):
    dim = weights_ref.shape[1]
    heads = weights_ref.shape[0] // 3
    initial = initial_of(weights_ref)
    steps = [scalars[2 + head_no] for head_no in range(heads)]
    weights = renewed(initial, load_matrices(total_ref, dim), initial, steps)
    store_matrices(weight_ref, 0, weights)
    for head_no in range(heads):
        cols = slice(head_no * dim, (head_no + 1) * dim)
        grads = fast_grads(
            weights[3 * head_no : 3 * head_no + 3], att_ref[:, cols], kv_ref[att_ref.shape[0] :, cols]
        )
        store_matrices(grad_ref, 3 * head_no, grads)


def apply_kernel(
    scalars, total_ref, weight_ref, att_ref, q_ref, weights_ref, comb_ref, square_ref
):
    dim = weights_ref.shape[1]
    heads = weights_ref.shape[0] // 3
    initial = initial_of(weights_ref)
    steps = [scalars[2 + head_no] for head_no in range(heads)]
    earlier = load_matrices(weight_ref, dim)
    weights = renewed(earlier, load_matrices(total_ref, dim), initial, steps)
    late = scalars[1] != 0
    weights = [jnp.where(late, new, old) for new, old in zip(weights, earlier)]
    for head_no in range(heads):
        cols = slice(head_no * dim, (head_no + 1) * dim)
        gate_w, up_w, down_t = weights[3 * head_no : 3 * head_no + 3]
        query = q_ref[:, cols].astype(f32)
        square = jnp.mean(query * query, axis=1, keepdims=True)
        query = (query * lax.rsqrt(square + 1e-06)).astype(bf16)
        gate, upward = gate_and_up(query, gate_w, up_w)
        hidden = gate / (1.0 + jnp.exp(-gate)) * upward
        output = folded(
            dot(jnp.concatenate(parts_of(hidden), 1), rows2(*parts_of(down_t)), across)
        )
        fast_out = (output * scalars[2 + heads + head_no]).astype(bf16)
        comb_ref[:, cols] = att_ref[:, cols].astype(f32) + fast_out.astype(f32)
    combined = comb_ref[...]
    square = combined * combined
    ones = jnp.ones((8, square.shape[1]), bf16)
    high, low = parts_of(square)
    square_ref[...] = dot(ones, high, across) + dot(ones, low, across)


def final_kernel(square_ref, comb_ref, gain_ref, out_ref, *, features):
    ones = jnp.ones((square_ref.shape[0], 128), bf16)
    squares = square_ref[...]
    high, low = parts_of(squares)
    first = (((0,), (0,)), ((), ()))
    total = dot(high, ones, first) + dot(low, ones, first)
    scale = lax.rsqrt(total / features + 1e-05)
    for no in range(comb_ref.shape[1] // 128):
        cols = slice(no * 128, (no + 1) * 128)
        out_ref[:, cols] = (comb_ref[:, cols] * scale * gain_ref[:, cols]).astype(bf16)


def call(kernel, outs, *args, scalars=0, hbm=0, scratch=(), flops=0):
    spec = pl.BlockSpec(memory_space=pltpu.VMEM)
    first = [pl.BlockSpec(memory_space=pltpu.SMEM)] * scalars
    first += [pl.BlockSpec(memory_space=pltpu.HBM)] * hbm
    shapes = [jax.ShapeDtypeStruct(*out) for out in outs]
    return pl.pallas_call(
        kernel,
        out_shape=shapes,
        in_specs=first + [spec] * (len(args) - len(first)),
        out_specs=[spec] * len(shapes),
        scratch_shapes=scratch,
        compiler_params=pltpu.CompilerParams(vmem_limit_bytes=40 * 2**20),
        cost_estimate=pl.CostEstimate(flops=flops, bytes_accessed=2**21, transcendentals=0),
    )(*args)


def exchange(array, groups):
    return lax.all_to_all(
        array, "frame", split_axis=0, concat_axis=0, tiled=True, axis_index_groups=groups
    )


def shards(
    queries, key_rows, values, gate_init, up_init, down_init, step_size, head_scale, out_gain
):
    frame_len, width = queries.shape
    heads, dim = gate_init.shape[0], gate_init.shape[1]
    frames = lax.axis_size("frame")
    position = lax.axis_index("frame")
    near = frames // 4
    near_groups = [list(range(near * i, near * i + near)) for i in range(4)]
    far_groups = [list(range(i, frames, near)) for i in range(near)]
    rows = 3 * heads * dim
    piece = rows // near
    flags = jnp.stack([position, position // (frames // 2)]).astype(f32)
    scalars = jnp.concatenate([flags, step_size, head_scale])

    route = [(i, i + 1) for i in range(frames - 1)]
    here = jnp.concatenate([key_rows, values], axis=0)
    past = lax.ppermute(here, "frame", route)
    all_weights = jnp.concatenate([gate_init, up_init, down_init], axis=0)
    probs, stats = call(
        within_kernel,
        [((heads * frame_len, frame_len), f32), ((heads * frame_len, 256), f32)],
        queries,
        here,
        flops=2 * 10**9,
    )
    attended, grads = call(
        attend_kernel,
        [((frame_len, width), bf16), ((rows, dim), WIRE)],
        scalars,
        queries,
        past,
        here,
        all_weights,
        probs,
        stats,
        scalars=1,
        flops=3 * 10**9,
    )

    def near_sum(grads):
        return jnp.sum(exchange(grads, near_groups).reshape(near, piece, dim).astype(f32), axis=0)

    def spread(part):
        part = part.astype(WIRE)
        return exchange(
            jnp.broadcast_to(part[None], (near, piece, dim)).reshape(rows, dim), near_groups
        )

    part = near_sum(grads).astype(WIRE)
    parts = exchange(
        jnp.broadcast_to(part[None], (4, piece, dim)).reshape(4 * piece, dim), far_groups
    ).reshape(4, piece, dim)
    total = spread(parts[0].astype(f32) + parts[1].astype(f32))
    weights, grads = call(
        second_kernel,
        [((rows, dim), f32), ((rows, dim), WIRE)],
        scalars,
        total,
        attended,
        here,
        all_weights,
        scalars=1,
        flops=4 * 10**9,
    )
    part = near_sum(grads).astype(WIRE)
    other = lax.ppermute(part, "frame", [(i, i ^ near) for i in range(frames)])
    total = spread(part.astype(f32) + other.astype(f32))
    combined, square = call(
        apply_kernel,
        [((frame_len, width), f32), ((8, frame_len), f32)],
        scalars,
        total,
        weights,
        attended,
        queries,
        all_weights,
        scalars=1,
        flops=4 * 10**9,
    )
    columns = lax.axis_size("head")
    squares = lax.all_to_all(
        jnp.broadcast_to(square[:1], (columns, frame_len)),
        "head",
        split_axis=0,
        concat_axis=0,
        tiled=True,
    )
    (out,) = call(
        lambda *refs: final_kernel(*refs, features=width * columns),
        [((frame_len, width), bf16)],
        squares,
        combined,
        out_gain[None, :],
    )
    return out


def solution(mesh):
    in_specs = (
        P("frame", "head"),
        P("frame", "head"),
        P("frame", "head"),
        P("head", None, None),
        P("head", None, None),
        P("head", None, None),
        P("head"),
        P("head"),
        P("head"),
    )
    out_specs = P("frame", "head")
    return jax.shard_map(shards, mesh=mesh, in_specs=in_specs, out_specs=out_specs, check_vma=False)
```

```python
import math

import jax
import jax.numpy as jnp
from jax import lax
from jax.experimental import pallas as pl
from jax.experimental.pallas import tpu as pltpu
from jax.sharding import PartitionSpec as P

NS_ITERS = 5
quintic_terms = (3.4445, -4.775, 2.0315)
f32, bf16 = jnp.float32, jnp.bfloat16
f16 = jnp.float16
TOP = 12.0
ROWS = 128

inside = (((1,), (0,)), ((), ()))
across = (((1,), (1,)), ((), ()))


def dot(a, b, dims):
    return lax.dot_general(a, b, dims, preferred_element_type=f32)


def parts_of(matrix):
    high = matrix.astype(bf16)
    low = (matrix - high.astype(f32)).astype(bf16)
    return high, low


def rows2(high, low):
    return jnp.concatenate([jnp.concatenate([high, high], 1), jnp.concatenate([low, low], 1)], 0)


def cols2(high, low):
    both = jnp.concatenate([high, low], 1)
    return jnp.concatenate([both, both], 0)


def folded(wide):
    half = wide.shape[1] // 2
    return wide[:, :half] + wide[:, half:]


def newton_schulz(gradients):
    matrices = []
    for gradient in gradients:
        total = jnp.sum(jnp.sum(gradient * gradient, axis=1, keepdims=True), axis=0, keepdims=True)
        matrices.append(gradient / (jnp.sqrt(total) + 1e-07))
    for _ in range(NS_ITERS):
        split = [parts_of(matrix) for matrix in matrices]
        squares = [
            folded(dot(jnp.concatenate(pair, 1), rows2(*pair), across)) for pair in split
        ]
        halves = [parts_of(square) for square in squares]
        quartics = [
            folded(dot(jnp.concatenate(pair, 1), cols2(*pair), inside)) for pair in halves
        ]
        mixings = [
            parts_of(quintic_terms[1] * square + quintic_terms[2] * quartic)
            for square, quartic in zip(squares, quartics)
        ]
        products = [
            folded(dot(jnp.concatenate(pair, 1), cols2(*other), inside))
            for pair, other in zip(mixings, split)
        ]
        matrices = [
            quintic_terms[0] * matrix + product for matrix, product in zip(matrices, products)
        ]
    return matrices


def renewed(weights, gradients, initial, steps):
    result = []
    for no, (weight, ortho, first) in enumerate(zip(weights, newton_schulz(gradients), initial)):
        axis = 1 if no % 3 == 2 else 0
        moved = weight - steps[no // 3] * ortho
        target = jnp.sqrt(jnp.sum(first * first, axis=axis, keepdims=True))
        length = jnp.sqrt(jnp.sum(moved * moved, axis=axis, keepdims=True))
        result.append(moved * (target / (length + 1e-06)))
    return result


def gate_and_up(rows, gate_w, up_w):
    gate_parts, up_parts = parts_of(gate_w), parts_of(up_w)
    stacked = jnp.concatenate(
        [jnp.concatenate([gate_parts[i], up_parts[i]], 1) for i in range(2)], 0
    )
    both = dot(jnp.concatenate([rows, rows], 1), stacked, inside)
    dim = gate_w.shape[1]
    return both[:, :dim], both[:, dim:]


def fast_grads(weights, key, value):
    gate_w, up_w, down_t = weights
    gate, upward = gate_and_up(key, gate_w, up_w)
    sigma = 1.0 / (1.0 + jnp.exp(-gate))
    active = gate * sigma
    hidden = active * upward
    back = dot(jnp.concatenate([value, value], 1), jnp.concatenate(parts_of(down_t), 0), inside)
    back_gate = back * upward * sigma * (1.0 + gate * (1.0 - sigma))
    back_up = back * active
    gate_parts, up_parts, hidden_parts = parts_of(back_gate), parts_of(back_up), parts_of(hidden)
    key_t, value_t = key.T, value.T
    dim = key.shape[1]
    both = dot(key_t, jnp.concatenate([gate_parts[0], up_parts[0]], 1), inside)
    both = both + dot(key_t, jnp.concatenate([gate_parts[1], up_parts[1]], 1), inside)
    down = folded(dot(value_t, jnp.concatenate(hidden_parts, 1), inside))
    return -both[:, :dim], -both[:, dim:], -down


def initial_of(weights_ref):
    heads = weights_ref.shape[0] // 3
    dim = weights_ref.shape[1]
    weights = []
    for head_no in range(heads):
        weights += [weights_ref[head_no], weights_ref[heads + head_no]]
        weights.append(weights_ref[2 * heads + head_no].T)
    return weights


def store_matrices(ref, first, matrices):
    for no, matrix in enumerate(matrices):
        rows = matrix.shape[0]
        ref[(first + no) * rows : (first + no + 1) * rows, :] = matrix.astype(ref.dtype)


def store_scaled(ref, matrices):
    dim = matrices[0].shape[0]
    piece = ref.shape[1] - 8
    unit = math.gcd(piece, dim)
    peak = matrices[0]
    for matrix in matrices[1:]:
        peak = jnp.maximum(jnp.abs(peak), jnp.abs(matrix))
    peak = jnp.max(jnp.max(jnp.abs(peak), axis=1, keepdims=True), axis=0, keepdims=True)
    exponent = jnp.floor(jnp.log2(jnp.maximum(peak, 1e-30)))
    factor = jnp.exp2(TOP - exponent)
    for no, matrix in enumerate(matrices):
        for step in range(dim // unit):
            row = no * dim + step * unit
            place = slice(row % piece, row % piece + unit)
            ref[row // piece, place, :] = matrix[step * unit : (step + 1) * unit, :] * factor
    for no in range(ref.shape[0]):
        ref[no, piece:, :] = jnp.broadcast_to(exponent, (8, dim))


def load_matrices(ref, dim):
    return [
        ref[no * dim : (no + 1) * dim, :].astype(f32) for no in range(ref.shape[0] // dim)
    ]


def combine_kernel(*refs):
    parts, out_ref = refs[:-1], refs[-1]
    piece = out_ref.shape[0] - 8
    terms = [(ref, no) for ref in parts for no in range(ref.shape[0])]
    exponents = [ref[no, piece : piece + 1, :] for ref, no in terms]
    exponent = exponents[0]
    for other in exponents[1:]:
        exponent = jnp.maximum(exponent, other)
    exponent = exponent + float(math.ceil(math.log2(len(terms))))
    total = None
    for (ref, no), own in zip(terms, exponents):
        term = ref[no, :piece, :] * jnp.exp2(own - exponent)
        total = term if total is None else total + term
    out_ref[:piece, :] = total
    out_ref[piece:, :] = jnp.broadcast_to(exponent, (8, total.shape[1]))


def load_scaled(ref):
    piece, dim = ref.shape[1] - 8, ref.shape[2]
    unit = math.gcd(piece, dim)
    factors = [jnp.exp2(ref[no, piece : piece + 1, :] - TOP) for no in range(ref.shape[0])]
    matrices = []
    for first in range(0, ref.shape[0] * piece, dim):
        chunks = []
        for row in range(first, first + dim, unit):
            place = slice(row % piece, row % piece + unit)
            chunks.append(ref[row // piece, place, :] * factors[row // piece])
        matrices.append(jnp.concatenate(chunks, axis=0))
    return matrices


def within_kernel(q_ref, kv_ref, prob_ref, stat_ref):
    frame_len, width = q_ref.shape
    dim = 128
    heads = width // dim
    scale = math.log2(math.e) / math.sqrt(dim)
    for head_no in range(heads):
        cols = slice(head_no * dim, (head_no + 1) * dim)
        for block in range(frame_len // ROWS):
            here = slice(block * ROWS, (block + 1) * ROWS)
            place = slice(head_no * frame_len + block * ROWS, head_no * frame_len + (block + 1) * ROWS)
            within = dot(q_ref[here, cols], kv_ref[0:frame_len, cols], across)
            top = jnp.max(within, axis=1, keepdims=True)
            within = jnp.exp2((within - top) * scale)
            total = jnp.sum(within, axis=1, keepdims=True)
            prob_ref[place, :] = within
            stat_ref[place, 0:128] = jnp.broadcast_to(top, (ROWS, 128))
            stat_ref[place, 128:256] = jnp.broadcast_to(total, (ROWS, 128))


def attend_kernel(
    scalars, q_ref, past_ref, kv_ref, weights_ref, prob_ref, stat_ref, att_ref, grad_ref
):
    dim = weights_ref.shape[1]
    heads = weights_ref.shape[0] // 3
    frame_len = q_ref.shape[0]
    scale = math.log2(math.e) / math.sqrt(dim)
    bias = jnp.where(scalars[0] == 0, -1e30, 0.0).astype(f32)
    weights = initial_of(weights_ref)
    grads = []
    for head_no in range(heads):
        cols = slice(head_no * dim, (head_no + 1) * dim)
        for block in range(frame_len // ROWS):
            here = slice(block * ROWS, (block + 1) * ROWS)
            place = slice(head_no * frame_len + block * ROWS, head_no * frame_len + (block + 1) * ROWS)
            before = dot(q_ref[here, cols], past_ref[0:frame_len, cols], across) + bias
            top_within = stat_ref[place, 0:1]
            top = jnp.maximum(jnp.max(before, axis=1, keepdims=True), top_within)
            before = jnp.exp2((before - top) * scale)
            shrink = jnp.exp2((top_within - top) * scale)
            total = jnp.sum(before, axis=1, keepdims=True) + stat_ref[place, 128:129] * shrink
            share = 1.0 / total
            mixed = dot((before * share).astype(bf16), past_ref[frame_len:, cols], inside)
            within = (prob_ref[place, :] * (shrink * share)).astype(bf16)
            mixed = mixed + dot(within, kv_ref[frame_len:, cols], inside)
            square = jnp.mean(mixed * mixed, axis=1, keepdims=True)
            att_ref[here, cols] = (mixed * lax.rsqrt(square + 1e-06)).astype(bf16)
        grads += fast_grads(
            weights[3 * head_no : 3 * head_no + 3], att_ref[:, cols], kv_ref[frame_len:, cols]
        )
    store_scaled(grad_ref, grads)


def second_kernel(scalars, total_ref, att_ref, kv_ref, weights_ref, weight_ref, grad_ref):
    dim = weights_ref.shape[1]
    heads = weights_ref.shape[0] // 3
    initial = initial_of(weights_ref)
    steps = [scalars[2 + head_no] for head_no in range(heads)]
    weights = renewed(initial, load_scaled(total_ref), initial, steps)
    store_matrices(weight_ref, 0, weights)
    grads = []
    for head_no in range(heads):
        cols = slice(head_no * dim, (head_no + 1) * dim)
        grads += fast_grads(
            weights[3 * head_no : 3 * head_no + 3],
            att_ref[:, cols],
            kv_ref[att_ref.shape[0] :, cols],
        )
    store_scaled(grad_ref, grads)


def apply_kernel(
    scalars, total_ref, weight_ref, att_ref, q_ref, weights_ref, comb_ref, square_ref
):
    dim = weights_ref.shape[1]
    heads = weights_ref.shape[0] // 3
    initial = initial_of(weights_ref)
    steps = [scalars[2 + head_no] for head_no in range(heads)]
    earlier = load_matrices(weight_ref, dim)
    weights = renewed(earlier, load_scaled(total_ref), initial, steps)
    late = scalars[1] != 0
    weights = [jnp.where(late, new, old) for new, old in zip(weights, earlier)]
    for head_no in range(heads):
        cols = slice(head_no * dim, (head_no + 1) * dim)
        gate_w, up_w, down_t = weights[3 * head_no : 3 * head_no + 3]
        query = q_ref[:, cols].astype(f32)
        square = jnp.mean(query * query, axis=1, keepdims=True)
        query = (query * lax.rsqrt(square + 1e-06)).astype(bf16)
        gate, upward = gate_and_up(query, gate_w, up_w)
        hidden = gate / (1.0 + jnp.exp(-gate)) * upward
        output = folded(
            dot(jnp.concatenate(parts_of(hidden), 1), rows2(*parts_of(down_t)), across)
        )
        fast_out = (output * scalars[2 + heads + head_no]).astype(bf16)
        comb_ref[:, cols] = att_ref[:, cols].astype(f32) + fast_out.astype(f32)
    combined = comb_ref[...]
    square = combined * combined
    ones = jnp.ones((8, square.shape[1]), bf16)
    high, low = parts_of(square)
    square_ref[...] = dot(ones, high, across) + dot(ones, low, across)


def final_kernel(square_ref, comb_ref, gain_ref, out_ref, *, features):
    ones = jnp.ones((square_ref.shape[0], 128), bf16)
    squares = square_ref[...]
    high, low = parts_of(squares)
    first = (((0,), (0,)), ((), ()))
    total = dot(high, ones, first) + dot(low, ones, first)
    scale = lax.rsqrt(total / features + 1e-05)
    for no in range(comb_ref.shape[1] // 128):
        cols = slice(no * 128, (no + 1) * 128)
        out_ref[:, cols] = (comb_ref[:, cols] * scale * gain_ref[:, cols]).astype(bf16)


def call(kernel, outs, *args, scalars=0, hbm=0, scratch=(), flops=0):
    spec = pl.BlockSpec(memory_space=pltpu.VMEM)
    first = [pl.BlockSpec(memory_space=pltpu.SMEM)] * scalars
    first += [pl.BlockSpec(memory_space=pltpu.HBM)] * hbm
    shapes = [jax.ShapeDtypeStruct(*out) for out in outs]
    return pl.pallas_call(
        kernel,
        out_shape=shapes,
        in_specs=first + [spec] * (len(args) - len(first)),
        out_specs=[spec] * len(shapes),
        scratch_shapes=scratch,
        compiler_params=pltpu.CompilerParams(vmem_limit_bytes=40 * 2**20),
        cost_estimate=pl.CostEstimate(flops=flops, bytes_accessed=2**21, transcendentals=0),
    )(*args)


def exchange(array, groups):
    return lax.all_to_all(
        array, "frame", split_axis=0, concat_axis=0, tiled=True, axis_index_groups=groups
    )


def shards(
    queries, key_rows, values, gate_init, up_init, down_init, step_size, head_scale, out_gain
):
    frame_len, width = queries.shape
    heads, dim = gate_init.shape[0], gate_init.shape[1]
    frames = lax.axis_size("frame")
    position = lax.axis_index("frame")
    near = frames // 4
    near_groups = [list(range(near * i, near * i + near)) for i in range(4)]
    far_groups = [list(range(i, frames, near)) for i in range(near)]
    rows = 3 * heads * dim
    piece = rows // near
    flags = jnp.stack([position, position // (frames // 2)]).astype(f32)
    scalars = jnp.concatenate([flags, step_size, head_scale])

    route = [(i, i + 1) for i in range(frames - 1)]
    here = jnp.concatenate([key_rows, values], axis=0)
    past = lax.ppermute(here, "frame", route)
    all_weights = jnp.concatenate([gate_init, up_init, down_init], axis=0)
    probs, stats = call(
        within_kernel,
        [((heads * frame_len, frame_len), f32), ((heads * frame_len, 256), f32)],
        queries,
        here,
        flops=2 * 10**9,
    )
    attended, grads = call(
        attend_kernel,
        [((frame_len, width), bf16), ((near, piece + 8, dim), f32)],
        scalars,
        queries,
        past,
        here,
        all_weights,
        probs,
        stats,
        scalars=1,
        flops=3 * 10**9,
    )

    def combined_of(*parts):
        return call(combine_kernel, [((piece + 8, dim), f32)], *parts)[0]

    def wired(part, copies, groups):
        part = part.astype(f16)
        if copies:
            part = jnp.broadcast_to(part[None], (copies,) + part.shape)
        return exchange(part, groups).astype(f32)

    part = combined_of(wired(grads, 0, near_groups))
    part = combined_of(wired(part, 4, far_groups)[:2])
    total = wired(part, near, near_groups)
    weights, grads = call(
        second_kernel,
        [((rows, dim), f32), ((near, piece + 8, dim), f32)],
        scalars,
        total,
        attended,
        here,
        all_weights,
        scalars=1,
        flops=4 * 10**9,
    )
    part = combined_of(wired(grads, 0, near_groups))
    other = lax.ppermute(part, "frame", [(i, i ^ near) for i in range(frames)])
    part = combined_of(part[None], other[None])
    total = wired(part, near, near_groups)
    combined, square = call(
        apply_kernel,
        [((frame_len, width), f32), ((8, frame_len), f32)],
        scalars,
        total,
        weights,
        attended,
        queries,
        all_weights,
        scalars=1,
        flops=4 * 10**9,
    )
    columns = lax.axis_size("head")
    squares = lax.all_to_all(
        jnp.broadcast_to(square[:1], (columns, frame_len)),
        "head",
        split_axis=0,
        concat_axis=0,
        tiled=True,
    )
    (out,) = call(
        lambda *refs: final_kernel(*refs, features=width * columns),
        [((frame_len, width), bf16)],
        squares,
        combined,
        out_gain[None, :],
    )
    return out


def solution(mesh):
    in_specs = (
        P("frame", "head"),
        P("frame", "head"),
        P("frame", "head"),
        P("head", None, None),
        P("head", None, None),
        P("head", None, None),
        P("head"),
        P("head"),
        P("head"),
    )
    out_specs = P("frame", "head")
    return jax.shard_map(shards, mesh=mesh, in_specs=in_specs, out_specs=out_specs, check_vma=False)
```

```python
import math

import jax
import jax.numpy as jnp
from jax import lax
from jax.experimental import pallas as pl
from jax.experimental.pallas import tpu as pltpu
from jax.sharding import PartitionSpec as P

NS_ITERS = 5
quintic_terms = (3.4445, -4.775, 2.0315)
f32, bf16 = jnp.float32, jnp.bfloat16
f16 = jnp.float16
TOP = 12.0

inside = (((1,), (0,)), ((), ()))
across = (((1,), (1,)), ((), ()))


def dot(a, b, dims):
    return lax.dot_general(a, b, dims, preferred_element_type=f32)


def parts_of(matrix):
    high = matrix.astype(bf16)
    low = (matrix - high.astype(f32)).astype(bf16)
    return high, low


def folded(wide):
    half = wide.shape[1] // 2
    return wide[:, :half] + wide[:, half:]


def product(left, right, dims):
    both = jnp.concatenate(right, 0 if dims == across else 1)
    return folded(dot(left[0], both, dims)) + dot(left[1], right[0], dims)


def newton_schulz(gradients):
    matrices = []
    for gradient in gradients:
        total = jnp.sum(jnp.sum(gradient * gradient, axis=1, keepdims=True), axis=0, keepdims=True)
        matrices.append(gradient / (jnp.sqrt(total) + 1e-07))
    for _ in range(NS_ITERS):
        split = [parts_of(matrix) for matrix in matrices]
        squares = [product(pair, pair, across) for pair in split]
        halves = [parts_of(square) for square in squares]
        quartics = [product(pair, pair, inside) for pair in halves]
        mixings = [
            parts_of(quintic_terms[1] * square + quintic_terms[2] * quartic)
            for square, quartic in zip(squares, quartics)
        ]
        products = [product(pair, other, inside) for pair, other in zip(mixings, split)]
        matrices = [
            quintic_terms[0] * matrix + product for matrix, product in zip(matrices, products)
        ]
    return matrices


def renewed(weights, gradients, initial, steps):
    result = []
    for no, (weight, ortho, first) in enumerate(zip(weights, newton_schulz(gradients), initial)):
        axis = 1 if no % 3 == 2 else 0
        moved = weight - steps[no // 3] * ortho
        target = jnp.sqrt(jnp.sum(first * first, axis=axis, keepdims=True))
        length = jnp.sqrt(jnp.sum(moved * moved, axis=axis, keepdims=True))
        result.append(moved * (target / (length + 1e-06)))
    return result


def gate_and_up(rows, gate_w, up_w):
    gate_parts, up_parts = parts_of(gate_w), parts_of(up_w)
    stacked = jnp.concatenate(
        [jnp.concatenate([gate_parts[i], up_parts[i]], 1) for i in range(2)], 0
    )
    both = dot(jnp.concatenate([rows, rows], 1), stacked, inside)
    dim = gate_w.shape[1]
    return both[:, :dim], both[:, dim:]


def fast_grads(weights, key, value, key_t, value_t):
    gate_w, up_w, down_t = weights
    gate, upward = gate_and_up(key, gate_w, up_w)
    sigma = 1.0 / (1.0 + jnp.exp(-gate))
    active = gate * sigma
    hidden = active * upward
    back = dot(jnp.concatenate([value, value], 1), jnp.concatenate(parts_of(down_t), 0), inside)
    back_gate = back * upward * sigma * (1.0 + gate * (1.0 - sigma))
    back_up = back * active
    gate_parts, up_parts, hidden_parts = parts_of(back_gate), parts_of(back_up), parts_of(hidden)
    dim = key.shape[1]
    both = dot(key_t, jnp.concatenate([gate_parts[0], up_parts[0]], 1), inside)
    both = both + dot(key_t, jnp.concatenate([gate_parts[1], up_parts[1]], 1), inside)
    down = folded(dot(value_t, jnp.concatenate(hidden_parts, 1), inside))
    return -both[:, :dim], -both[:, dim:], -down


def initial_of(weights_ref):
    return [weights_ref[no] for no in range(weights_ref.shape[0])]


def store_matrices(ref, first, matrices):
    for no, matrix in enumerate(matrices):
        rows = matrix.shape[0]
        ref[(first + no) * rows : (first + no + 1) * rows, :] = matrix.astype(ref.dtype)


def store_scaled(ref, matrices):
    dim = matrices[0].shape[0]
    piece = ref.shape[1] - 8
    unit = math.gcd(piece, dim)
    peak = matrices[0]
    for matrix in matrices[1:]:
        peak = jnp.maximum(jnp.abs(peak), jnp.abs(matrix))
    peak = jnp.max(jnp.max(jnp.abs(peak), axis=1, keepdims=True), axis=0, keepdims=True)
    exponent = jnp.floor(jnp.log2(jnp.maximum(peak, 1e-30)))
    factor = jnp.exp2(TOP - exponent)
    for no, matrix in enumerate(matrices):
        for step in range(dim // unit):
            row = no * dim + step * unit
            place = slice(row % piece, row % piece + unit)
            ref[row // piece, place, :] = matrix[step * unit : (step + 1) * unit, :] * factor
    for no in range(ref.shape[0]):
        ref[no, piece:, :] = jnp.broadcast_to(exponent, (8, dim))


def load_matrices(ref, dim):
    return [
        ref[no * dim : (no + 1) * dim, :].astype(f32) for no in range(ref.shape[0] // dim)
    ]


def combine_kernel(*refs):
    parts, out_ref = refs[:-1], refs[-1]
    piece = out_ref.shape[0] - 8
    terms = [(ref, no) for ref in parts for no in range(ref.shape[0])]
    exponents = [ref[no, piece : piece + 1, :] for ref, no in terms]
    exponent = exponents[0]
    for other in exponents[1:]:
        exponent = jnp.maximum(exponent, other)
    exponent = exponent + float(math.ceil(math.log2(len(terms))))
    total = None
    for (ref, no), own in zip(terms, exponents):
        term = ref[no, :piece, :] * jnp.exp2(own - exponent)
        total = term if total is None else total + term
    out_ref[:piece, :] = total
    out_ref[piece:, :] = jnp.broadcast_to(exponent, (8, total.shape[1]))


def load_scaled(ref):
    piece, dim = ref.shape[1] - 8, ref.shape[2]
    unit = math.gcd(piece, dim)
    factors = [jnp.exp2(ref[no, piece : piece + 1, :] - TOP) for no in range(ref.shape[0])]
    matrices = []
    for first in range(0, ref.shape[0] * piece, dim):
        chunks = []
        for row in range(first, first + dim, unit):
            place = slice(row % piece, row % piece + unit)
            chunks.append(ref[row // piece, place, :] * factors[row // piece])
        matrices.append(jnp.concatenate(chunks, axis=0))
    return matrices


def exponentials(scores, top, dim):
    return jnp.exp2((scores - top) * (math.log2(math.e) / math.sqrt(dim)))


def within_kernel(
    q_hbm,
    k_hbm,
    v_hbm,
    gate_hbm,
    up_hbm,
    down_hbm,
    q_ref,
    v_ref,
    norm_ref,
    turned_ref,
    weights_ref,
    prob_ref,
    stat_ref,
    k_ref,
    raw_ref,
    sems,
):
    heads, dim = gate_hbm.shape[0], gate_hbm.shape[1]
    frame_len = q_hbm.shape[0]
    pairs = [(q_hbm, q_ref), (k_hbm, k_ref), (v_hbm, v_ref)]
    pairs += [
        (source, raw_ref.at[no * heads : (no + 1) * heads])
        for no, source in enumerate([gate_hbm, up_hbm, down_hbm])
    ]
    copies = [
        pltpu.make_async_copy(source, target, sems.at[no])
        for no, (source, target) in enumerate(pairs)
    ]
    for copy in copies:
        copy.start()
    copies[0].wait()
    copies[1].wait()
    for head_no in range(heads):
        cols = slice(head_no * dim, (head_no + 1) * dim)
        scores = dot(k_ref[:, cols], q_ref[:, cols], across)
        top = jnp.max(scores, axis=0, keepdims=True)
        scores = exponentials(scores, top, dim)
        prob_ref[head_no] = scores
        stat_ref[head_no, 0:1, :] = top
        stat_ref[head_no, 1:2, :] = jnp.sum(scores, axis=0, keepdims=True)
        query = q_ref[:, cols].astype(f32)
        square = jnp.mean(query * query, axis=1, keepdims=True)
        norm_ref[:, cols] = (query * lax.rsqrt(square + 1e-06)).astype(bf16)
    for copy in copies[2:]:
        copy.wait()
    for head_no in range(heads):
        cols = slice(head_no * dim, (head_no + 1) * dim)
        turned_ref[head_no] = v_ref[:, cols].T
        weights_ref[3 * head_no] = raw_ref[head_no]
        weights_ref[3 * head_no + 1] = raw_ref[heads + head_no]
        weights_ref[3 * head_no + 2] = raw_ref[2 * heads + head_no].T


def probs_kernel(scalars, q_ref, past_ref, prob_ref, stat_ref, turned_ref, share_ref, mixed_ref):
    heads, dim, frame_len = turned_ref.shape
    bias = jnp.where(scalars[0] == 0, -1e30, 0.0).astype(f32)
    for head_no in range(heads):
        cols = slice(head_no * dim, (head_no + 1) * dim)
        before = dot(past_ref[:, cols], q_ref[:, cols], across) + bias
        near_top = stat_ref[head_no, 0:1, :]
        top = jnp.maximum(jnp.max(before, axis=0, keepdims=True), near_top)
        before = exponentials(before, top, dim)
        shrink = exponentials(near_top, top, dim)
        total = jnp.sum(before, axis=0, keepdims=True) + stat_ref[head_no, 1:2, :] * shrink
        share = 1.0 / total
        share_ref[head_no] = (before * share).astype(bf16)
        within = (prob_ref[head_no] * (shrink * share)).astype(bf16)
        mixed_ref[head_no] = dot(turned_ref[head_no], within, inside)


def attend_kernel(
    share_ref, mixed_ref, past_ref, v_ref, turned_ref, weights_ref, att_ref, att_t_ref, grad_ref
):
    heads, dim, frame_len = turned_ref.shape
    weights = initial_of(weights_ref)
    grads = []
    for head_no in range(heads):
        cols = slice(head_no * dim, (head_no + 1) * dim)
        mixed = mixed_ref[head_no] + dot(past_ref[:, cols].T, share_ref[head_no], inside)
        square = jnp.mean(mixed * mixed, axis=0, keepdims=True)
        att_t = (mixed * lax.rsqrt(square + 1e-06)).astype(bf16)
        att = att_t.T
        att_t_ref[head_no] = att_t
        att_ref[:, cols] = att
        grads += fast_grads(
            weights[3 * head_no : 3 * head_no + 3], att, v_ref[:, cols], att_t, turned_ref[head_no]
        )
    store_scaled(grad_ref, grads)


def second_kernel(
    scalars,
    total_ref,
    att_ref,
    att_t_ref,
    v_ref,
    turned_ref,
    weights_ref,
    weight_ref,
    grad_ref,
):
    heads, dim, frame_len = turned_ref.shape
    initial = initial_of(weights_ref)
    steps = [scalars[2 + head_no] for head_no in range(heads)]
    weights = renewed(initial, load_scaled(total_ref), initial, steps)
    store_matrices(weight_ref, 0, weights)
    grads = []
    for head_no in range(heads):
        cols = slice(head_no * dim, (head_no + 1) * dim)
        grads += fast_grads(
            weights[3 * head_no : 3 * head_no + 3],
            att_ref[:, cols],
            v_ref[:, cols],
            att_t_ref[head_no],
            turned_ref[head_no],
        )
    store_scaled(grad_ref, grads)


def apply_kernel(
    scalars, total_ref, weight_ref, att_ref, norm_ref, weights_ref, comb_ref, square_ref
):
    dim = weights_ref.shape[1]
    heads = weights_ref.shape[0] // 3
    initial = initial_of(weights_ref)
    steps = [scalars[2 + head_no] for head_no in range(heads)]
    earlier = load_matrices(weight_ref, dim)
    weights = renewed(earlier, load_scaled(total_ref), initial, steps)
    late = scalars[1] != 0
    weights = [jnp.where(late, new, old) for new, old in zip(weights, earlier)]
    for head_no in range(heads):
        cols = slice(head_no * dim, (head_no + 1) * dim)
        gate_w, up_w, down_t = weights[3 * head_no : 3 * head_no + 3]
        gate, upward = gate_and_up(norm_ref[:, cols], gate_w, up_w)
        hidden = gate / (1.0 + jnp.exp(-gate)) * upward
        output = product(parts_of(hidden), parts_of(down_t), across)
        fast_out = (output * scalars[2 + heads + head_no]).astype(bf16)
        comb_ref[:, cols] = att_ref[:, cols].astype(f32) + fast_out.astype(f32)
    combined = comb_ref[...]
    square = combined * combined
    ones = jnp.ones((8, square.shape[1]), bf16)
    high, low = parts_of(square)
    square_ref[...] = dot(ones, high, across) + dot(ones, low, across)


def final_kernel(square_ref, comb_ref, gain_ref, out_ref, *, features):
    ones = jnp.ones((square_ref.shape[0], 128), bf16)
    squares = square_ref[...]
    high, low = parts_of(squares)
    first = (((0,), (0,)), ((), ()))
    total = dot(high, ones, first) + dot(low, ones, first)
    scale = lax.rsqrt(total / features + 1e-05)
    for no in range(comb_ref.shape[1] // 128):
        cols = slice(no * 128, (no + 1) * 128)
        out_ref[:, cols] = (comb_ref[:, cols] * scale * gain_ref[:, cols]).astype(bf16)


def call(kernel, outs, *args, scalars=0, hbm=0, scratch=(), flops=0):
    spec = pl.BlockSpec(memory_space=pltpu.VMEM)
    first = [pl.BlockSpec(memory_space=pltpu.SMEM)] * scalars
    first += [pl.BlockSpec(memory_space=pltpu.HBM)] * hbm
    shapes = [jax.ShapeDtypeStruct(*out) for out in outs]
    args = [
        pltpu.with_memory_space_constraint(arg, pltpu.HBM) if scalars <= no < scalars + hbm else arg
        for no, arg in enumerate(args)
    ]
    return pl.pallas_call(
        kernel,
        out_shape=shapes,
        in_specs=first + [spec] * (len(args) - len(first)),
        out_specs=[spec] * len(shapes),
        scratch_shapes=scratch,
        compiler_params=pltpu.CompilerParams(vmem_limit_bytes=40 * 2**20),
        cost_estimate=pl.CostEstimate(flops=flops, bytes_accessed=2**21, transcendentals=0),
    )(*args)


def exchange(array, groups):
    return lax.all_to_all(
        array, "frame", split_axis=0, concat_axis=0, tiled=True, axis_index_groups=groups
    )


def shards(
    queries, key_rows, values, gate_init, up_init, down_init, step_size, head_scale, out_gain
):
    frame_len, width = queries.shape
    heads, dim = gate_init.shape[0], gate_init.shape[1]
    frames = lax.axis_size("frame")
    position = lax.axis_index("frame")
    near = frames // 4
    near_groups = [list(range(near * i, near * i + near)) for i in range(4)]
    far_groups = [list(range(i, frames, near)) for i in range(near)]
    rows = 3 * heads * dim
    piece = rows // near
    flags = jnp.stack([position, position // (frames // 2)]).astype(f32)
    scalars = jnp.concatenate([flags, step_size, head_scale])

    route = [(i, i + 1) for i in range(frames - 1)]
    keys_prev = lax.ppermute(key_rows, "frame", route)
    values_prev = lax.ppermute(values, "frame", route)
    turned = (heads, dim, frame_len)
    queries_v, values_v, norms, values_t, weights_v, probs, stats = call(
        within_kernel,
        [
            ((frame_len, width), bf16),
            ((frame_len, width), bf16),
            ((frame_len, width), bf16),
            (turned, bf16),
            ((3 * heads, dim, dim), f32),
            ((heads, frame_len, frame_len), f32),
            ((heads, 8, frame_len), f32),
        ],
        queries,
        key_rows,
        values,
        gate_init,
        up_init,
        down_init,
        hbm=6,
        scratch=[
            pltpu.VMEM((frame_len, width), bf16),
            pltpu.VMEM((3 * heads, dim, dim), f32),
            pltpu.SemaphoreType.DMA((6,)),
        ],
        flops=2 * 10**9,
    )
    shares, mixed = call(
        probs_kernel,
        [((heads, frame_len, frame_len), bf16), (turned, f32)],
        scalars,
        queries_v,
        keys_prev,
        probs,
        stats,
        values_t,
        scalars=1,
        flops=2 * 10**9,
    )
    attended, attended_t, grads = call(
        attend_kernel,
        [((frame_len, width), bf16), (turned, bf16), ((near, piece + 8, dim), f32)],
        shares,
        mixed,
        values_prev,
        values_v,
        values_t,
        weights_v,
        flops=3 * 10**9,
    )

    def combined_of(*parts):
        return call(combine_kernel, [((piece + 8, dim), f32)], *parts)[0]

    def wired(part, copies, groups):
        part = part.astype(f16)
        if copies:
            part = jnp.broadcast_to(part[None], (copies,) + part.shape)
        return exchange(part, groups).astype(f32)

    part = combined_of(wired(grads, 0, near_groups))
    part = combined_of(wired(part, 4, far_groups)[:2])
    total = wired(part, near, near_groups)
    weights, grads = call(
        second_kernel,
        [((rows, dim), f32), ((near, piece + 8, dim), f32)],
        scalars,
        total,
        attended,
        attended_t,
        values_v,
        values_t,
        weights_v,
        scalars=1,
        flops=4 * 10**9,
    )
    part = combined_of(wired(grads, 0, near_groups))
    other = lax.ppermute(part, "frame", [(i, i ^ near) for i in range(frames)])
    part = combined_of(part[None], other[None])
    total = wired(part, near, near_groups)
    combined, square = call(
        apply_kernel,
        [((frame_len, width), f32), ((8, frame_len), f32)],
        scalars,
        total,
        weights,
        attended,
        norms,
        weights_v,
        scalars=1,
        flops=4 * 10**9,
    )
    columns = lax.axis_size("head")
    squares = lax.all_to_all(
        jnp.broadcast_to(square[:1], (columns, frame_len)),
        "head",
        split_axis=0,
        concat_axis=0,
        tiled=True,
    )
    (out,) = call(
        lambda *refs: final_kernel(*refs, features=width * columns),
        [((frame_len, width), bf16)],
        squares,
        combined,
        out_gain[None, :],
    )
    return out


def solution(mesh):
    in_specs = (
        P("frame", "head"),
        P("frame", "head"),
        P("frame", "head"),
        P("head", None, None),
        P("head", None, None),
        P("head", None, None),
        P("head"),
        P("head"),
        P("head"),
    )
    out_specs = P("frame", "head")
    return jax.shard_map(shards, mesh=mesh, in_specs=in_specs, out_specs=out_specs, check_vma=False)
```

```python
import math

import jax
import jax.numpy as jnp
from jax import lax
from jax.experimental import pallas as pl
from jax.experimental.pallas import tpu as pltpu
from jax.sharding import PartitionSpec as P

NS_ITERS = 5
quintic_terms = (3.4445, -4.775, 2.0315)
f32, bf16 = jnp.float32, jnp.bfloat16
f16 = jnp.float16
TOP = 12.0

inside = (((1,), (0,)), ((), ()))
across = (((1,), (1,)), ((), ()))


def dot(a, b, dims):
    return lax.dot_general(a, b, dims, preferred_element_type=f32)


def parts_of(matrix):
    high = matrix.astype(bf16)
    low = (matrix - high.astype(f32)).astype(bf16)
    return high, low


def folded(wide):
    half = wide.shape[1] // 2
    return wide[:, :half] + wide[:, half:]


def product(left, right, dims):
    both = jnp.concatenate(right, 0 if dims == across else 1)
    return folded(dot(left[0], both, dims)) + dot(left[1], right[0], dims)


def newton_schulz(gradients):
    matrices = []
    for gradient in gradients:
        total = jnp.sum(jnp.sum(gradient * gradient, axis=1, keepdims=True), axis=0, keepdims=True)
        matrices.append(gradient / (jnp.sqrt(total) + 1e-07))
    for _ in range(NS_ITERS):
        split = [parts_of(matrix) for matrix in matrices]
        squares = [product(pair, pair, across) for pair in split]
        halves = [parts_of(square) for square in squares]
        quartics = [product(pair, pair, inside) for pair in halves]
        mixings = [
            parts_of(quintic_terms[1] * square + quintic_terms[2] * quartic)
            for square, quartic in zip(squares, quartics)
        ]
        products = [product(pair, other, inside) for pair, other in zip(mixings, split)]
        matrices = [
            quintic_terms[0] * matrix + product for matrix, product in zip(matrices, products)
        ]
    return matrices


def renewed(weights, gradients, initial, steps):
    result = []
    for no, (weight, ortho, first) in enumerate(zip(weights, newton_schulz(gradients), initial)):
        axis = 1 if no % 3 == 2 else 0
        moved = weight - steps[no // 3] * ortho
        target = jnp.sqrt(jnp.sum(first * first, axis=axis, keepdims=True))
        length = jnp.sqrt(jnp.sum(moved * moved, axis=axis, keepdims=True))
        result.append(moved * (target / (length + 1e-06)))
    return result


def gate_and_up(rows, gate_w, up_w):
    gate_parts, up_parts = parts_of(gate_w), parts_of(up_w)
    stacked = jnp.concatenate(
        [jnp.concatenate([gate_parts[i], up_parts[i]], 1) for i in range(2)], 0
    )
    both = dot(jnp.concatenate([rows, rows], 1), stacked, inside)
    dim = gate_w.shape[1]
    return both[:, :dim], both[:, dim:]


def fast_grads(weights, key, value, key_t, value_t):
    gate_w, up_w, down_t = weights
    gate, upward = gate_and_up(key, gate_w, up_w)
    sigma = 1.0 / (1.0 + jnp.exp(-gate))
    active = gate * sigma
    hidden = active * upward
    back = dot(jnp.concatenate([value, value], 1), jnp.concatenate(parts_of(down_t), 0), inside)
    back_gate = back * upward * sigma * (1.0 + gate * (1.0 - sigma))
    back_up = back * active
    gate_parts, up_parts, hidden_parts = parts_of(back_gate), parts_of(back_up), parts_of(hidden)
    dim = key.shape[1]
    both = dot(key_t, jnp.concatenate([gate_parts[0], up_parts[0]], 1), inside)
    both = both + dot(key_t, jnp.concatenate([gate_parts[1], up_parts[1]], 1), inside)
    down = folded(dot(value_t, jnp.concatenate(hidden_parts, 1), inside))
    return -both[:, :dim], -both[:, dim:], -down


def initial_of(weights_ref):
    return [weights_ref[no] for no in range(weights_ref.shape[0])]


def store_matrices(ref, first, matrices):
    for no, matrix in enumerate(matrices):
        rows = matrix.shape[0]
        ref[(first + no) * rows : (first + no + 1) * rows, :] = matrix.astype(ref.dtype)


def store_scaled(ref, matrices):
    dim = matrices[0].shape[0]
    piece = ref.shape[1] - 8
    unit = math.gcd(piece, dim)
    peak = matrices[0]
    for matrix in matrices[1:]:
        peak = jnp.maximum(jnp.abs(peak), jnp.abs(matrix))
    peak = jnp.max(jnp.max(jnp.abs(peak), axis=1, keepdims=True), axis=0, keepdims=True)
    exponent = jnp.floor(jnp.log2(jnp.maximum(peak, 1e-30)))
    factor = jnp.exp2(TOP - exponent)
    for no, matrix in enumerate(matrices):
        for step in range(dim // unit):
            row = no * dim + step * unit
            place = slice(row % piece, row % piece + unit)
            ref[row // piece, place, :] = matrix[step * unit : (step + 1) * unit, :] * factor
    for no in range(ref.shape[0]):
        ref[no, piece:, :] = jnp.broadcast_to(exponent, (8, dim))


def load_matrices(ref, dim):
    return [
        ref[no * dim : (no + 1) * dim, :].astype(f32) for no in range(ref.shape[0] // dim)
    ]


def combine_kernel(*refs):
    parts, out_ref = refs[:-1], refs[-1]
    piece = out_ref.shape[0] - 8
    terms = [(ref, no) for ref in parts for no in range(ref.shape[0])]
    exponents = [ref[no, piece : piece + 1, :] for ref, no in terms]
    exponent = exponents[0]
    for other in exponents[1:]:
        exponent = jnp.maximum(exponent, other)
    exponent = exponent + float(math.ceil(math.log2(len(terms))))
    total = None
    for (ref, no), own in zip(terms, exponents):
        term = ref[no, :piece, :] * jnp.exp2(own - exponent)
        total = term if total is None else total + term
    out_ref[:piece, :] = total
    out_ref[piece:, :] = jnp.broadcast_to(exponent, (8, total.shape[1]))


def load_scaled(ref):
    piece, dim = ref.shape[1] - 8, ref.shape[2]
    unit = math.gcd(piece, dim)
    factors = [jnp.exp2(ref[no, piece : piece + 1, :] - TOP) for no in range(ref.shape[0])]
    matrices = []
    for first in range(0, ref.shape[0] * piece, dim):
        chunks = []
        for row in range(first, first + dim, unit):
            place = slice(row % piece, row % piece + unit)
            chunks.append(ref[row // piece, place, :] * factors[row // piece])
        matrices.append(jnp.concatenate(chunks, axis=0))
    return matrices


def exponentials(scores, top, dim):
    return jnp.exp2((scores - top) * (math.log2(math.e) / math.sqrt(dim)))


def within_kernel(
    q_hbm,
    k_hbm,
    v_hbm,
    gate_hbm,
    up_hbm,
    down_hbm,
    q_ref,
    v_ref,
    norm_ref,
    turned_ref,
    weights_ref,
    prob_ref,
    stat_ref,
    k_ref,
    raw_ref,
    sems,
):
    heads, dim = gate_hbm.shape[0], gate_hbm.shape[1]
    frame_len = q_hbm.shape[0]
    pairs = [(q_hbm, q_ref), (k_hbm, k_ref), (v_hbm, v_ref)]
    pairs += [
        (source, raw_ref.at[no * heads : (no + 1) * heads])
        for no, source in enumerate([gate_hbm, up_hbm, down_hbm])
    ]
    copies = [
        pltpu.make_async_copy(source, target, sems.at[no])
        for no, (source, target) in enumerate(pairs)
    ]
    for copy in copies:
        copy.start()
    copies[0].wait()
    copies[1].wait()
    for head_no in range(heads):
        cols = slice(head_no * dim, (head_no + 1) * dim)
        scores = dot(k_ref[:, cols], q_ref[:, cols], across)
        top = jnp.max(scores, axis=0, keepdims=True)
        scores = exponentials(scores, top, dim)
        prob_ref[head_no] = scores
        stat_ref[head_no, 0:1, :] = top
        stat_ref[head_no, 1:2, :] = jnp.sum(scores, axis=0, keepdims=True)
        query = q_ref[:, cols].astype(f32)
        square = jnp.mean(query * query, axis=1, keepdims=True)
        norm_ref[:, cols] = (query * lax.rsqrt(square + 1e-06)).astype(bf16)
    for copy in copies[2:]:
        copy.wait()
    for head_no in range(heads):
        cols = slice(head_no * dim, (head_no + 1) * dim)
        turned_ref[head_no] = v_ref[:, cols].T
        weights_ref[3 * head_no] = raw_ref[head_no]
        weights_ref[3 * head_no + 1] = raw_ref[heads + head_no]
        weights_ref[3 * head_no + 2] = raw_ref[2 * heads + head_no].T


def probs_kernel(scalars, q_ref, past_ref, prob_ref, stat_ref, turned_ref, share_ref, mixed_ref):
    heads, dim, frame_len = turned_ref.shape
    bias = jnp.where(scalars[0] == 0, -1e30, 0.0).astype(f32)
    for head_no in range(heads):
        cols = slice(head_no * dim, (head_no + 1) * dim)
        before = dot(past_ref[:, cols], q_ref[:, cols], across) + bias
        near_top = stat_ref[head_no, 0:1, :]
        top = jnp.maximum(jnp.max(before, axis=0, keepdims=True), near_top)
        before = exponentials(before, top, dim)
        shrink = exponentials(near_top, top, dim)
        total = jnp.sum(before, axis=0, keepdims=True) + stat_ref[head_no, 1:2, :] * shrink
        share = 1.0 / total
        share_ref[head_no] = (before * share).astype(bf16)
        within = (prob_ref[head_no] * (shrink * share)).astype(bf16)
        mixed_ref[head_no] = dot(turned_ref[head_no], within, inside)


def attend_kernel(
    share_ref, mixed_ref, past_ref, v_ref, turned_ref, weights_ref, att_ref, att_t_ref, grad_ref
):
    heads, dim, frame_len = turned_ref.shape
    weights = initial_of(weights_ref)
    grads = []
    for head_no in range(heads):
        cols = slice(head_no * dim, (head_no + 1) * dim)
        mixed = mixed_ref[head_no] + dot(past_ref[:, cols].T, share_ref[head_no], inside)
        square = jnp.mean(mixed * mixed, axis=0, keepdims=True)
        att_t = (mixed * lax.rsqrt(square + 1e-06)).astype(bf16)
        att = att_t.T
        att_t_ref[head_no] = att_t
        att_ref[:, cols] = att
        grads += fast_grads(
            weights[3 * head_no : 3 * head_no + 3], att, v_ref[:, cols], att_t, turned_ref[head_no]
        )
    store_scaled(grad_ref, grads)


def second_kernel(
    scalars,
    total_ref,
    att_ref,
    att_t_ref,
    v_ref,
    turned_ref,
    weights_ref,
    weight_ref,
    grad_ref,
):
    heads, dim, frame_len = turned_ref.shape
    initial = initial_of(weights_ref)
    steps = [scalars[2 + head_no] for head_no in range(heads)]
    weights = renewed(initial, load_scaled(total_ref), initial, steps)
    store_matrices(weight_ref, 0, weights)
    grads = []
    for head_no in range(heads):
        cols = slice(head_no * dim, (head_no + 1) * dim)
        grads += fast_grads(
            weights[3 * head_no : 3 * head_no + 3],
            att_ref[:, cols],
            v_ref[:, cols],
            att_t_ref[head_no],
            turned_ref[head_no],
        )
    store_scaled(grad_ref, grads)


def late_kernel(
    scalars, weight_ref, att_ref, norm_ref, total_ref, weights_ref, comb_ref, square_ref
):
    dim = weights_ref.shape[1]
    heads = weights_ref.shape[0] // 3
    initial = initial_of(weights_ref)
    steps = [scalars[2 + head_no] for head_no in range(heads)]
    weights = renewed(load_matrices(weight_ref, dim), load_scaled(total_ref), initial, steps)
    apply_weights(weights, scalars, att_ref, norm_ref, comb_ref, square_ref)


def early_kernel(scalars, weight_ref, att_ref, norm_ref, comb_ref, square_ref):
    weights = load_matrices(weight_ref, weight_ref.shape[1])
    apply_weights(weights, scalars, att_ref, norm_ref, comb_ref, square_ref)


def apply_weights(weights, scalars, att_ref, norm_ref, comb_ref, square_ref):
    heads, dim = len(weights) // 3, weights[0].shape[0]
    for head_no in range(heads):
        cols = slice(head_no * dim, (head_no + 1) * dim)
        gate_w, up_w, down_t = weights[3 * head_no : 3 * head_no + 3]
        gate, upward = gate_and_up(norm_ref[:, cols], gate_w, up_w)
        hidden = gate / (1.0 + jnp.exp(-gate)) * upward
        output = product(parts_of(hidden), parts_of(down_t), across)
        fast_out = (output * scalars[2 + heads + head_no]).astype(bf16)
        comb_ref[:, cols] = att_ref[:, cols].astype(f32) + fast_out.astype(f32)
    combined = comb_ref[...]
    square = combined * combined
    ones = jnp.ones((8, square.shape[1]), bf16)
    high, low = parts_of(square)
    square_ref[...] = dot(ones, high, across) + dot(ones, low, across)


def final_kernel(square_ref, comb_ref, gain_ref, out_ref, *, features):
    ones = jnp.ones((square_ref.shape[0], 128), bf16)
    squares = square_ref[...]
    high, low = parts_of(squares)
    first = (((0,), (0,)), ((), ()))
    total = dot(high, ones, first) + dot(low, ones, first)
    scale = lax.rsqrt(total / features + 1e-05)
    for no in range(comb_ref.shape[1] // 128):
        cols = slice(no * 128, (no + 1) * 128)
        out_ref[:, cols] = (comb_ref[:, cols] * scale * gain_ref[:, cols]).astype(bf16)


def call(kernel, outs, *args, scalars=0, hbm=0, scratch=(), flops=0):
    spec = pl.BlockSpec(memory_space=pltpu.VMEM)
    first = [pl.BlockSpec(memory_space=pltpu.SMEM)] * scalars
    first += [pl.BlockSpec(memory_space=pltpu.HBM)] * hbm
    shapes = [jax.ShapeDtypeStruct(*out) for out in outs]
    args = [
        pltpu.with_memory_space_constraint(arg, pltpu.HBM) if scalars <= no < scalars + hbm else arg
        for no, arg in enumerate(args)
    ]
    return pl.pallas_call(
        kernel,
        out_shape=shapes,
        in_specs=first + [spec] * (len(args) - len(first)),
        out_specs=[spec] * len(shapes),
        scratch_shapes=scratch,
        compiler_params=pltpu.CompilerParams(vmem_limit_bytes=40 * 2**20),
        cost_estimate=pl.CostEstimate(flops=flops, bytes_accessed=2**21, transcendentals=0),
    )(*args)


def exchange(array, groups):
    return lax.all_to_all(
        array, "frame", split_axis=0, concat_axis=0, tiled=True, axis_index_groups=groups
    )


def shards(
    queries, key_rows, values, gate_init, up_init, down_init, step_size, head_scale, out_gain
):
    frame_len, width = queries.shape
    heads, dim = gate_init.shape[0], gate_init.shape[1]
    frames = lax.axis_size("frame")
    position = lax.axis_index("frame")
    near = frames // 4
    near_groups = [list(range(near * i, near * i + near)) for i in range(4)]
    far_groups = [list(range(i, frames, near)) for i in range(near)]
    rows = 3 * heads * dim
    piece = rows // near
    flags = jnp.stack([position, position]).astype(f32)
    scalars = jnp.concatenate([flags, step_size, head_scale])

    route = [(i, i + 1) for i in range(frames - 1)]
    keys_prev = lax.ppermute(key_rows, "frame", route)
    values_prev = lax.ppermute(values, "frame", route)
    turned = (heads, dim, frame_len)
    queries_v, values_v, norms, values_t, weights_v, probs, stats = call(
        within_kernel,
        [
            ((frame_len, width), bf16),
            ((frame_len, width), bf16),
            ((frame_len, width), bf16),
            (turned, bf16),
            ((3 * heads, dim, dim), f32),
            ((heads, frame_len, frame_len), f32),
            ((heads, 8, frame_len), f32),
        ],
        queries,
        key_rows,
        values,
        gate_init,
        up_init,
        down_init,
        hbm=6,
        scratch=[
            pltpu.VMEM((frame_len, width), bf16),
            pltpu.VMEM((3 * heads, dim, dim), f32),
            pltpu.SemaphoreType.DMA((6,)),
        ],
        flops=2 * 10**9,
    )
    shares, mixed = call(
        probs_kernel,
        [((heads, frame_len, frame_len), bf16), (turned, f32)],
        scalars,
        queries_v,
        keys_prev,
        probs,
        stats,
        values_t,
        scalars=1,
        flops=2 * 10**9,
    )
    attended, attended_t, grads = call(
        attend_kernel,
        [((frame_len, width), bf16), (turned, bf16), ((near, piece + 8, dim), f32)],
        shares,
        mixed,
        values_prev,
        values_v,
        values_t,
        weights_v,
        flops=3 * 10**9,
    )

    def combined_of(*parts):
        return call(combine_kernel, [((piece + 8, dim), f32)], *parts)[0]

    def wired(part, copies, groups):
        part = part.astype(f16)
        if copies:
            part = jnp.broadcast_to(part[None], (copies,) + part.shape)
        return exchange(part, groups).astype(f32)

    late = position >= frames // 2
    part = lax.cond(
        late,
        lambda grads: jnp.zeros((piece + 8, dim), f32),
        lambda grads: combined_of(wired(grads, 0, near_groups)),
        grads,
    )
    part = combined_of(wired(part, 4, far_groups)[:2])
    total = wired(part, near, near_groups)
    weights, grads = call(
        second_kernel,
        [((rows, dim), f32), ((near, piece + 8, dim), f32)],
        scalars,
        total,
        attended,
        attended_t,
        values_v,
        values_t,
        weights_v,
        scalars=1,
        flops=4 * 10**9,
    )
    results = [((frame_len, width), f32), ((8, frame_len), f32)]

    def with_second_sum(scalars, weights, attended, norms, grads, weights_v):
        part = combined_of(wired(grads, 0, near_groups))
        other = lax.ppermute(part, "frame", [(i, i ^ near) for i in range(frames)])
        part = combined_of(part[None], other[None])
        total = wired(part, near, near_groups)
        return call(
            late_kernel,
            results,
            scalars,
            weights,
            attended,
            norms,
            total,
            weights_v,
            scalars=1,
            flops=4 * 10**9,
        )

    def with_first_sum(scalars, weights, attended, norms, grads, weights_v):
        return call(
            early_kernel,
            results,
            scalars,
            weights,
            attended,
            norms,
            scalars=1,
            flops=10**9,
        )

    combined, square = lax.cond(
        late,
        with_second_sum,
        with_first_sum,
        scalars,
        weights,
        attended,
        norms,
        grads,
        weights_v,
    )
    columns = lax.axis_size("head")
    squares = lax.all_to_all(
        jnp.broadcast_to(square[:1], (columns, frame_len)),
        "head",
        split_axis=0,
        concat_axis=0,
        tiled=True,
    )
    (out,) = call(
        lambda *refs: final_kernel(*refs, features=width * columns),
        [((frame_len, width), bf16)],
        squares,
        combined,
        out_gain[None, :],
    )
    return out


def solution(mesh):
    in_specs = (
        P("frame", "head"),
        P("frame", "head"),
        P("frame", "head"),
        P("head", None, None),
        P("head", None, None),
        P("head", None, None),
        P("head"),
        P("head"),
        P("head"),
    )
    out_specs = P("frame", "head")
    return jax.shard_map(shards, mesh=mesh, in_specs=in_specs, out_specs=out_specs, check_vma=False)
```

```python
import math

import jax
import jax.numpy as jnp
from jax import lax
from jax.experimental import pallas as pl
from jax.experimental.pallas import tpu as pltpu
from jax.sharding import PartitionSpec as P

NS_ITERS = 5
quintic_terms = (3.4445, -4.775, 2.0315)
f32, bf16 = jnp.float32, jnp.bfloat16
f16 = jnp.float16
TOP = 12.0

inside = (((1,), (0,)), ((), ()))
across = (((1,), (1,)), ((), ()))


def dot(a, b, dims):
    return lax.dot_general(a, b, dims, preferred_element_type=f32)


def parts_of(matrix):
    high = matrix.astype(bf16)
    low = (matrix - high.astype(f32)).astype(bf16)
    return high, low


def folded(wide):
    half = wide.shape[1] // 2
    return wide[:, :half] + wide[:, half:]


def product(left, right, dims):
    both = jnp.concatenate(right, 0 if dims == across else 1)
    return folded(dot(left[0], both, dims)) + dot(left[1], right[0], dims)


def newton_schulz(gradients):
    matrices = []
    for gradient in gradients:
        total = jnp.sum(jnp.sum(gradient * gradient, axis=1, keepdims=True), axis=0, keepdims=True)
        matrices.append(gradient / (jnp.sqrt(total) + 1e-07))
    for _ in range(NS_ITERS):
        split = [parts_of(matrix) for matrix in matrices]
        squares = [product(pair, pair, across) for pair in split]
        halves = [parts_of(square) for square in squares]
        quartics = [product(pair, pair, inside) for pair in halves]
        mixings = [
            parts_of(quintic_terms[1] * square + quintic_terms[2] * quartic)
            for square, quartic in zip(squares, quartics)
        ]
        products = [product(pair, other, inside) for pair, other in zip(mixings, split)]
        matrices = [
            quintic_terms[0] * matrix + product for matrix, product in zip(matrices, products)
        ]
    return matrices


def renewed(weights, gradients, initial, steps):
    result = []
    for no, (weight, ortho, first) in enumerate(zip(weights, newton_schulz(gradients), initial)):
        axis = 1 if no % 3 == 2 else 0
        moved = weight - steps[no // 3] * ortho
        target = jnp.sqrt(jnp.sum(first * first, axis=axis, keepdims=True))
        length = jnp.sqrt(jnp.sum(moved * moved, axis=axis, keepdims=True))
        result.append(moved * (target / (length + 1e-06)))
    return result


def gate_and_up(rows, gate_w, up_w):
    gate_parts, up_parts = parts_of(gate_w), parts_of(up_w)
    stacked = jnp.concatenate(
        [jnp.concatenate([gate_parts[i], up_parts[i]], 1) for i in range(2)], 0
    )
    both = dot(jnp.concatenate([rows, rows], 1), stacked, inside)
    dim = gate_w.shape[1]
    return both[:, :dim], both[:, dim:]


def fast_grads(weights, key, value, key_t, value_t):
    gate_w, up_w, down_t = weights
    gate, upward = gate_and_up(key, gate_w, up_w)
    sigma = 1.0 / (1.0 + jnp.exp(-gate))
    active = gate * sigma
    hidden = active * upward
    back = dot(jnp.concatenate([value, value], 1), jnp.concatenate(parts_of(down_t), 0), inside)
    back_gate = back * upward * sigma * (1.0 + gate * (1.0 - sigma))
    back_up = back * active
    gate_parts, up_parts, hidden_parts = parts_of(back_gate), parts_of(back_up), parts_of(hidden)
    dim = key.shape[1]
    both = dot(key_t, jnp.concatenate([gate_parts[0], up_parts[0]], 1), inside)
    both = both + dot(key_t, jnp.concatenate([gate_parts[1], up_parts[1]], 1), inside)
    down = folded(dot(value_t, jnp.concatenate(hidden_parts, 1), inside))
    return -both[:, :dim], -both[:, dim:], -down


def initial_of(weights_ref):
    return [weights_ref[no] for no in range(weights_ref.shape[0])]


def store_matrices(ref, first, matrices):
    for no, matrix in enumerate(matrices):
        rows = matrix.shape[0]
        ref[(first + no) * rows : (first + no + 1) * rows, :] = matrix.astype(ref.dtype)


def store_scaled(ref, matrices):
    dim = matrices[0].shape[0]
    piece = ref.shape[1] - 8
    unit = math.gcd(piece, dim)
    peak = matrices[0]
    for matrix in matrices[1:]:
        peak = jnp.maximum(jnp.abs(peak), jnp.abs(matrix))
    peak = jnp.max(jnp.max(jnp.abs(peak), axis=1, keepdims=True), axis=0, keepdims=True)
    exponent = jnp.floor(jnp.log2(jnp.maximum(peak, 1e-30)))
    factor = jnp.exp2(TOP - exponent)
    for no, matrix in enumerate(matrices):
        for step in range(dim // unit):
            row = no * dim + step * unit
            place = slice(row % piece, row % piece + unit)
            ref[row // piece, place, :] = matrix[step * unit : (step + 1) * unit, :] * factor
    for no in range(ref.shape[0]):
        ref[no, piece:, :] = jnp.broadcast_to(exponent, (8, dim))


def load_matrices(ref, dim):
    return [
        ref[no * dim : (no + 1) * dim, :].astype(f32) for no in range(ref.shape[0] // dim)
    ]


def combine_kernel(*refs):
    parts, out_ref = refs[:-1], refs[-1]
    piece = out_ref.shape[0] - 8
    terms = [(ref, no) for ref in parts for no in range(ref.shape[0])]
    exponents = [ref[no, piece : piece + 1, :] for ref, no in terms]
    exponent = exponents[0]
    for other in exponents[1:]:
        exponent = jnp.maximum(exponent, other)
    exponent = exponent + float(math.ceil(math.log2(len(terms))))
    total = None
    for (ref, no), own in zip(terms, exponents):
        term = ref[no, :piece, :] * jnp.exp2(own - exponent)
        total = term if total is None else total + term
    out_ref[:piece, :] = total
    out_ref[piece:, :] = jnp.broadcast_to(exponent, (8, total.shape[1]))


def load_scaled(ref):
    piece, dim = ref.shape[1] - 8, ref.shape[2]
    unit = math.gcd(piece, dim)
    factors = [jnp.exp2(ref[no, piece : piece + 1, :] - TOP) for no in range(ref.shape[0])]
    matrices = []
    for first in range(0, ref.shape[0] * piece, dim):
        chunks = []
        for row in range(first, first + dim, unit):
            place = slice(row % piece, row % piece + unit)
            chunks.append(ref[row // piece, place, :] * factors[row // piece])
        matrices.append(jnp.concatenate(chunks, axis=0))
    return matrices


def exponentials(scores, top, dim):
    return jnp.exp2((scores - top) * (math.log2(math.e) / math.sqrt(dim)))


def within_kernel(
    q_hbm,
    k_hbm,
    v_hbm,
    gate_hbm,
    up_hbm,
    down_hbm,
    q_ref,
    v_ref,
    norm_ref,
    turned_ref,
    weights_ref,
    prob_ref,
    stat_ref,
    k_ref,
    raw_ref,
    sems,
):
    heads, dim = gate_hbm.shape[0], gate_hbm.shape[1]
    frame_len = q_hbm.shape[0]
    pairs = [(q_hbm, q_ref), (k_hbm, k_ref), (v_hbm, v_ref)]
    pairs += [
        (source, raw_ref.at[no * heads : (no + 1) * heads])
        for no, source in enumerate([gate_hbm, up_hbm, down_hbm])
    ]
    copies = [
        pltpu.make_async_copy(source, target, sems.at[no])
        for no, (source, target) in enumerate(pairs)
    ]
    for copy in copies:
        copy.start()
    copies[0].wait()
    copies[1].wait()
    for head_no in range(heads):
        cols = slice(head_no * dim, (head_no + 1) * dim)
        scores = dot(k_ref[:, cols], q_ref[:, cols], across)
        top = jnp.max(scores, axis=0, keepdims=True)
        scores = exponentials(scores, top, dim)
        prob_ref[head_no] = scores
        stat_ref[head_no, 0:1, :] = top
        stat_ref[head_no, 1:2, :] = jnp.sum(scores, axis=0, keepdims=True)
        query = q_ref[:, cols].astype(f32)
        square = jnp.mean(query * query, axis=1, keepdims=True)
        norm_ref[:, cols] = (query * lax.rsqrt(square + 1e-06)).astype(bf16)
    for copy in copies[2:]:
        copy.wait()
    for head_no in range(heads):
        cols = slice(head_no * dim, (head_no + 1) * dim)
        turned_ref[head_no] = v_ref[:, cols].T
        weights_ref[3 * head_no] = raw_ref[head_no]
        weights_ref[3 * head_no + 1] = raw_ref[heads + head_no]
        weights_ref[3 * head_no + 2] = raw_ref[2 * heads + head_no].T


def probs_kernel(scalars, q_ref, past_ref, prob_ref, stat_ref, turned_ref, share_ref, mixed_ref):
    heads, dim, frame_len = turned_ref.shape
    bias = jnp.where(scalars[0] == 0, -1e30, 0.0).astype(f32)
    for head_no in range(heads):
        cols = slice(head_no * dim, (head_no + 1) * dim)
        before = dot(past_ref[:, cols], q_ref[:, cols], across) + bias
        near_top = stat_ref[head_no, 0:1, :]
        top = jnp.maximum(jnp.max(before, axis=0, keepdims=True), near_top)
        before = exponentials(before, top, dim)
        shrink = exponentials(near_top, top, dim)
        total = jnp.sum(before, axis=0, keepdims=True) + stat_ref[head_no, 1:2, :] * shrink
        share = 1.0 / total
        share_ref[head_no] = (before * share).astype(bf16)
        within = (prob_ref[head_no] * (shrink * share)).astype(bf16)
        mixed_ref[head_no] = dot(turned_ref[head_no], within, inside)


def attend_kernel(
    share_ref, mixed_ref, past_ref, v_ref, turned_ref, weights_ref, att_ref, att_t_ref, grad_ref
):
    heads, dim, frame_len = turned_ref.shape
    weights = initial_of(weights_ref)
    grads = []
    for head_no in range(heads):
        cols = slice(head_no * dim, (head_no + 1) * dim)
        mixed = mixed_ref[head_no] + dot(past_ref[:, cols].T, share_ref[head_no], inside)
        square = jnp.mean(mixed * mixed, axis=0, keepdims=True)
        att_t = (mixed * lax.rsqrt(square + 1e-06)).astype(bf16)
        att = att_t.T
        att_t_ref[head_no] = att_t
        att_ref[:, cols] = att
        grads += fast_grads(
            weights[3 * head_no : 3 * head_no + 3], att, v_ref[:, cols], att_t, turned_ref[head_no]
        )
    store_scaled(grad_ref, grads)


def second_kernel(
    scalars,
    total_ref,
    att_ref,
    att_t_ref,
    v_ref,
    turned_ref,
    weights_ref,
    weight_ref,
    grad_ref,
):
    heads, dim, frame_len = turned_ref.shape
    initial = initial_of(weights_ref)
    steps = [scalars[2 + head_no] for head_no in range(heads)]
    weights = renewed(initial, load_scaled(total_ref), initial, steps)
    store_matrices(weight_ref, 0, weights)
    grads = []
    for head_no in range(heads):
        cols = slice(head_no * dim, (head_no + 1) * dim)
        grads += fast_grads(
            weights[3 * head_no : 3 * head_no + 3],
            att_ref[:, cols],
            v_ref[:, cols],
            att_t_ref[head_no],
            turned_ref[head_no],
        )
    store_scaled(grad_ref, grads)


def late_kernel(
    scalars, weight_ref, att_ref, norm_ref, total_ref, weights_ref, comb_ref, square_ref
):
    dim = weights_ref.shape[1]
    heads = weights_ref.shape[0] // 3
    initial = initial_of(weights_ref)
    steps = [scalars[2 + head_no] for head_no in range(heads)]
    weights = renewed(load_matrices(weight_ref, dim), load_scaled(total_ref), initial, steps)
    apply_weights(weights, scalars, att_ref, norm_ref, comb_ref, square_ref)


def early_kernel(scalars, weight_ref, att_ref, norm_ref, comb_ref, square_ref):
    weights = load_matrices(weight_ref, weight_ref.shape[1])
    apply_weights(weights, scalars, att_ref, norm_ref, comb_ref, square_ref)


def apply_weights(weights, scalars, att_ref, norm_ref, comb_ref, square_ref):
    heads, dim = len(weights) // 3, weights[0].shape[0]
    for head_no in range(heads):
        cols = slice(head_no * dim, (head_no + 1) * dim)
        gate_w, up_w, down_t = weights[3 * head_no : 3 * head_no + 3]
        gate, upward = gate_and_up(norm_ref[:, cols], gate_w, up_w)
        hidden = gate / (1.0 + jnp.exp(-gate)) * upward
        output = product(parts_of(hidden), parts_of(down_t), across)
        fast_out = (output * scalars[2 + heads + head_no]).astype(bf16)
        comb_ref[:, cols] = att_ref[:, cols].astype(f32) + fast_out.astype(f32)
    combined = comb_ref[...]
    square = combined * combined
    ones = jnp.ones((8, square.shape[1]), bf16)
    high, low = parts_of(square)
    square_ref[...] = dot(ones, high, across) + dot(ones, low, across)


def final_kernel(square_ref, comb_ref, gain_ref, out_ref, *, features):
    ones = jnp.ones((square_ref.shape[0], 128), bf16)
    squares = square_ref[...]
    high, low = parts_of(squares)
    first = (((0,), (0,)), ((), ()))
    total = dot(high, ones, first) + dot(low, ones, first)
    scale = lax.rsqrt(total / features + 1e-05)
    for no in range(comb_ref.shape[1] // 128):
        cols = slice(no * 128, (no + 1) * 128)
        out_ref[:, cols] = (comb_ref[:, cols] * scale * gain_ref[:, cols]).astype(bf16)


def call(kernel, outs, *args, scalars=0, hbm=0, scratch=(), flops=0):
    spec = pl.BlockSpec(memory_space=pltpu.VMEM)
    first = [pl.BlockSpec(memory_space=pltpu.SMEM)] * scalars
    first += [pl.BlockSpec(memory_space=pltpu.HBM)] * hbm
    shapes = [jax.ShapeDtypeStruct(*out) for out in outs]
    args = [
        pltpu.with_memory_space_constraint(arg, pltpu.HBM) if scalars <= no < scalars + hbm else arg
        for no, arg in enumerate(args)
    ]
    return pl.pallas_call(
        kernel,
        out_shape=shapes,
        in_specs=first + [spec] * (len(args) - len(first)),
        out_specs=[spec] * len(shapes),
        scratch_shapes=scratch,
        compiler_params=pltpu.CompilerParams(vmem_limit_bytes=40 * 2**20),
        cost_estimate=pl.CostEstimate(flops=flops, bytes_accessed=2**21, transcendentals=0),
    )(*args)


def exchange(array, groups):
    return lax.all_to_all(
        array, "frame", split_axis=0, concat_axis=0, tiled=True, axis_index_groups=groups
    )


def sum_groups(frames):
    cores, chips = 2, frames // 8
    half = chips // 2
    turned = [(i + half) % chips for i in range(chips)]
    orders = [list(range(chips)), turned, turned, list(range(chips))]
    near_groups = [
        [(group * chips + chip) * cores + core for chip in order for core in range(cores)]
        for group, order in enumerate(orders)
    ]
    far_groups = [list(members) for members in zip(*near_groups)]
    return near_groups, far_groups


def shards(
    queries, key_rows, values, gate_init, up_init, down_init, step_size, head_scale, out_gain
):
    frame_len, width = queries.shape
    heads, dim = gate_init.shape[0], gate_init.shape[1]
    frames = lax.axis_size("frame")
    position = lax.axis_index("frame")
    near = frames // 4
    near_groups, far_groups = sum_groups(frames)
    plain_groups = [list(range(near * i, near * i + near)) for i in range(4)]
    rows = 3 * heads * dim
    piece = rows // near
    flags = jnp.stack([position, position]).astype(f32)
    scalars = jnp.concatenate([flags, step_size, head_scale])

    route = [(i, i + 1) for i in range(frames - 1)]
    keys_prev = lax.ppermute(key_rows, "frame", route)
    values_prev = lax.ppermute(values, "frame", route)
    turned = (heads, dim, frame_len)
    queries_v, values_v, norms, values_t, weights_v, probs, stats = call(
        within_kernel,
        [
            ((frame_len, width), bf16),
            ((frame_len, width), bf16),
            ((frame_len, width), bf16),
            (turned, bf16),
            ((3 * heads, dim, dim), f32),
            ((heads, frame_len, frame_len), f32),
            ((heads, 8, frame_len), f32),
        ],
        queries,
        key_rows,
        values,
        gate_init,
        up_init,
        down_init,
        hbm=6,
        scratch=[
            pltpu.VMEM((frame_len, width), bf16),
            pltpu.VMEM((3 * heads, dim, dim), f32),
            pltpu.SemaphoreType.DMA((6,)),
        ],
        flops=2 * 10**9,
    )
    shares, mixed = call(
        probs_kernel,
        [((heads, frame_len, frame_len), bf16), (turned, f32)],
        scalars,
        queries_v,
        keys_prev,
        probs,
        stats,
        values_t,
        scalars=1,
        flops=2 * 10**9,
    )
    attended, attended_t, grads = call(
        attend_kernel,
        [((frame_len, width), bf16), (turned, bf16), ((near, piece + 8, dim), f32)],
        shares,
        mixed,
        values_prev,
        values_v,
        values_t,
        weights_v,
        flops=3 * 10**9,
    )

    def combined_of(*parts):
        return call(combine_kernel, [((piece + 8, dim), f32)], *parts)[0]

    def wired(part, copies, groups):
        part = part.astype(f16)
        if copies:
            part = jnp.broadcast_to(part[None], (copies,) + part.shape)
        return exchange(part, groups).astype(f32)

    late = position >= frames // 2
    part = lax.cond(
        late,
        lambda grads: jnp.zeros((piece + 8, dim), f32),
        lambda grads: combined_of(wired(grads, 0, near_groups)),
        grads,
    )
    part = combined_of(wired(part, 4, far_groups)[:2])
    total = wired(part, near, near_groups)
    weights, grads = call(
        second_kernel,
        [((rows, dim), f32), ((near, piece + 8, dim), f32)],
        scalars,
        total,
        attended,
        attended_t,
        values_v,
        values_t,
        weights_v,
        scalars=1,
        flops=4 * 10**9,
    )
    results = [((frame_len, width), f32), ((8, frame_len), f32)]

    def with_second_sum(scalars, weights, attended, norms, grads, weights_v):
        part = combined_of(wired(grads, 0, plain_groups))
        pairs = [(i, i ^ near) for i in range(frames // 2, frames)]
        other = lax.ppermute(part.astype(f16), "frame", pairs).astype(f32)
        part = combined_of(part[None], other[None])
        total = wired(part, near, plain_groups)
        return call(
            late_kernel,
            results,
            scalars,
            weights,
            attended,
            norms,
            total,
            weights_v,
            scalars=1,
            flops=4 * 10**9,
        )

    def with_first_sum(scalars, weights, attended, norms, grads, weights_v):
        return call(
            early_kernel,
            results,
            scalars,
            weights,
            attended,
            norms,
            scalars=1,
            flops=10**9,
        )

    combined, square = lax.cond(
        late,
        with_second_sum,
        with_first_sum,
        scalars,
        weights,
        attended,
        norms,
        grads,
        weights_v,
    )
    columns = lax.axis_size("head")
    squares = lax.all_to_all(
        jnp.broadcast_to(square[:1], (columns, frame_len)),
        "head",
        split_axis=0,
        concat_axis=0,
        tiled=True,
    )
    (out,) = call(
        lambda *refs: final_kernel(*refs, features=width * columns),
        [((frame_len, width), bf16)],
        squares,
        combined,
        out_gain[None, :],
    )
    return out


def solution(mesh):
    in_specs = (
        P("frame", "head"),
        P("frame", "head"),
        P("frame", "head"),
        P("head", None, None),
        P("head", None, None),
        P("head", None, None),
        P("head"),
        P("head"),
        P("head"),
    )
    out_specs = P("frame", "head")
    return jax.shard_map(shards, mesh=mesh, in_specs=in_specs, out_specs=out_specs, check_vma=False)
```

```python
import math

import jax
import jax.numpy as jnp
from jax import lax
from jax.experimental import pallas as pl
from jax.experimental.pallas import tpu as pltpu
from jax.sharding import PartitionSpec as P

NS_ITERS = 5
quintic_terms = (3.4445, -4.775, 2.0315)
f32, bf16 = jnp.float32, jnp.bfloat16
f16 = jnp.float16
TOP = 12.0

inside = (((1,), (0,)), ((), ()))
across = (((1,), (1,)), ((), ()))


def dot(a, b, dims):
    return lax.dot_general(a, b, dims, preferred_element_type=f32)


def parts_of(matrix):
    high = matrix.astype(bf16)
    low = (matrix - high.astype(f32)).astype(bf16)
    return high, low


def folded(wide):
    half = wide.shape[1] // 2
    return wide[:, :half] + wide[:, half:]


def product(left, right, dims):
    both = jnp.concatenate(right, 0 if dims == across else 1)
    return folded(dot(left[0], both, dims)) + dot(left[1], right[0], dims)


def newton_schulz(gradients):
    matrices = []
    for gradient in gradients:
        total = jnp.sum(jnp.sum(gradient * gradient, axis=1, keepdims=True), axis=0, keepdims=True)
        matrices.append(gradient / (jnp.sqrt(total) + 1e-07))
    for _ in range(NS_ITERS):
        split = [parts_of(matrix) for matrix in matrices]
        squares = [product(pair, pair, across) for pair in split]
        halves = [parts_of(square) for square in squares]
        quartics = [product(pair, pair, inside) for pair in halves]
        mixings = [
            parts_of(quintic_terms[1] * square + quintic_terms[2] * quartic)
            for square, quartic in zip(squares, quartics)
        ]
        products = [product(pair, other, inside) for pair, other in zip(mixings, split)]
        matrices = [
            quintic_terms[0] * matrix + product for matrix, product in zip(matrices, products)
        ]
    return matrices


def renewed(weights, gradients, initial, steps):
    result = []
    for no, (weight, ortho, first) in enumerate(zip(weights, newton_schulz(gradients), initial)):
        axis = 1 if no % 3 == 2 else 0
        moved = weight - steps[no // 3] * ortho
        target = jnp.sqrt(jnp.sum(first * first, axis=axis, keepdims=True))
        length = jnp.sqrt(jnp.sum(moved * moved, axis=axis, keepdims=True))
        result.append(moved * (target / (length + 1e-06)))
    return result


def gate_and_up(rows, gate_w, up_w):
    gate_parts, up_parts = parts_of(gate_w), parts_of(up_w)
    stacked = jnp.concatenate(
        [jnp.concatenate([gate_parts[i], up_parts[i]], 1) for i in range(2)], 0
    )
    both = dot(jnp.concatenate([rows, rows], 1), stacked, inside)
    dim = gate_w.shape[1]
    return both[:, :dim], both[:, dim:]


def fast_grads(weights, key, value, key_t, value_t):
    gate_w, up_w, down_t = weights
    gate, upward = gate_and_up(key, gate_w, up_w)
    sigma = 1.0 / (1.0 + jnp.exp(-gate))
    active = gate * sigma
    hidden = active * upward
    back = dot(jnp.concatenate([value, value], 1), jnp.concatenate(parts_of(down_t), 0), inside)
    back_gate = back * upward * sigma * (1.0 + gate * (1.0 - sigma))
    back_up = back * active
    gate_parts, up_parts, hidden_parts = parts_of(back_gate), parts_of(back_up), parts_of(hidden)
    dim = key.shape[1]
    both = dot(key_t, jnp.concatenate([gate_parts[0], up_parts[0]], 1), inside)
    both = both + dot(key_t, jnp.concatenate([gate_parts[1], up_parts[1]], 1), inside)
    down = folded(dot(value_t, jnp.concatenate(hidden_parts, 1), inside))
    return -both[:, :dim], -both[:, dim:], -down


def initial_of(weights_ref):
    return [weights_ref[no] for no in range(weights_ref.shape[0])]


def store_matrices(ref, first, matrices):
    for no, matrix in enumerate(matrices):
        rows = matrix.shape[0]
        ref[(first + no) * rows : (first + no + 1) * rows, :] = matrix.astype(ref.dtype)


def store_scaled(ref, per_head):
    heads, dim = len(per_head), per_head[0][0].shape[0]
    piece = ref.shape[1] - 8
    unit = math.gcd(piece, dim)
    matrices = [matrix for group in per_head for matrix in group]
    peak = matrices[0]
    for matrix in matrices[1:]:
        peak = jnp.maximum(jnp.abs(peak), jnp.abs(matrix))
    peak = jnp.max(jnp.max(jnp.abs(peak), axis=1, keepdims=True), axis=0, keepdims=True)
    exponent = jnp.floor(jnp.log2(jnp.maximum(peak, 1e-30)))
    factor = jnp.exp2(TOP - exponent)
    for head_no, group in enumerate(per_head):
        for no, matrix in enumerate(group):
            for step in range(dim // unit):
                row = no * dim + step * unit
                place = slice(row % piece, row % piece + unit)
                ref[row // piece * heads + head_no, place, :] = (
                    matrix[step * unit : (step + 1) * unit, :] * factor
                )
    for no in range(ref.shape[0]):
        ref[no, piece:, :] = jnp.broadcast_to(exponent, (8, dim))


def load_matrices(ref, dim):
    return [
        ref[no * dim : (no + 1) * dim, :].astype(f32) for no in range(ref.shape[0] // dim)
    ]


def combine_kernel(*refs):
    parts, out_ref = refs[:-1], refs[-1]
    piece = out_ref.shape[0] - 8
    terms = [(ref, no) for ref in parts for no in range(ref.shape[0])]
    exponents = [ref[no, piece : piece + 1, :] for ref, no in terms]
    exponent = exponents[0]
    for other in exponents[1:]:
        exponent = jnp.maximum(exponent, other)
    exponent = exponent + float(math.ceil(math.log2(len(terms))))
    total = None
    for (ref, no), own in zip(terms, exponents):
        term = ref[no, :piece, :] * jnp.exp2(own - exponent)
        total = term if total is None else total + term
    out_ref[:piece, :] = total
    out_ref[piece:, :] = jnp.broadcast_to(exponent, (8, total.shape[1]))


def load_scaled(ref, heads):
    piece, dim = ref.shape[1] - 8, ref.shape[2]
    unit = math.gcd(piece, dim)
    factors = [jnp.exp2(ref[no, piece : piece + 1, :] - TOP) for no in range(ref.shape[0])]
    matrices = []
    for head_no in range(heads):
        for first in range(0, ref.shape[0] // heads * piece, dim):
            chunks = []
            for row in range(first, first + dim, unit):
                no = row // piece * heads + head_no
                chunks.append(ref[no, row % piece : row % piece + unit, :] * factors[no])
            matrices.append(jnp.concatenate(chunks, axis=0))
    return matrices


def exponentials(scores, top, dim):
    return jnp.exp2((scores - top) * (math.log2(math.e) / math.sqrt(dim)))


def within_kernel(
    q_hbm,
    k_hbm,
    v_hbm,
    gate_hbm,
    up_hbm,
    down_hbm,
    q_ref,
    v_ref,
    norm_ref,
    turned_ref,
    weights_ref,
    prob_ref,
    stat_ref,
    k_ref,
    raw_ref,
    sems,
):
    heads, dim = gate_hbm.shape[0], gate_hbm.shape[1]
    frame_len = q_hbm.shape[0]
    pairs = [(q_hbm, q_ref), (k_hbm, k_ref), (v_hbm, v_ref)]
    pairs += [
        (source, raw_ref.at[no * heads : (no + 1) * heads])
        for no, source in enumerate([gate_hbm, up_hbm, down_hbm])
    ]
    copies = [
        pltpu.make_async_copy(source, target, sems.at[no])
        for no, (source, target) in enumerate(pairs)
    ]
    for copy in copies:
        copy.start()
    copies[0].wait()
    copies[1].wait()
    for head_no in range(heads):
        cols = slice(head_no * dim, (head_no + 1) * dim)
        scores = dot(k_ref[:, cols], q_ref[:, cols], across)
        top = jnp.max(scores, axis=0, keepdims=True)
        scores = exponentials(scores, top, dim)
        prob_ref[head_no] = scores
        stat_ref[head_no, 0:1, :] = top
        stat_ref[head_no, 1:2, :] = jnp.sum(scores, axis=0, keepdims=True)
        query = q_ref[:, cols].astype(f32)
        square = jnp.mean(query * query, axis=1, keepdims=True)
        norm_ref[:, cols] = (query * lax.rsqrt(square + 1e-06)).astype(bf16)
    for copy in copies[2:]:
        copy.wait()
    for head_no in range(heads):
        cols = slice(head_no * dim, (head_no + 1) * dim)
        turned_ref[head_no] = v_ref[:, cols].T
        weights_ref[3 * head_no] = raw_ref[head_no]
        weights_ref[3 * head_no + 1] = raw_ref[heads + head_no]
        weights_ref[3 * head_no + 2] = raw_ref[2 * heads + head_no].T


def probs_kernel(scalars, q_ref, past_ref, prob_ref, stat_ref, turned_ref, share_ref, mixed_ref):
    heads, dim, frame_len = turned_ref.shape
    bias = jnp.where(scalars[0] == 0, -1e30, 0.0).astype(f32)
    for head_no in range(heads):
        cols = slice(head_no * dim, (head_no + 1) * dim)
        before = dot(past_ref[:, cols], q_ref[:, cols], across) + bias
        near_top = stat_ref[head_no, 0:1, :]
        top = jnp.maximum(jnp.max(before, axis=0, keepdims=True), near_top)
        before = exponentials(before, top, dim)
        shrink = exponentials(near_top, top, dim)
        total = jnp.sum(before, axis=0, keepdims=True) + stat_ref[head_no, 1:2, :] * shrink
        share = 1.0 / total
        share_ref[head_no] = (before * share).astype(bf16)
        within = (prob_ref[head_no] * (shrink * share)).astype(bf16)
        mixed_ref[head_no] = dot(turned_ref[head_no], within, inside)


def attend_kernel(
    share_ref, mixed_ref, past_ref, v_ref, turned_ref, weights_ref, att_ref, att_t_ref, grad_ref
):
    heads, dim, frame_len = turned_ref.shape
    weights = initial_of(weights_ref)
    grads = []
    for head_no in range(heads):
        cols = slice(head_no * dim, (head_no + 1) * dim)
        mixed = mixed_ref[head_no] + dot(past_ref[:, cols].T, share_ref[head_no], inside)
        square = jnp.mean(mixed * mixed, axis=0, keepdims=True)
        att_t = (mixed * lax.rsqrt(square + 1e-06)).astype(bf16)
        att = att_t.T
        att_t_ref[head_no] = att_t
        att_ref[:, cols] = att
        grads.append(
            fast_grads(
                weights[3 * head_no : 3 * head_no + 3],
                att,
                v_ref[:, cols],
                att_t,
                turned_ref[head_no],
            )
        )
    store_scaled(grad_ref, grads)


def unused_kernel(out_ref):
    out_ref[:, 0:16, :] = jnp.zeros((out_ref.shape[0], 16, out_ref.shape[2]), out_ref.dtype)


def second_kernel(
    scalars,
    total_ref,
    att_ref,
    att_t_ref,
    v_ref,
    turned_ref,
    other_ref,
    weights_ref,
    weight_ref,
    grad_ref,
):
    heads, dim, frame_len = turned_ref.shape
    initial = initial_of(weights_ref)
    steps = [scalars[2 + head_no] for head_no in range(heads)]
    weights = renewed(initial, load_scaled(total_ref, heads), initial, steps)
    store_matrices(weight_ref, 0, weights)
    first = scalars[1] == 0

    def mine(zero, one):
        return jnp.where(first, zero, one)

    def rows_of(ref, received):
        own = mine(ref[:, :dim].astype(f32), ref[:, dim:].astype(f32)).astype(bf16)
        return jnp.concatenate([own, received], axis=0)

    def columns_of(ref, received):
        own = mine(ref[0].astype(f32), ref[1].astype(f32)).astype(bf16)
        return jnp.concatenate([own, received.T], axis=1)

    grads = fast_grads(
        [mine(weights[no], weights[3 + no]) for no in range(3)],
        rows_of(att_ref, other_ref[0]),
        rows_of(v_ref, other_ref[1]),
        columns_of(att_t_ref, other_ref[0]),
        columns_of(turned_ref, other_ref[1]),
    )
    store_scaled(grad_ref, [grads])


def late_kernel(
    scalars, weight_ref, att_ref, norm_ref, total_ref, weights_ref, comb_ref, square_ref
):
    dim = weights_ref.shape[1]
    heads = weights_ref.shape[0] // 3
    initial = initial_of(weights_ref)
    steps = [scalars[2 + head_no] for head_no in range(heads)]
    weights = renewed(load_matrices(weight_ref, dim), load_scaled(total_ref, heads), initial, steps)
    apply_weights(weights, scalars, att_ref, norm_ref, comb_ref, square_ref)


def apply_weights(weights, scalars, att_ref, norm_ref, comb_ref, square_ref):
    heads, dim = len(weights) // 3, weights[0].shape[0]
    for head_no in range(heads):
        cols = slice(head_no * dim, (head_no + 1) * dim)
        gate_w, up_w, down_t = weights[3 * head_no : 3 * head_no + 3]
        gate, upward = gate_and_up(norm_ref[:, cols], gate_w, up_w)
        hidden = gate / (1.0 + jnp.exp(-gate)) * upward
        output = product(parts_of(hidden), parts_of(down_t), across)
        fast_out = (output * scalars[2 + heads + head_no]).astype(bf16)
        comb_ref[:, cols] = att_ref[:, cols].astype(f32) + fast_out.astype(f32)
    combined = comb_ref[...]
    square = combined * combined
    ones = jnp.ones((8, square.shape[1]), bf16)
    high, low = parts_of(square)
    square_ref[...] = dot(ones, high, across) + dot(ones, low, across)


def final_kernel(square_ref, comb_ref, gain_ref, out_ref, *, features):
    ones = jnp.ones((square_ref.shape[0], 128), bf16)
    squares = square_ref[...]
    high, low = parts_of(squares)
    first = (((0,), (0,)), ((), ()))
    total = dot(high, ones, first) + dot(low, ones, first)
    scale = lax.rsqrt(total / features + 1e-05)
    for no in range(comb_ref.shape[1] // 128):
        cols = slice(no * 128, (no + 1) * 128)
        out_ref[:, cols] = (comb_ref[:, cols] * scale * gain_ref[:, cols]).astype(bf16)


def call(kernel, outs, *args, scalars=0, hbm=0, scratch=(), flops=0):
    spec = pl.BlockSpec(memory_space=pltpu.VMEM)
    first = [pl.BlockSpec(memory_space=pltpu.SMEM)] * scalars
    first += [pl.BlockSpec(memory_space=pltpu.HBM)] * hbm
    shapes = [jax.ShapeDtypeStruct(*out) for out in outs]
    args = [
        pltpu.with_memory_space_constraint(arg, pltpu.HBM) if scalars <= no < scalars + hbm else arg
        for no, arg in enumerate(args)
    ]
    return pl.pallas_call(
        kernel,
        out_shape=shapes,
        in_specs=first + [spec] * (len(args) - len(first)),
        out_specs=[spec] * len(shapes),
        scratch_shapes=scratch,
        compiler_params=pltpu.CompilerParams(vmem_limit_bytes=40 * 2**20),
        cost_estimate=pl.CostEstimate(flops=flops, bytes_accessed=2**21, transcendentals=0),
    )(*args)


def exchange(array, groups):
    return lax.all_to_all(
        array, "frame", split_axis=0, concat_axis=0, tiled=True, axis_index_groups=groups
    )


def sum_groups(frames):
    cores, chips = 2, frames // 8
    half = chips // 2
    turned = [(i + half) % chips for i in range(chips)]
    orders = [list(range(chips)), turned, turned, list(range(chips))]
    near_groups = [
        [(group * chips + chip) * cores + core for chip in order for core in range(cores)]
        for group, order in enumerate(orders)
    ]
    far_groups = [list(members) for members in zip(*near_groups)]
    return near_groups, far_groups


def shards(
    queries, key_rows, values, gate_init, up_init, down_init, step_size, head_scale, out_gain
):
    frame_len, width = queries.shape
    heads, dim = gate_init.shape[0], gate_init.shape[1]
    frames = lax.axis_size("frame")
    position = lax.axis_index("frame")
    near = frames // 4
    near_groups, far_groups = sum_groups(frames)
    plain_groups = [list(range(near * i, near * i + near)) for i in range(4)]
    rows = 3 * heads * dim
    piece = rows // near
    core = position % heads
    flags = jnp.stack([position, core]).astype(f32)
    scalars = jnp.concatenate([flags, step_size, head_scale])

    route = [(i, i + 1) for i in range(frames - 1)]
    keys_prev = lax.ppermute(key_rows, "frame", route)
    values_prev = lax.ppermute(values, "frame", route)
    turned = (heads, dim, frame_len)
    queries_v, values_v, norms, values_t, weights_v, probs, stats = call(
        within_kernel,
        [
            ((frame_len, width), bf16),
            ((frame_len, width), bf16),
            ((frame_len, width), bf16),
            (turned, bf16),
            ((3 * heads, dim, dim), f32),
            ((heads, frame_len, frame_len), f32),
            ((heads, 8, frame_len), f32),
        ],
        queries,
        key_rows,
        values,
        gate_init,
        up_init,
        down_init,
        hbm=6,
        scratch=[
            pltpu.VMEM((frame_len, width), bf16),
            pltpu.VMEM((3 * heads, dim, dim), f32),
            pltpu.SemaphoreType.DMA((6,)),
        ],
        flops=2 * 10**9,
    )
    shares, mixed = call(
        probs_kernel,
        [((heads, frame_len, frame_len), bf16), (turned, f32)],
        scalars,
        queries_v,
        keys_prev,
        probs,
        stats,
        values_t,
        scalars=1,
        flops=2 * 10**9,
    )
    attended, attended_t, grads = call(
        attend_kernel,
        [((frame_len, width), bf16), (turned, bf16), ((near, piece + 8, dim), f32)],
        shares,
        mixed,
        values_prev,
        values_v,
        values_t,
        weights_v,
        flops=3 * 10**9,
    )

    def combined_of(*parts):
        return call(combine_kernel, [((piece + 8, dim), f32)], *parts)[0]

    def wired(part, copies, groups):
        part = part.astype(f16)
        if copies:
            part = jnp.broadcast_to(part[None], (copies,) + part.shape)
        return exchange(part, groups).astype(f32)

    late = position >= frames // 2
    cores = [(i, i ^ 1) for i in range(frames // 2, frames)]
    same_core = [group[core_no::heads] for group in plain_groups for core_no in range(heads)]

    def swapped(grads, attended, values):
        both = jnp.stack([attended, values])
        leaving = jnp.where(core == 0, both[:, :, dim:], both[:, :, :dim])
        return jnp.zeros((piece + 8, dim), f32), lax.ppermute(leaving, "frame", cores)

    def summed(grads, attended, values):
        part = combined_of(wired(grads, 0, near_groups))
        return part, call(unused_kernel, [((2, frame_len, dim), bf16)])[0]

    part, other_frame = lax.cond(late, swapped, summed, grads, attended, values_v)
    part = combined_of(wired(part, 4, far_groups)[:2])
    total = wired(part, near, near_groups)
    results = [((frame_len, width), f32), ((8, frame_len), f32)]

    def applied(weights, total, scalars, attended, norms, weights_v):
        return call(
            late_kernel,
            results,
            scalars,
            weights,
            attended,
            norms,
            total,
            weights_v,
            scalars=1,
            flops=4 * 10**9,
        )

    def with_second_sum(
        scalars, total, attended, attended_t, norms, values_v, values_t, other_frame, weights_v
    ):
        weights, grads = call(
            second_kernel,
            [((rows, dim), f32), ((near // heads, piece + 8, dim), f32)],
            scalars,
            total,
            attended,
            attended_t,
            values_v,
            values_t,
            other_frame,
            weights_v,
            scalars=1,
            flops=4 * 10**9,
        )
        part = combined_of(wired(grads, 0, same_core))
        pairs = [(i, i ^ near) for i in range(frames // 2, frames)]
        other = lax.ppermute(part.astype(f16), "frame", pairs).astype(f32)
        part = combined_of(part[None], other[None])
        total = wired(part, near, plain_groups)
        return applied(weights, total, scalars, attended, norms, weights_v)

    def with_first_sum(
        scalars, total, attended, attended_t, norms, values_v, values_t, other_frame, weights_v
    ):
        return applied(
            weights_v.reshape(rows, dim), total, scalars, attended, norms, weights_v
        )

    combined, square = lax.cond(
        late,
        with_second_sum,
        with_first_sum,
        scalars,
        total,
        attended,
        attended_t,
        norms,
        values_v,
        values_t,
        other_frame,
        weights_v,
    )
    columns = lax.axis_size("head")
    squares = lax.all_to_all(
        jnp.broadcast_to(square[:1], (columns, frame_len)),
        "head",
        split_axis=0,
        concat_axis=0,
        tiled=True,
    )
    (out,) = call(
        lambda *refs: final_kernel(*refs, features=width * columns),
        [((frame_len, width), bf16)],
        squares,
        combined,
        out_gain[None, :],
    )
    return out


def solution(mesh):
    in_specs = (
        P("frame", "head"),
        P("frame", "head"),
        P("frame", "head"),
        P("head", None, None),
        P("head", None, None),
        P("head", None, None),
        P("head"),
        P("head"),
        P("head"),
    )
    out_specs = P("frame", "head")
    return jax.shard_map(shards, mesh=mesh, in_specs=in_specs, out_specs=out_specs, check_vma=False)
```

```python
import math

import jax
import jax.numpy as jnp
from jax import lax
from jax.experimental import pallas as pl
from jax.experimental.pallas import tpu as pltpu
from jax.sharding import PartitionSpec as P

NS_ITERS = 5
quintic_terms = (3.4445, -4.775, 2.0315)
f32, bf16 = jnp.float32, jnp.bfloat16
f16 = jnp.float16
TOP = 12.0

inside = (((1,), (0,)), ((), ()))
across = (((1,), (1,)), ((), ()))


def dot(a, b, dims):
    return lax.dot_general(a, b, dims, preferred_element_type=f32)


def parts_of(matrix):
    high = matrix.astype(bf16)
    low = (matrix - high.astype(f32)).astype(bf16)
    return high, low


def folded(wide):
    half = wide.shape[1] // 2
    return wide[:, :half] + wide[:, half:]


def product(left, right, dims):
    both = jnp.concatenate(right, 0 if dims == across else 1)
    return folded(dot(left[0], both, dims)) + dot(left[1], right[0], dims)


def newton_schulz(gradients):
    matrices = []
    for gradient in gradients:
        total = jnp.sum(jnp.sum(gradient * gradient, axis=1, keepdims=True), axis=0, keepdims=True)
        matrices.append(gradient / (jnp.sqrt(total) + 1e-07))
    for _ in range(NS_ITERS):
        split = [parts_of(matrix) for matrix in matrices]
        squares = [product(pair, pair, across) for pair in split]
        halves = [parts_of(square) for square in squares]
        quartics = [product(pair, pair, inside) for pair in halves]
        mixings = [
            parts_of(quintic_terms[1] * square + quintic_terms[2] * quartic)
            for square, quartic in zip(squares, quartics)
        ]
        products = [product(pair, other, inside) for pair, other in zip(mixings, split)]
        matrices = [
            quintic_terms[0] * matrix + product for matrix, product in zip(matrices, products)
        ]
    return matrices


def renewed(weights, gradients, initial, steps):
    result = []
    for no, (weight, ortho, first) in enumerate(zip(weights, newton_schulz(gradients), initial)):
        axis = 1 if no % 3 == 2 else 0
        moved = weight - steps[no // 3] * ortho
        target = jnp.sqrt(jnp.sum(first * first, axis=axis, keepdims=True))
        length = jnp.sqrt(jnp.sum(moved * moved, axis=axis, keepdims=True))
        result.append(moved * (target / (length + 1e-06)))
    return result


def gate_and_up(rows, gate_w, up_w):
    gate_parts, up_parts = parts_of(gate_w), parts_of(up_w)
    stacked = jnp.concatenate(
        [jnp.concatenate([gate_parts[i], up_parts[i]], 1) for i in range(2)], 0
    )
    both = dot(jnp.concatenate([rows, rows], 1), stacked, inside)
    dim = gate_w.shape[1]
    return both[:, :dim], both[:, dim:]


def fast_grads(weights, key, value, key_t, value_t):
    gate_w, up_w, down_t = weights
    gate, upward = gate_and_up(key, gate_w, up_w)
    sigma = 1.0 / (1.0 + jnp.exp(-gate))
    active = gate * sigma
    hidden = active * upward
    back = dot(jnp.concatenate([value, value], 1), jnp.concatenate(parts_of(down_t), 0), inside)
    back_gate = back * upward * sigma * (1.0 + gate * (1.0 - sigma))
    back_up = back * active
    gate_parts, up_parts, hidden_parts = parts_of(back_gate), parts_of(back_up), parts_of(hidden)
    dim = key.shape[1]
    both = dot(key_t, jnp.concatenate([gate_parts[0], up_parts[0]], 1), inside)
    both = both + dot(key_t, jnp.concatenate([gate_parts[1], up_parts[1]], 1), inside)
    down = folded(dot(value_t, jnp.concatenate(hidden_parts, 1), inside))
    return -both[:, :dim], -both[:, dim:], -down


def initial_of(weights_ref):
    return [weights_ref[no] for no in range(weights_ref.shape[0])]


def store_matrices(ref, first, matrices):
    for no, matrix in enumerate(matrices):
        rows = matrix.shape[0]
        ref[(first + no) * rows : (first + no + 1) * rows, :] = matrix.astype(ref.dtype)


def store_scaled(ref, per_head):
    heads, dim = len(per_head), per_head[0][0].shape[0]
    piece = ref.shape[1] - 8
    unit = math.gcd(piece, dim)
    matrices = [matrix for group in per_head for matrix in group]
    peak = matrices[0]
    for matrix in matrices[1:]:
        peak = jnp.maximum(jnp.abs(peak), jnp.abs(matrix))
    peak = jnp.max(jnp.max(jnp.abs(peak), axis=1, keepdims=True), axis=0, keepdims=True)
    exponent = jnp.floor(jnp.log2(jnp.maximum(peak, 1e-30)))
    factor = jnp.exp2(TOP - exponent)
    for head_no, group in enumerate(per_head):
        for no, matrix in enumerate(group):
            for step in range(dim // unit):
                row = no * dim + step * unit
                place = slice(row % piece, row % piece + unit)
                ref[row // piece * heads + head_no, place, :] = (
                    matrix[step * unit : (step + 1) * unit, :] * factor
                )
    for no in range(ref.shape[0]):
        ref[no, piece:, :] = jnp.broadcast_to(exponent, (8, dim))


def load_matrices(ref, dim):
    return [
        ref[no * dim : (no + 1) * dim, :].astype(f32) for no in range(ref.shape[0] // dim)
    ]


def combine_kernel(*refs):
    parts, out_ref = refs[:-1], refs[-1]
    piece = out_ref.shape[0] - 8
    terms = [(ref, no) for ref in parts for no in range(ref.shape[0])]
    exponents = [ref[no, piece : piece + 1, :] for ref, no in terms]
    exponent = exponents[0]
    for other in exponents[1:]:
        exponent = jnp.maximum(exponent, other)
    exponent = exponent + float(math.ceil(math.log2(len(terms))))
    total = None
    for (ref, no), own in zip(terms, exponents):
        term = ref[no, :piece, :] * jnp.exp2(own - exponent)
        total = term if total is None else total + term
    out_ref[:piece, :] = total
    out_ref[piece:, :] = jnp.broadcast_to(exponent, (8, total.shape[1]))


def load_scaled(ref, heads):
    piece, dim = ref.shape[1] - 8, ref.shape[2]
    unit = math.gcd(piece, dim)
    factors = [jnp.exp2(ref[no, piece : piece + 1, :] - TOP) for no in range(ref.shape[0])]
    matrices = []
    for head_no in range(heads):
        for first in range(0, ref.shape[0] // heads * piece, dim):
            chunks = []
            for row in range(first, first + dim, unit):
                no = row // piece * heads + head_no
                chunks.append(ref[no, row % piece : row % piece + unit, :] * factors[no])
            matrices.append(jnp.concatenate(chunks, axis=0))
    return matrices


def exponentials(scores, top, dim):
    return jnp.exp2((scores - top) * (math.log2(math.e) / math.sqrt(dim)))


def within_kernel(
    q_hbm,
    k_hbm,
    v_hbm,
    gate_hbm,
    up_hbm,
    down_hbm,
    q_ref,
    v_ref,
    norm_ref,
    turned_ref,
    weights_ref,
    prob_ref,
    stat_ref,
    k_ref,
    raw_ref,
    sems,
):
    heads, dim = gate_hbm.shape[0], gate_hbm.shape[1]
    frame_len = q_hbm.shape[0]
    pairs = [(q_hbm, q_ref), (k_hbm, k_ref), (v_hbm, v_ref)]
    pairs += [
        (source, raw_ref.at[no * heads : (no + 1) * heads])
        for no, source in enumerate([gate_hbm, up_hbm, down_hbm])
    ]
    copies = [
        pltpu.make_async_copy(source, target, sems.at[no])
        for no, (source, target) in enumerate(pairs)
    ]
    for copy in copies:
        copy.start()
    copies[0].wait()
    copies[1].wait()
    for head_no in range(heads):
        cols = slice(head_no * dim, (head_no + 1) * dim)
        scores = dot(k_ref[:, cols], q_ref[:, cols], across)
        top = jnp.max(scores, axis=0, keepdims=True)
        scores = exponentials(scores, top, dim)
        prob_ref[head_no] = scores
        stat_ref[head_no, 0:1, :] = top
        stat_ref[head_no, 1:2, :] = jnp.sum(scores, axis=0, keepdims=True)
        query = q_ref[:, cols].astype(f32)
        square = jnp.mean(query * query, axis=1, keepdims=True)
        norm_ref[:, cols] = (query * lax.rsqrt(square + 1e-06)).astype(bf16)
    for copy in copies[2:]:
        copy.wait()
    for head_no in range(heads):
        cols = slice(head_no * dim, (head_no + 1) * dim)
        turned_ref[head_no] = v_ref[:, cols].T
        weights_ref[3 * head_no] = raw_ref[head_no]
        weights_ref[3 * head_no + 1] = raw_ref[heads + head_no]
        weights_ref[3 * head_no + 2] = raw_ref[2 * heads + head_no].T


def probs_kernel(scalars, q_ref, past_ref, prob_ref, stat_ref, turned_ref, share_ref, mixed_ref):
    heads, dim, frame_len = turned_ref.shape
    bias = jnp.where(scalars[0] == 0, -1e30, 0.0).astype(f32)
    for head_no in range(heads):
        cols = slice(head_no * dim, (head_no + 1) * dim)
        before = dot(past_ref[:, cols], q_ref[:, cols], across) + bias
        near_top = stat_ref[head_no, 0:1, :]
        top = jnp.maximum(jnp.max(before, axis=0, keepdims=True), near_top)
        before = exponentials(before, top, dim)
        shrink = exponentials(near_top, top, dim)
        total = jnp.sum(before, axis=0, keepdims=True) + stat_ref[head_no, 1:2, :] * shrink
        share = 1.0 / total
        share_ref[head_no] = (before * share).astype(bf16)
        within = (prob_ref[head_no] * (shrink * share)).astype(bf16)
        mixed_ref[head_no] = dot(turned_ref[head_no], within, inside)


def attend_kernel(
    share_ref, mixed_ref, past_ref, v_ref, turned_ref, weights_ref, att_ref, att_t_ref, grad_ref
):
    heads, dim, frame_len = turned_ref.shape
    weights = initial_of(weights_ref)
    grads = []
    for head_no in range(heads):
        cols = slice(head_no * dim, (head_no + 1) * dim)
        mixed = mixed_ref[head_no] + dot(past_ref[:, cols].T, share_ref[head_no], inside)
        square = jnp.mean(mixed * mixed, axis=0, keepdims=True)
        att_t = (mixed * lax.rsqrt(square + 1e-06)).astype(bf16)
        att = att_t.T
        att_t_ref[head_no] = att_t
        att_ref[:, cols] = att
        grads.append(
            fast_grads(
                weights[3 * head_no : 3 * head_no + 3],
                att,
                v_ref[:, cols],
                att_t,
                turned_ref[head_no],
            )
        )
    store_scaled(grad_ref, grads)


def unused_kernel(out_ref):
    out_ref[:, 0:16, :] = jnp.zeros((out_ref.shape[0], 16, out_ref.shape[2]), out_ref.dtype)


def one_head(scalars, weights_ref, dim):
    core = scalars[1].astype(jnp.int32)
    cols = pl.ds(pl.multiple_of(core * dim, dim), dim)
    return core, cols, [weights_ref[3 * core + no] for no in range(3)]


def second_kernel(
    scalars,
    total_ref,
    att_ref,
    att_t_ref,
    v_ref,
    turned_ref,
    other_ref,
    weights_ref,
    weight_ref,
    grad_ref,
):
    heads, dim, frame_len = turned_ref.shape
    core, cols, initial = one_head(scalars, weights_ref, dim)
    weights = renewed(initial, load_scaled(total_ref, 1), initial, [scalars[2 + core]])
    store_matrices(weight_ref, 0, weights)
    grads = fast_grads(
        weights,
        jnp.concatenate([att_ref[:, cols], other_ref[0]], axis=0),
        jnp.concatenate([v_ref[:, cols], other_ref[1]], axis=0),
        jnp.concatenate([att_t_ref[core], other_ref[0].T], axis=1),
        jnp.concatenate([turned_ref[core], other_ref[1].T], axis=1),
    )
    store_scaled(grad_ref, [grads])


def fast_rows(weights, rows, scale):
    gate_w, up_w, down_t = weights
    gate, upward = gate_and_up(rows, gate_w, up_w)
    hidden = gate / (1.0 + jnp.exp(-gate)) * upward
    return (product(parts_of(hidden), parts_of(down_t), across) * scale).astype(bf16)


def store_combined(att_ref, fast, comb_ref, square_ref):
    combined = att_ref[...].astype(f32) + jnp.concatenate(fast, axis=1).astype(f32)
    comb_ref[...] = combined
    square = combined * combined
    ones = jnp.ones((8, square.shape[1]), bf16)
    high, low = parts_of(square)
    square_ref[...] = dot(ones, high, across) + dot(ones, low, across)


def late_kernel(
    scalars, weight_ref, norm_ref, other_ref, total_ref, weights_ref, own_ref, away_ref
):
    frame_len, dim = own_ref.shape
    heads = weights_ref.shape[0] // 3
    core, cols, initial = one_head(scalars, weights_ref, dim)
    weights = renewed(
        load_matrices(weight_ref, dim), load_scaled(total_ref, 1), initial, [scalars[2 + core]]
    )
    rows = jnp.concatenate([norm_ref[:, cols], other_ref[2]], axis=0)
    fast = fast_rows(weights, rows, scalars[2 + heads + core])
    own_ref[...] = fast[:frame_len]
    away_ref[...] = fast[frame_len:]


def merge_kernel(scalars, att_ref, own_ref, back_ref, comb_ref, square_ref):
    first = scalars[1] == 0
    own, back = own_ref[...].astype(f32), back_ref[...].astype(f32)
    fast = [jnp.where(first, own, back), jnp.where(first, back, own)]
    store_combined(att_ref, fast, comb_ref, square_ref)


def early_kernel(scalars, att_ref, norm_ref, total_ref, weights_ref, comb_ref, square_ref):
    dim = weights_ref.shape[1]
    heads = weights_ref.shape[0] // 3
    initial = initial_of(weights_ref)
    steps = [scalars[2 + head_no] for head_no in range(heads)]
    weights = renewed(initial, load_scaled(total_ref, heads), initial, steps)
    fast = [
        fast_rows(
            weights[3 * head_no : 3 * head_no + 3],
            norm_ref[:, head_no * dim : (head_no + 1) * dim],
            scalars[2 + heads + head_no],
        )
        for head_no in range(heads)
    ]
    store_combined(att_ref, fast, comb_ref, square_ref)


def final_kernel(square_ref, comb_ref, gain_ref, out_ref, *, features):
    ones = jnp.ones((square_ref.shape[0], 128), bf16)
    squares = square_ref[...]
    high, low = parts_of(squares)
    first = (((0,), (0,)), ((), ()))
    total = dot(high, ones, first) + dot(low, ones, first)
    scale = lax.rsqrt(total / features + 1e-05)
    for no in range(comb_ref.shape[1] // 128):
        cols = slice(no * 128, (no + 1) * 128)
        out_ref[:, cols] = (comb_ref[:, cols] * scale * gain_ref[:, cols]).astype(bf16)


def call(kernel, outs, *args, scalars=0, hbm=0, scratch=(), flops=0):
    spec = pl.BlockSpec(memory_space=pltpu.VMEM)
    first = [pl.BlockSpec(memory_space=pltpu.SMEM)] * scalars
    first += [pl.BlockSpec(memory_space=pltpu.HBM)] * hbm
    shapes = [jax.ShapeDtypeStruct(*out) for out in outs]
    args = [
        pltpu.with_memory_space_constraint(arg, pltpu.HBM) if scalars <= no < scalars + hbm else arg
        for no, arg in enumerate(args)
    ]
    return pl.pallas_call(
        kernel,
        out_shape=shapes,
        in_specs=first + [spec] * (len(args) - len(first)),
        out_specs=[spec] * len(shapes),
        scratch_shapes=scratch,
        compiler_params=pltpu.CompilerParams(vmem_limit_bytes=40 * 2**20),
        cost_estimate=pl.CostEstimate(flops=flops, bytes_accessed=2**21, transcendentals=0),
    )(*args)


def exchange(array, groups):
    return lax.all_to_all(
        array, "frame", split_axis=0, concat_axis=0, tiled=True, axis_index_groups=groups
    )


def sum_groups(frames):
    cores, chips = 2, frames // 8
    half = chips // 2
    turned = [(i + half) % chips for i in range(chips)]
    orders = [list(range(chips)), turned, turned, list(range(chips))]
    near_groups = [
        [(group * chips + chip) * cores + core for chip in order for core in range(cores)]
        for group, order in enumerate(orders)
    ]
    far_groups = [list(members) for members in zip(*near_groups)]
    return near_groups, far_groups


def shards(
    queries, key_rows, values, gate_init, up_init, down_init, step_size, head_scale, out_gain
):
    frame_len, width = queries.shape
    heads, dim = gate_init.shape[0], gate_init.shape[1]
    frames = lax.axis_size("frame")
    position = lax.axis_index("frame")
    near = frames // 4
    near_groups, far_groups = sum_groups(frames)
    plain_groups = [list(range(near * i, near * i + near)) for i in range(4)]
    rows = 3 * heads * dim
    piece = rows // near
    core = position % heads
    flags = jnp.stack([position, core]).astype(f32)
    scalars = jnp.concatenate([flags, step_size, head_scale])

    route = [(i, i + 1) for i in range(frames - 1)]
    keys_prev = lax.ppermute(key_rows, "frame", route)
    values_prev = lax.ppermute(values, "frame", route)
    turned = (heads, dim, frame_len)
    queries_v, values_v, norms, values_t, weights_v, probs, stats = call(
        within_kernel,
        [
            ((frame_len, width), bf16),
            ((frame_len, width), bf16),
            ((frame_len, width), bf16),
            (turned, bf16),
            ((3 * heads, dim, dim), f32),
            ((heads, frame_len, frame_len), f32),
            ((heads, 8, frame_len), f32),
        ],
        queries,
        key_rows,
        values,
        gate_init,
        up_init,
        down_init,
        hbm=6,
        scratch=[
            pltpu.VMEM((frame_len, width), bf16),
            pltpu.VMEM((3 * heads, dim, dim), f32),
            pltpu.SemaphoreType.DMA((6,)),
        ],
        flops=2 * 10**9,
    )
    shares, mixed = call(
        probs_kernel,
        [((heads, frame_len, frame_len), bf16), (turned, f32)],
        scalars,
        queries_v,
        keys_prev,
        probs,
        stats,
        values_t,
        scalars=1,
        flops=2 * 10**9,
    )
    attended, attended_t, grads = call(
        attend_kernel,
        [((frame_len, width), bf16), (turned, bf16), ((near, piece + 8, dim), f32)],
        shares,
        mixed,
        values_prev,
        values_v,
        values_t,
        weights_v,
        flops=3 * 10**9,
    )

    def combined_of(*parts):
        return call(combine_kernel, [((piece + 8, dim), f32)], *parts)[0]

    def wired(part, copies, groups):
        part = part.astype(f16)
        if copies:
            part = jnp.broadcast_to(part[None], (copies,) + part.shape)
        return exchange(part, groups).astype(f32)

    late = position >= frames // 2
    cores = [(i, i ^ 1) for i in range(frames // 2, frames)]
    def same_core(groups):
        return [group[core_no::heads] for group in groups for core_no in range(heads)]

    def swapped(grads, attended, values, norms):
        each = jnp.stack([attended, values, norms])
        leaving = jnp.where(core == 0, each[:, :, dim:], each[:, :, :dim])
        return jnp.zeros((piece + 8, dim), f32), lax.ppermute(leaving, "frame", cores)

    def summed(grads, attended, values, norms):
        part = combined_of(wired(grads, 0, near_groups))
        return part, call(unused_kernel, [((3, frame_len, dim), bf16)])[0]

    part, other_frame = lax.cond(late, swapped, summed, grads, attended, values_v, norms)
    part = combined_of(wired(part, 4, far_groups)[:2])
    results = [((frame_len, width), f32), ((8, frame_len), f32)]
    quarter = near // heads

    def with_second_sum(
        scalars, part, attended, attended_t, norms, values_v, values_t, other_frame, weights_v
    ):
        weights, grads = call(
            second_kernel,
            [((3 * dim, dim), f32), ((quarter, piece + 8, dim), f32)],
            scalars,
            wired(part, quarter, same_core(near_groups)),
            attended,
            attended_t,
            values_v,
            values_t,
            other_frame,
            weights_v,
            scalars=1,
            flops=4 * 10**9,
        )
        part = combined_of(wired(grads, 0, same_core(plain_groups)))
        pairs = [(i, i ^ near) for i in range(frames // 2, frames)]
        other = lax.ppermute(part.astype(f16), "frame", pairs).astype(f32)
        part = combined_of(part[None], other[None])
        own, away = call(
            late_kernel,
            [((frame_len, dim), bf16)] * 2,
            scalars,
            weights,
            norms,
            other_frame,
            wired(part, quarter, same_core(plain_groups)),
            weights_v,
            scalars=1,
            flops=4 * 10**9,
        )
        back = lax.ppermute(away, "frame", cores)
        return call(merge_kernel, results, scalars, attended, own, back, scalars=1, flops=10**8)

    def with_first_sum(
        scalars, part, attended, attended_t, norms, values_v, values_t, other_frame, weights_v
    ):
        return call(
            early_kernel,
            results,
            scalars,
            attended,
            norms,
            wired(part, near, near_groups),
            weights_v,
            scalars=1,
            flops=4 * 10**9,
        )

    combined, square = lax.cond(
        late,
        with_second_sum,
        with_first_sum,
        scalars,
        part,
        attended,
        attended_t,
        norms,
        values_v,
        values_t,
        other_frame,
        weights_v,
    )
    columns = lax.axis_size("head")
    squares = lax.all_to_all(
        jnp.broadcast_to(square[:1], (columns, frame_len)),
        "head",
        split_axis=0,
        concat_axis=0,
        tiled=True,
    )
    (out,) = call(
        lambda *refs: final_kernel(*refs, features=width * columns),
        [((frame_len, width), bf16)],
        squares,
        combined,
        out_gain[None, :],
    )
    return out


def solution(mesh):
    in_specs = (
        P("frame", "head"),
        P("frame", "head"),
        P("frame", "head"),
        P("head", None, None),
        P("head", None, None),
        P("head", None, None),
        P("head"),
        P("head"),
        P("head"),
    )
    out_specs = P("frame", "head")
    return jax.shard_map(shards, mesh=mesh, in_specs=in_specs, out_specs=out_specs, check_vma=False)
```

```python
import math

import jax
import jax.numpy as jnp
from jax import lax
from jax.experimental import pallas as pl
from jax.experimental.pallas import tpu as pltpu
from jax.sharding import PartitionSpec as P

NS_ITERS = 5
quintic_terms = (3.4445, -4.775, 2.0315)
f32, bf16 = jnp.float32, jnp.bfloat16
f16 = jnp.float16
TOP = 12.0

inside = (((1,), (0,)), ((), ()))
across = (((1,), (1,)), ((), ()))


def dot(a, b, dims):
    return lax.dot_general(a, b, dims, preferred_element_type=f32)


def parts_of(matrix):
    high = matrix.astype(bf16)
    low = (matrix - high.astype(f32)).astype(bf16)
    return high, low


def folded(wide):
    half = wide.shape[1] // 2
    return wide[:, :half] + wide[:, half:]


def product(left, right, dims):
    both = jnp.concatenate(right, 0 if dims == across else 1)
    return folded(dot(left[0], both, dims)) + dot(left[1], right[0], dims)


def newton_schulz(gradients):
    matrices = []
    for gradient in gradients:
        total = jnp.sum(jnp.sum(gradient * gradient, axis=1, keepdims=True), axis=0, keepdims=True)
        matrices.append(gradient / (jnp.sqrt(total) + 1e-07))
    for _ in range(NS_ITERS):
        split = [parts_of(matrix) for matrix in matrices]
        squares = [product(pair, pair, across) for pair in split]
        halves = [parts_of(square) for square in squares]
        quartics = [product(pair, pair, inside) for pair in halves]
        mixings = [
            parts_of(quintic_terms[1] * square + quintic_terms[2] * quartic)
            for square, quartic in zip(squares, quartics)
        ]
        products = [product(pair, other, inside) for pair, other in zip(mixings, split)]
        matrices = [
            quintic_terms[0] * matrix + product for matrix, product in zip(matrices, products)
        ]
    return matrices


def renewed(weights, gradients, initial, steps):
    result = []
    for no, (weight, ortho, first) in enumerate(zip(weights, newton_schulz(gradients), initial)):
        axis = 1 if no % 3 == 2 else 0
        moved = weight - steps[no // 3] * ortho
        target = jnp.sqrt(jnp.sum(first * first, axis=axis, keepdims=True))
        length = jnp.sqrt(jnp.sum(moved * moved, axis=axis, keepdims=True))
        result.append(moved * (target / (length + 1e-06)))
    return result


def gate_and_up(rows, gate_w, up_w):
    gate_parts, up_parts = parts_of(gate_w), parts_of(up_w)
    stacked = jnp.concatenate(
        [jnp.concatenate([gate_parts[i], up_parts[i]], 1) for i in range(2)], 0
    )
    both = dot(jnp.concatenate([rows, rows], 1), stacked, inside)
    dim = gate_w.shape[1]
    return both[:, :dim], both[:, dim:]


def fast_grads(weights, key, value, key_t, value_t):
    gate_w, up_w, down_t = weights
    gate, upward = gate_and_up(key, gate_w, up_w)
    sigma = 1.0 / (1.0 + jnp.exp(-gate))
    active = gate * sigma
    hidden = active * upward
    back = dot(jnp.concatenate([value, value], 1), jnp.concatenate(parts_of(down_t), 0), inside)
    back_gate = back * upward * sigma * (1.0 + gate * (1.0 - sigma))
    back_up = back * active
    gate_parts, up_parts, hidden_parts = parts_of(back_gate), parts_of(back_up), parts_of(hidden)
    dim = key.shape[1]
    both = dot(key_t, jnp.concatenate([gate_parts[0], up_parts[0]], 1), inside)
    both = both + dot(key_t, jnp.concatenate([gate_parts[1], up_parts[1]], 1), inside)
    down = folded(dot(value_t, jnp.concatenate(hidden_parts, 1), inside))
    return -both[:, :dim], -both[:, dim:], -down


def initial_of(weights_ref):
    return [weights_ref[no] for no in range(weights_ref.shape[0])]


def store_matrices(ref, first, matrices):
    for no, matrix in enumerate(matrices):
        rows = matrix.shape[0]
        ref[(first + no) * rows : (first + no + 1) * rows, :] = matrix.astype(ref.dtype)


def store_scaled(ref, per_head):
    heads, dim = len(per_head), per_head[0][0].shape[0]
    piece = ref.shape[1] - 8
    unit = math.gcd(piece, dim)
    matrices = [matrix for group in per_head for matrix in group]
    peak = matrices[0]
    for matrix in matrices[1:]:
        peak = jnp.maximum(jnp.abs(peak), jnp.abs(matrix))
    peak = jnp.max(jnp.max(jnp.abs(peak), axis=1, keepdims=True), axis=0, keepdims=True)
    exponent = jnp.floor(jnp.log2(jnp.maximum(peak, 1e-30)))
    factor = jnp.exp2(TOP - exponent)
    for head_no, group in enumerate(per_head):
        for no, matrix in enumerate(group):
            for step in range(dim // unit):
                row = no * dim + step * unit
                place = slice(row % piece, row % piece + unit)
                ref[row // piece * heads + head_no, place, :] = (
                    matrix[step * unit : (step + 1) * unit, :] * factor
                )
    for no in range(ref.shape[0]):
        ref[no, piece:, :] = jnp.broadcast_to(exponent, (8, dim))


def load_matrices(ref, dim):
    return [
        ref[no * dim : (no + 1) * dim, :].astype(f32) for no in range(ref.shape[0] // dim)
    ]


def combine_kernel(*refs):
    parts, out_ref = refs[:-1], refs[-1]
    piece = out_ref.shape[0] - 8
    terms = [(ref, no) for ref in parts for no in range(ref.shape[0])]
    exponents = [ref[no, piece : piece + 1, :] for ref, no in terms]
    exponent = exponents[0]
    for other in exponents[1:]:
        exponent = jnp.maximum(exponent, other)
    exponent = exponent + float(math.ceil(math.log2(len(terms))))
    total = None
    for (ref, no), own in zip(terms, exponents):
        term = ref[no, :piece, :] * jnp.exp2(own - exponent)
        total = term if total is None else total + term
    out_ref[:piece, :] = total
    out_ref[piece:, :] = jnp.broadcast_to(exponent, (8, total.shape[1]))


def load_scaled(ref, heads):
    piece, dim = ref.shape[1] - 8, ref.shape[2]
    unit = math.gcd(piece, dim)
    factors = [jnp.exp2(ref[no, piece : piece + 1, :] - TOP) for no in range(ref.shape[0])]
    matrices = []
    for head_no in range(heads):
        for first in range(0, ref.shape[0] // heads * piece, dim):
            chunks = []
            for row in range(first, first + dim, unit):
                no = row // piece * heads + head_no
                chunks.append(ref[no, row % piece : row % piece + unit, :] * factors[no])
            matrices.append(jnp.concatenate(chunks, axis=0))
    return matrices


def exponentials(scores, top, dim):
    return jnp.exp2((scores - top) * (math.log2(math.e) / math.sqrt(dim)))


def within_kernel(
    q_hbm,
    k_hbm,
    v_hbm,
    gate_hbm,
    up_hbm,
    down_hbm,
    q_ref,
    v_ref,
    norm_ref,
    turned_ref,
    weights_ref,
    prob_ref,
    stat_ref,
    k_ref,
    raw_ref,
    sems,
):
    heads, dim = gate_hbm.shape[0], gate_hbm.shape[1]
    frame_len = q_hbm.shape[0]
    pairs = [(q_hbm, q_ref), (k_hbm, k_ref), (v_hbm, v_ref)]
    pairs += [
        (source, raw_ref.at[no * heads : (no + 1) * heads])
        for no, source in enumerate([gate_hbm, up_hbm, down_hbm])
    ]
    copies = [
        pltpu.make_async_copy(source, target, sems.at[no])
        for no, (source, target) in enumerate(pairs)
    ]
    for copy in copies:
        copy.start()
    copies[0].wait()
    copies[1].wait()
    for head_no in range(heads):
        cols = slice(head_no * dim, (head_no + 1) * dim)
        scores = dot(k_ref[:, cols], q_ref[:, cols], across)
        top = jnp.max(scores, axis=0, keepdims=True)
        scores = exponentials(scores, top, dim)
        prob_ref[head_no] = scores
        stat_ref[head_no, 0:1, :] = top
        stat_ref[head_no, 1:2, :] = jnp.sum(scores, axis=0, keepdims=True)
        query = q_ref[:, cols].astype(f32)
        square = jnp.mean(query * query, axis=1, keepdims=True)
        norm_ref[:, cols] = (query * lax.rsqrt(square + 1e-06)).astype(bf16)
    for copy in copies[2:]:
        copy.wait()
    for head_no in range(heads):
        cols = slice(head_no * dim, (head_no + 1) * dim)
        turned_ref[head_no] = v_ref[:, cols].T
        weights_ref[3 * head_no] = raw_ref[head_no]
        weights_ref[3 * head_no + 1] = raw_ref[heads + head_no]
        weights_ref[3 * head_no + 2] = raw_ref[2 * heads + head_no].T


def probs_kernel(scalars, q_ref, past_ref, prob_ref, stat_ref, turned_ref, share_ref, mixed_ref):
    heads, dim, frame_len = turned_ref.shape
    bias = jnp.where(scalars[0] == 0, -1e30, 0.0).astype(f32)
    for head_no in range(heads):
        cols = slice(head_no * dim, (head_no + 1) * dim)
        before = dot(past_ref[:, cols], q_ref[:, cols], across) + bias
        near_top = stat_ref[head_no, 0:1, :]
        top = jnp.maximum(jnp.max(before, axis=0, keepdims=True), near_top)
        before = exponentials(before, top, dim)
        shrink = exponentials(near_top, top, dim)
        total = jnp.sum(before, axis=0, keepdims=True) + stat_ref[head_no, 1:2, :] * shrink
        share = 1.0 / total
        share_ref[head_no] = (before * share).astype(bf16)
        within = (prob_ref[head_no] * (shrink * share)).astype(bf16)
        mixed_ref[head_no] = dot(turned_ref[head_no], within, inside)


def attend_kernel(
    share_ref, mixed_ref, past_ref, v_ref, turned_ref, weights_ref, att_ref, att_t_ref, grad_ref
):
    heads, dim, frame_len = turned_ref.shape
    weights = initial_of(weights_ref)
    grads = []
    for head_no in range(heads):
        cols = slice(head_no * dim, (head_no + 1) * dim)
        mixed = mixed_ref[head_no] + dot(past_ref[:, cols].T, share_ref[head_no], inside)
        square = jnp.mean(mixed * mixed, axis=0, keepdims=True)
        att_t = (mixed * lax.rsqrt(square + 1e-06)).astype(bf16)
        att = att_t.T
        att_t_ref[head_no] = att_t
        att_ref[:, cols] = att
        grads.append(
            fast_grads(
                weights[3 * head_no : 3 * head_no + 3],
                att,
                v_ref[:, cols],
                att_t,
                turned_ref[head_no],
            )
        )
    store_scaled(grad_ref, grads)


def unused_kernel(out_ref):
    out_ref[:, 0:16, :] = jnp.zeros((out_ref.shape[0], 16, out_ref.shape[2]), out_ref.dtype)


def one_head(scalars, weights_ref, dim):
    core = scalars[1].astype(jnp.int32)
    cols = pl.ds(pl.multiple_of(core * dim, dim), dim)
    return core, cols, [weights_ref[3 * core + no] for no in range(3)]


def second_kernel(
    scalars,
    total_ref,
    att_ref,
    att_t_ref,
    v_ref,
    turned_ref,
    other_ref,
    weights_ref,
    weight_ref,
    grad_ref,
):
    heads, dim, frame_len = turned_ref.shape
    core, cols, initial = one_head(scalars, weights_ref, dim)
    weights = renewed(initial, load_scaled(total_ref, 1), initial, [scalars[2 + core]])
    store_matrices(weight_ref, 0, weights)
    grads = fast_grads(
        weights,
        jnp.concatenate([att_ref[:, cols], other_ref[0]], axis=0),
        jnp.concatenate([v_ref[:, cols], other_ref[1]], axis=0),
        jnp.concatenate([att_t_ref[core], other_ref[0].T], axis=1),
        jnp.concatenate([turned_ref[core], other_ref[1].T], axis=1),
    )
    store_scaled(grad_ref, [grads])


def fast_rows(weights, rows, scale):
    gate_w, up_w, down_t = weights
    gate, upward = gate_and_up(rows, gate_w, up_w)
    hidden = gate / (1.0 + jnp.exp(-gate)) * upward
    return (product(parts_of(hidden), parts_of(down_t), across) * scale).astype(bf16)


def store_combined(att_ref, fast, comb_ref, square_ref):
    combined = att_ref[...].astype(f32) + jnp.concatenate(fast, axis=1).astype(f32)
    comb_ref[...] = combined
    square = combined * combined
    ones = jnp.ones((8, square.shape[1]), bf16)
    high, low = parts_of(square)
    square_ref[...] = dot(ones, high, across) + dot(ones, low, across)


def late_kernel(
    scalars, weight_ref, norm_ref, other_ref, total_ref, weights_ref, own_ref, away_ref
):
    frame_len, dim = own_ref.shape
    heads = weights_ref.shape[0] // 3
    core, cols, initial = one_head(scalars, weights_ref, dim)
    weights = renewed(
        load_matrices(weight_ref, dim), load_scaled(total_ref, 1), initial, [scalars[2 + core]]
    )
    rows = jnp.concatenate([norm_ref[:, cols], other_ref[2]], axis=0)
    fast = fast_rows(weights, rows, scalars[2 + heads + core])
    own_ref[...] = fast[:frame_len]
    away_ref[...] = fast[frame_len:]


def merge_kernel(scalars, att_ref, own_ref, back_ref, comb_ref, square_ref):
    first = scalars[1] == 0
    own, back = own_ref[...].astype(f32), back_ref[...].astype(f32)
    fast = [jnp.where(first, own, back), jnp.where(first, back, own)]
    store_combined(att_ref, fast, comb_ref, square_ref)


def early_kernel(scalars, att_ref, norm_ref, total_ref, weights_ref, comb_ref, square_ref):
    dim = weights_ref.shape[1]
    heads = weights_ref.shape[0] // 3
    initial = initial_of(weights_ref)
    steps = [scalars[2 + head_no] for head_no in range(heads)]
    weights = renewed(initial, load_scaled(total_ref, heads), initial, steps)
    fast = [
        fast_rows(
            weights[3 * head_no : 3 * head_no + 3],
            norm_ref[:, head_no * dim : (head_no + 1) * dim],
            scalars[2 + heads + head_no],
        )
        for head_no in range(heads)
    ]
    store_combined(att_ref, fast, comb_ref, square_ref)


def final_kernel(square_ref, comb_ref, gain_ref, out_ref, *, features):
    ones = jnp.ones((square_ref.shape[0], 128), bf16)
    squares = square_ref[...]
    high, low = parts_of(squares)
    first = (((0,), (0,)), ((), ()))
    total = dot(high, ones, first) + dot(low, ones, first)
    scale = lax.rsqrt(total / features + 1e-05)
    for no in range(comb_ref.shape[1] // 128):
        cols = slice(no * 128, (no + 1) * 128)
        out_ref[:, cols] = (comb_ref[:, cols] * scale * gain_ref[:, cols]).astype(bf16)


def call(kernel, outs, *args, scalars=0, hbm=0, scratch=(), flops=0):
    spec = pl.BlockSpec(memory_space=pltpu.VMEM)
    first = [pl.BlockSpec(memory_space=pltpu.SMEM)] * scalars
    first += [pl.BlockSpec(memory_space=pltpu.HBM)] * hbm
    shapes = [jax.ShapeDtypeStruct(*out) for out in outs]
    args = [
        pltpu.with_memory_space_constraint(arg, pltpu.HBM) if scalars <= no < scalars + hbm else arg
        for no, arg in enumerate(args)
    ]
    return pl.pallas_call(
        kernel,
        out_shape=shapes,
        in_specs=first + [spec] * (len(args) - len(first)),
        out_specs=[spec] * len(shapes),
        scratch_shapes=scratch,
        compiler_params=pltpu.CompilerParams(vmem_limit_bytes=40 * 2**20),
        cost_estimate=pl.CostEstimate(flops=flops, bytes_accessed=2**21, transcendentals=0),
    )(*args)


def exchange(array, groups):
    return lax.all_to_all(
        array, "frame", split_axis=0, concat_axis=0, tiled=True, axis_index_groups=groups
    )


def sum_groups(frames):
    cores, chips = 2, frames // 8
    half = chips // 2
    turned = [(i + half) % chips for i in range(chips)]
    orders = [list(range(chips)), turned, turned, list(range(chips))]
    near_groups = [
        [(group * chips + chip) * cores + core for chip in order for core in range(cores)]
        for group, order in enumerate(orders)
    ]
    far_groups = [list(members) for members in zip(*near_groups)]
    return near_groups, far_groups


def shards(
    queries, key_rows, values, gate_init, up_init, down_init, step_size, head_scale, out_gain
):
    frame_len, width = queries.shape
    heads, dim = gate_init.shape[0], gate_init.shape[1]
    frames = lax.axis_size("frame")
    position = lax.axis_index("frame")
    near = frames // 4
    near_groups, far_groups = sum_groups(frames)
    plain_groups = [list(range(near * i, near * i + near)) for i in range(4)]
    rows = 3 * heads * dim
    piece = rows // near
    core = position % heads
    flags = jnp.stack([position, core]).astype(f32)
    scalars = jnp.concatenate([flags, step_size, head_scale])

    route = [(i, i + 1) for i in range(frames - 1)]
    keys_prev = lax.ppermute(key_rows, "frame", route)
    values_prev = lax.ppermute(values, "frame", route)
    turned = (heads, dim, frame_len)
    queries_v, values_v, norms, values_t, weights_v, probs, stats = call(
        within_kernel,
        [
            ((frame_len, width), bf16),
            ((frame_len, width), bf16),
            ((frame_len, width), bf16),
            (turned, bf16),
            ((3 * heads, dim, dim), f32),
            ((heads, frame_len, frame_len), f32),
            ((heads, 8, frame_len), f32),
        ],
        queries,
        key_rows,
        values,
        gate_init,
        up_init,
        down_init,
        hbm=6,
        scratch=[
            pltpu.VMEM((frame_len, width), bf16),
            pltpu.VMEM((3 * heads, dim, dim), f32),
            pltpu.SemaphoreType.DMA((6,)),
        ],
        flops=2 * 10**9,
    )
    shares, mixed = call(
        probs_kernel,
        [((heads, frame_len, frame_len), bf16), (turned, f32)],
        scalars,
        queries_v,
        keys_prev,
        probs,
        stats,
        values_t,
        scalars=1,
        flops=2 * 10**9,
    )
    attended, attended_t, grads = call(
        attend_kernel,
        [((frame_len, width), bf16), (turned, bf16), ((near, piece + 8, dim), f32)],
        shares,
        mixed,
        values_prev,
        values_v,
        values_t,
        weights_v,
        flops=3 * 10**9,
    )

    def combined_of(*parts):
        return call(combine_kernel, [((piece + 8, dim), f32)], *parts)[0]

    def wired(part, copies, groups):
        part = part.astype(f16)
        if copies:
            part = jnp.broadcast_to(part[None], (copies,) + part.shape)
        return exchange(part, groups).astype(f32)

    late = position >= frames // 2
    cores = [(i, i ^ 1) for i in range(frames // 2, frames)]
    def same_core(groups):
        return [group[core_no::heads] for group in groups for core_no in range(heads)]

    def swapped(grads, attended, values, norms):
        each = jnp.stack([attended, values, norms])
        leaving = jnp.where(core == 0, each[:, :, dim:], each[:, :, :dim])
        return jnp.zeros((piece + 8, dim), f32), lax.ppermute(leaving, "frame", cores)

    def summed(grads, attended, values, norms):
        part = combined_of(wired(grads, 0, near_groups))
        return part, call(unused_kernel, [((3, frame_len, dim), bf16)])[0]

    part, other_frame = lax.cond(late, swapped, summed, grads, attended, values_v, norms)
    longer = [pair for a, b, c, d in far_groups for pair in ((b, d), (a, c))]
    shorter = [pair for a, b, c, d in far_groups for pair in ((b, c), (a, d))]
    halves = [pair for a, b, _, _ in far_groups for pair in ((a, b), (b, a))]
    leaving = part.astype(f16)
    far_parts = [lax.ppermute(leaving, "frame", route) for route in (longer, shorter)]
    results = [((frame_len, width), f32), ((8, frame_len), f32)]
    quarter = near // heads

    def with_second_sum(
        scalars,
        part,
        far_parts,
        attended,
        attended_t,
        norms,
        values_v,
        values_t,
        other_frame,
        weights_v,
    ):
        part = combined_of(*[far_part.astype(f32)[None] for far_part in far_parts])
        weights, grads = call(
            second_kernel,
            [((3 * dim, dim), f32), ((quarter, piece + 8, dim), f32)],
            scalars,
            wired(part, quarter, same_core(near_groups)),
            attended,
            attended_t,
            values_v,
            values_t,
            other_frame,
            weights_v,
            scalars=1,
            flops=4 * 10**9,
        )
        part = combined_of(wired(grads, 0, same_core(plain_groups)))
        pairs = [(i, i ^ near) for i in range(frames // 2, frames)]
        other = lax.ppermute(part.astype(f16), "frame", pairs).astype(f32)
        part = combined_of(part[None], other[None])
        own, away = call(
            late_kernel,
            [((frame_len, dim), bf16)] * 2,
            scalars,
            weights,
            norms,
            other_frame,
            wired(part, quarter, same_core(plain_groups)),
            weights_v,
            scalars=1,
            flops=4 * 10**9,
        )
        back = lax.ppermute(away, "frame", cores)
        return call(merge_kernel, results, scalars, attended, own, back, scalars=1, flops=10**8)

    def with_first_sum(
        scalars,
        part,
        far_parts,
        attended,
        attended_t,
        norms,
        values_v,
        values_t,
        other_frame,
        weights_v,
    ):
        other = lax.ppermute(part.astype(f16), "frame", halves).astype(f32)
        part = combined_of(part[None], other[None])
        return call(
            early_kernel,
            results,
            scalars,
            attended,
            norms,
            wired(part, near, near_groups),
            weights_v,
            scalars=1,
            flops=4 * 10**9,
        )

    combined, square = lax.cond(
        late,
        with_second_sum,
        with_first_sum,
        scalars,
        part,
        far_parts,
        attended,
        attended_t,
        norms,
        values_v,
        values_t,
        other_frame,
        weights_v,
    )
    columns = lax.axis_size("head")
    squares = lax.all_to_all(
        jnp.broadcast_to(square[:1], (columns, frame_len)),
        "head",
        split_axis=0,
        concat_axis=0,
        tiled=True,
    )
    (out,) = call(
        lambda *refs: final_kernel(*refs, features=width * columns),
        [((frame_len, width), bf16)],
        squares,
        combined,
        out_gain[None, :],
    )
    return out


def solution(mesh):
    in_specs = (
        P("frame", "head"),
        P("frame", "head"),
        P("frame", "head"),
        P("head", None, None),
        P("head", None, None),
        P("head", None, None),
        P("head"),
        P("head"),
        P("head"),
    )
    out_specs = P("frame", "head")
    return jax.shard_map(shards, mesh=mesh, in_specs=in_specs, out_specs=out_specs, check_vma=False)
```

```python
import math

import jax
import jax.numpy as jnp
from jax import lax
from jax.experimental import pallas as pl
from jax.experimental.pallas import tpu as pltpu
from jax.sharding import PartitionSpec as P

NS_ITERS = 5
quintic_terms = (3.4445, -4.775, 2.0315)
f32, bf16 = jnp.float32, jnp.bfloat16
f16 = jnp.float16
TOP = 12.0

inside = (((1,), (0,)), ((), ()))
across = (((1,), (1,)), ((), ()))


def dot(a, b, dims):
    return lax.dot_general(a, b, dims, preferred_element_type=f32)


def parts_of(matrix):
    high = matrix.astype(bf16)
    low = (matrix - high.astype(f32)).astype(bf16)
    return high, low


def folded(wide):
    half = wide.shape[1] // 2
    return wide[:, :half] + wide[:, half:]


def product(left, right, dims):
    both = jnp.concatenate(right, 0 if dims == across else 1)
    return folded(dot(left[0], both, dims)) + dot(left[1], right[0], dims)


def newton_schulz(gradients):
    matrices = []
    for gradient in gradients:
        total = jnp.sum(jnp.sum(gradient * gradient, axis=1, keepdims=True), axis=0, keepdims=True)
        matrices.append(gradient / (jnp.sqrt(total) + 1e-07))
    for _ in range(NS_ITERS):
        split = [parts_of(matrix) for matrix in matrices]
        squares = [product(pair, pair, across) for pair in split]
        halves = [parts_of(square) for square in squares]
        quartics = [product(pair, pair, inside) for pair in halves]
        mixings = [
            parts_of(quintic_terms[1] * square + quintic_terms[2] * quartic)
            for square, quartic in zip(squares, quartics)
        ]
        products = [product(pair, other, inside) for pair, other in zip(mixings, split)]
        matrices = [
            quintic_terms[0] * matrix + product for matrix, product in zip(matrices, products)
        ]
    return matrices


def renewed(weights, gradients, initial, steps):
    result = []
    for no, (weight, ortho, first) in enumerate(zip(weights, newton_schulz(gradients), initial)):
        axis = 1 if no % 3 == 2 else 0
        moved = weight - steps[no // 3] * ortho
        target = jnp.sqrt(jnp.sum(first * first, axis=axis, keepdims=True))
        length = jnp.sqrt(jnp.sum(moved * moved, axis=axis, keepdims=True))
        result.append(moved * (target / (length + 1e-06)))
    return result


def gate_and_up(rows, gate_w, up_w):
    gate_parts, up_parts = parts_of(gate_w), parts_of(up_w)
    stacked = jnp.concatenate(
        [jnp.concatenate([gate_parts[i], up_parts[i]], 1) for i in range(2)], 0
    )
    both = dot(jnp.concatenate([rows, rows], 1), stacked, inside)
    dim = gate_w.shape[1]
    return both[:, :dim], both[:, dim:]


def fast_grads(weights, key, value, key_t, value_t):
    gate_w, up_w, down_t = weights
    gate, upward = gate_and_up(key, gate_w, up_w)
    sigma = 1.0 / (1.0 + jnp.exp(-gate))
    active = gate * sigma
    hidden = active * upward
    back = dot(jnp.concatenate([value, value], 1), jnp.concatenate(parts_of(down_t), 0), inside)
    back_gate = back * upward * sigma * (1.0 + gate * (1.0 - sigma))
    back_up = back * active
    gate_parts, up_parts, hidden_parts = parts_of(back_gate), parts_of(back_up), parts_of(hidden)
    dim = key.shape[1]
    both = dot(key_t, jnp.concatenate([gate_parts[0], up_parts[0]], 1), inside)
    both = both + dot(key_t, jnp.concatenate([gate_parts[1], up_parts[1]], 1), inside)
    down = folded(dot(value_t, jnp.concatenate(hidden_parts, 1), inside))
    return -both[:, :dim], -both[:, dim:], -down


def initial_of(weights_ref):
    return [weights_ref[no] for no in range(weights_ref.shape[0])]


def store_matrices(ref, first, matrices):
    for no, matrix in enumerate(matrices):
        rows = matrix.shape[0]
        ref[(first + no) * rows : (first + no + 1) * rows, :] = matrix.astype(ref.dtype)


def store_scaled(ref, per_head):
    heads, dim = len(per_head), per_head[0][0].shape[0]
    piece = ref.shape[1] - 8
    unit = math.gcd(piece, dim)
    matrices = [matrix for group in per_head for matrix in group]
    peak = matrices[0]
    for matrix in matrices[1:]:
        peak = jnp.maximum(jnp.abs(peak), jnp.abs(matrix))
    peak = jnp.max(jnp.max(jnp.abs(peak), axis=1, keepdims=True), axis=0, keepdims=True)
    exponent = jnp.floor(jnp.log2(jnp.maximum(peak, 1e-30)))
    factor = jnp.exp2(TOP - exponent)
    for head_no, group in enumerate(per_head):
        for no, matrix in enumerate(group):
            for step in range(dim // unit):
                row = no * dim + step * unit
                place = slice(row % piece, row % piece + unit)
                ref[row // piece * heads + head_no, place, :] = (
                    matrix[step * unit : (step + 1) * unit, :] * factor
                )
    for no in range(ref.shape[0]):
        ref[no, piece:, :] = jnp.broadcast_to(exponent, (8, dim))


def load_matrices(ref, dim):
    return [
        ref[no * dim : (no + 1) * dim, :].astype(f32) for no in range(ref.shape[0] // dim)
    ]


def combine_kernel(*refs):
    parts, out_ref = refs[:-1], refs[-1]
    piece = out_ref.shape[0] - 8
    terms = [(ref, no) for ref in parts for no in range(ref.shape[0])]
    exponents = [ref[no, piece : piece + 1, :] for ref, no in terms]
    exponent = exponents[0]
    for other in exponents[1:]:
        exponent = jnp.maximum(exponent, other)
    exponent = exponent + float(math.ceil(math.log2(len(terms))))
    total = None
    for (ref, no), own in zip(terms, exponents):
        term = ref[no, :piece, :] * jnp.exp2(own - exponent)
        total = term if total is None else total + term
    out_ref[:piece, :] = total
    out_ref[piece:, :] = jnp.broadcast_to(exponent, (8, total.shape[1]))


def load_scaled(ref, heads):
    piece, dim = ref.shape[1] - 8, ref.shape[2]
    unit = math.gcd(piece, dim)
    factors = [jnp.exp2(ref[no, piece : piece + 1, :] - TOP) for no in range(ref.shape[0])]
    matrices = []
    for head_no in range(heads):
        for first in range(0, ref.shape[0] // heads * piece, dim):
            chunks = []
            for row in range(first, first + dim, unit):
                no = row // piece * heads + head_no
                chunks.append(ref[no, row % piece : row % piece + unit, :] * factors[no])
            matrices.append(jnp.concatenate(chunks, axis=0))
    return matrices


def exponentials(scores, top, dim):
    return jnp.exp2((scores - top) * (math.log2(math.e) / math.sqrt(dim)))


def within_kernel(
    q_hbm,
    k_hbm,
    v_hbm,
    gate_hbm,
    up_hbm,
    down_hbm,
    q_ref,
    v_ref,
    norm_ref,
    turned_ref,
    weights_ref,
    prob_ref,
    stat_ref,
    k_ref,
    raw_ref,
    sems,
):
    heads, dim = gate_hbm.shape[0], gate_hbm.shape[1]
    frame_len = q_hbm.shape[0]
    pairs = [(q_hbm, q_ref), (k_hbm, k_ref), (v_hbm, v_ref)]
    pairs += [
        (source, raw_ref.at[no * heads : (no + 1) * heads])
        for no, source in enumerate([gate_hbm, up_hbm, down_hbm])
    ]
    copies = [
        pltpu.make_async_copy(source, target, sems.at[no])
        for no, (source, target) in enumerate(pairs)
    ]
    for copy in copies:
        copy.start()
    copies[0].wait()
    copies[1].wait()
    for head_no in range(heads):
        cols = slice(head_no * dim, (head_no + 1) * dim)
        scores = dot(k_ref[:, cols], q_ref[:, cols], across)
        top = jnp.max(scores, axis=0, keepdims=True)
        scores = exponentials(scores, top, dim)
        prob_ref[head_no] = scores
        stat_ref[head_no, 0:1, :] = top
        stat_ref[head_no, 1:2, :] = jnp.sum(scores, axis=0, keepdims=True)
        query = q_ref[:, cols].astype(f32)
        square = jnp.mean(query * query, axis=1, keepdims=True)
        norm_ref[:, cols] = (query * lax.rsqrt(square + 1e-06)).astype(bf16)
    for copy in copies[2:]:
        copy.wait()
    for head_no in range(heads):
        cols = slice(head_no * dim, (head_no + 1) * dim)
        turned_ref[head_no] = v_ref[:, cols].T
        weights_ref[3 * head_no] = raw_ref[head_no]
        weights_ref[3 * head_no + 1] = raw_ref[heads + head_no]
        weights_ref[3 * head_no + 2] = raw_ref[2 * heads + head_no].T


def probs_kernel(scalars, q_ref, past_ref, prob_ref, stat_ref, turned_ref, share_ref, mixed_ref):
    heads, dim, frame_len = turned_ref.shape
    bias = jnp.where(scalars[0] == 0, -1e30, 0.0).astype(f32)
    for head_no in range(heads):
        cols = slice(head_no * dim, (head_no + 1) * dim)
        before = dot(past_ref[:, cols], q_ref[:, cols], across) + bias
        near_top = stat_ref[head_no, 0:1, :]
        top = jnp.maximum(jnp.max(before, axis=0, keepdims=True), near_top)
        before = exponentials(before, top, dim)
        shrink = exponentials(near_top, top, dim)
        total = jnp.sum(before, axis=0, keepdims=True) + stat_ref[head_no, 1:2, :] * shrink
        share = 1.0 / total
        share_ref[head_no] = (before * share).astype(bf16)
        within = (prob_ref[head_no] * (shrink * share)).astype(bf16)
        mixed_ref[head_no] = dot(turned_ref[head_no], within, inside)


def attend_kernel(
    share_ref, mixed_ref, past_ref, v_ref, turned_ref, weights_ref, att_ref, att_t_ref, grad_ref
):
    heads, dim, frame_len = turned_ref.shape
    weights = initial_of(weights_ref)
    grads = []
    for head_no in range(heads):
        cols = slice(head_no * dim, (head_no + 1) * dim)
        mixed = mixed_ref[head_no] + dot(past_ref[:, cols].T, share_ref[head_no], inside)
        square = jnp.mean(mixed * mixed, axis=0, keepdims=True)
        att_t = (mixed * lax.rsqrt(square + 1e-06)).astype(bf16)
        att = att_t.T
        att_t_ref[head_no] = att_t
        att_ref[:, cols] = att
        grads.append(
            fast_grads(
                weights[3 * head_no : 3 * head_no + 3],
                att,
                v_ref[:, cols],
                att_t,
                turned_ref[head_no],
            )
        )
    store_scaled(grad_ref, grads)


def unused_kernel(out_ref):
    out_ref[:, 0:16, :] = jnp.zeros((out_ref.shape[0], 16, out_ref.shape[2]), out_ref.dtype)


def one_head(scalars, weights_ref, dim):
    core = scalars[1].astype(jnp.int32)
    cols = pl.ds(pl.multiple_of(core * dim, dim), dim)
    return core, cols, [weights_ref[3 * core + no] for no in range(3)]


def second_kernel(
    scalars,
    total_ref,
    att_ref,
    att_t_ref,
    v_ref,
    turned_ref,
    other_ref,
    weights_ref,
    weight_ref,
    grad_ref,
):
    heads, dim, frame_len = turned_ref.shape
    core, cols, initial = one_head(scalars, weights_ref, dim)
    weights = renewed(initial, load_scaled(total_ref, 1), initial, [scalars[2 + core]])
    store_matrices(weight_ref, 0, weights)
    grads = fast_grads(
        weights,
        jnp.concatenate([att_ref[:, cols], other_ref[0]], axis=0),
        jnp.concatenate([v_ref[:, cols], other_ref[1]], axis=0),
        jnp.concatenate([att_t_ref[core], other_ref[0].T], axis=1),
        jnp.concatenate([turned_ref[core], other_ref[1].T], axis=1),
    )
    store_scaled(grad_ref, [grads])


def fast_rows(weights, rows, scale):
    gate_w, up_w, down_t = weights
    gate, upward = gate_and_up(rows, gate_w, up_w)
    hidden = gate / (1.0 + jnp.exp(-gate)) * upward
    return (product(parts_of(hidden), parts_of(down_t), across) * scale).astype(bf16)


def store_combined(att_ref, fast, comb_ref, square_ref):
    combined = att_ref[...].astype(f32) + jnp.concatenate(fast, axis=1).astype(f32)
    comb_ref[...] = combined
    square = combined * combined
    ones = jnp.ones((8, square.shape[1]), bf16)
    high, low = parts_of(square)
    square_ref[...] = dot(ones, high, across) + dot(ones, low, across)


def late_kernel(
    scalars, weight_ref, norm_ref, other_ref, total_ref, weights_ref, own_ref, away_ref
):
    frame_len, dim = own_ref.shape
    heads = weights_ref.shape[0] // 3
    core, cols, initial = one_head(scalars, weights_ref, dim)
    weights = renewed(
        load_matrices(weight_ref, dim), load_scaled(total_ref, 1), initial, [scalars[2 + core]]
    )
    rows = jnp.concatenate([norm_ref[:, cols], other_ref[2]], axis=0)
    fast = fast_rows(weights, rows, scalars[2 + heads + core])
    own_ref[...] = fast[:frame_len]
    away_ref[...] = fast[frame_len:]


def merge_kernel(scalars, att_ref, own_ref, back_ref, comb_ref, square_ref):
    first = scalars[1] == 0
    own, back = own_ref[...].astype(f32), back_ref[...].astype(f32)
    fast = [jnp.where(first, own, back), jnp.where(first, back, own)]
    store_combined(att_ref, fast, comb_ref, square_ref)


def early_kernel(scalars, att_ref, norm_ref, total_ref, weights_ref, comb_ref, square_ref):
    dim = weights_ref.shape[1]
    heads = weights_ref.shape[0] // 3
    initial = initial_of(weights_ref)
    steps = [scalars[2 + head_no] for head_no in range(heads)]
    weights = renewed(initial, load_scaled(total_ref, heads), initial, steps)
    fast = [
        fast_rows(
            weights[3 * head_no : 3 * head_no + 3],
            norm_ref[:, head_no * dim : (head_no + 1) * dim],
            scalars[2 + heads + head_no],
        )
        for head_no in range(heads)
    ]
    store_combined(att_ref, fast, comb_ref, square_ref)


def final_kernel(square_ref, comb_ref, gain_ref, out_ref, *, features):
    ones = jnp.ones((square_ref.shape[0], 128), bf16)
    squares = square_ref[...]
    high, low = parts_of(squares)
    first = (((0,), (0,)), ((), ()))
    total = dot(high, ones, first) + dot(low, ones, first)
    scale = lax.rsqrt(total / features + 1e-05)
    for no in range(comb_ref.shape[1] // 128):
        cols = slice(no * 128, (no + 1) * 128)
        out_ref[:, cols] = (comb_ref[:, cols] * scale * gain_ref[:, cols]).astype(bf16)


def call(kernel, outs, *args, scalars=0, hbm=0, scratch=(), flops=0):
    spec = pl.BlockSpec(memory_space=pltpu.VMEM)
    first = [pl.BlockSpec(memory_space=pltpu.SMEM)] * scalars
    first += [pl.BlockSpec(memory_space=pltpu.HBM)] * hbm
    shapes = [jax.ShapeDtypeStruct(*out) for out in outs]
    args = [
        pltpu.with_memory_space_constraint(arg, pltpu.HBM) if scalars <= no < scalars + hbm else arg
        for no, arg in enumerate(args)
    ]
    return pl.pallas_call(
        kernel,
        out_shape=shapes,
        in_specs=first + [spec] * (len(args) - len(first)),
        out_specs=[spec] * len(shapes),
        scratch_shapes=scratch,
        compiler_params=pltpu.CompilerParams(vmem_limit_bytes=40 * 2**20),
        cost_estimate=pl.CostEstimate(flops=flops, bytes_accessed=2**21, transcendentals=0),
    )(*args)


def exchange(array, groups):
    return lax.all_to_all(
        array, "frame", split_axis=0, concat_axis=0, tiled=True, axis_index_groups=groups
    )


def sum_groups(frames):
    cores, chips = 2, frames // 8
    half = chips // 2
    turned = [(i + half) % chips for i in range(chips)]
    orders = [list(range(chips)), turned, turned, list(range(chips))]
    near_groups = [
        [(group * chips + chip) * cores + core for chip in order for core in range(cores)]
        for group, order in enumerate(orders)
    ]
    far_groups = [list(members) for members in zip(*near_groups)]
    return near_groups, far_groups


def shards(
    queries, key_rows, values, gate_init, up_init, down_init, step_size, head_scale, out_gain
):
    frame_len, width = queries.shape
    heads, dim = gate_init.shape[0], gate_init.shape[1]
    frames = lax.axis_size("frame")
    position = lax.axis_index("frame")
    near = frames // 4
    near_groups, far_groups = sum_groups(frames)
    plain_groups = [list(range(near * i, near * i + near)) for i in range(4)]
    rows = 3 * heads * dim
    piece = rows // near
    core = position % heads
    flags = jnp.stack([position, core]).astype(f32)
    scalars = jnp.concatenate([flags, step_size, head_scale])

    route = [(i, i + 1) for i in range(frames - 1)]
    keys_prev = lax.ppermute(key_rows, "frame", route)
    values_prev = lax.ppermute(values, "frame", route)
    turned = (heads, dim, frame_len)
    queries_v, values_v, norms, values_t, weights_v, probs, stats = call(
        within_kernel,
        [
            ((frame_len, width), bf16),
            ((frame_len, width), bf16),
            ((frame_len, width), bf16),
            (turned, bf16),
            ((3 * heads, dim, dim), f32),
            ((heads, frame_len, frame_len), f32),
            ((heads, 8, frame_len), f32),
        ],
        queries,
        key_rows,
        values,
        gate_init,
        up_init,
        down_init,
        hbm=6,
        scratch=[
            pltpu.VMEM((frame_len, width), bf16),
            pltpu.VMEM((3 * heads, dim, dim), f32),
            pltpu.SemaphoreType.DMA((6,)),
        ],
        flops=2 * 10**9,
    )
    shares, mixed = call(
        probs_kernel,
        [((heads, frame_len, frame_len), bf16), (turned, f32)],
        scalars,
        queries_v,
        keys_prev,
        probs,
        stats,
        values_t,
        scalars=1,
        flops=2 * 10**9,
    )
    attended, attended_t, grads = call(
        attend_kernel,
        [((frame_len, width), bf16), (turned, bf16), ((near, piece + 8, dim), f32)],
        shares,
        mixed,
        values_prev,
        values_v,
        values_t,
        weights_v,
        flops=3 * 10**9,
    )

    def combined_of(*parts):
        return call(combine_kernel, [((piece + 8, dim), f32)], *parts)[0]

    def wired(part, copies, groups):
        part = part.astype(f16)
        if copies:
            part = jnp.broadcast_to(part[None], (copies,) + part.shape)
        return exchange(part, groups).astype(f32)

    late = position >= frames // 2
    cores = [(i, i ^ 1) for i in range(frames // 2, frames)]
    def same_core(groups):
        return [group[core_no::heads] for group in groups for core_no in range(heads)]

    def swapped(grads, attended, values, norms):
        each = jnp.stack([attended, values, norms])
        leaving = jnp.where(core == 0, each[:, :, dim:], each[:, :, :dim])
        return jnp.zeros((piece + 8, dim), f32), lax.ppermute(leaving, "frame", cores)

    def summed(grads, attended, values, norms):
        part = combined_of(wired(grads, 0, near_groups))
        return part, call(unused_kernel, [((3, frame_len, dim), bf16)])[0]

    part, other_frame = lax.cond(late, swapped, summed, grads, attended, values_v, norms)
    longer = [pair for a, b, c, d in far_groups for pair in ((b, d), (a, c))]
    shorter = [pair for a, b, c, d in far_groups for pair in ((b, c), (a, d))]
    halves = [pair for a, b, _, _ in far_groups for pair in ((a, b), (b, a))]
    leaving = part.astype(f16)
    far_parts = [lax.ppermute(leaving, "frame", route) for route in (shorter, longer)]
    results = [((frame_len, width), f32), ((8, frame_len), f32)]
    quarter = near // heads

    def with_second_sum(
        scalars,
        part,
        far_parts,
        attended,
        attended_t,
        norms,
        values_v,
        values_t,
        other_frame,
        weights_v,
    ):
        part = combined_of(*[far_part.astype(f32)[None] for far_part in far_parts])
        weights, grads = call(
            second_kernel,
            [((3 * dim, dim), f32), ((quarter, piece + 8, dim), f32)],
            scalars,
            wired(part, quarter, same_core(near_groups)),
            attended,
            attended_t,
            values_v,
            values_t,
            other_frame,
            weights_v,
            scalars=1,
            flops=4 * 10**9,
        )
        part = combined_of(wired(grads, 0, same_core(plain_groups)))
        pairs = [(i, i ^ near) for i in range(frames // 2, frames)]
        other = lax.ppermute(part.astype(f16), "frame", pairs).astype(f32)
        part = combined_of(part[None], other[None])
        own, away = call(
            late_kernel,
            [((frame_len, dim), bf16)] * 2,
            scalars,
            weights,
            norms,
            other_frame,
            wired(part, quarter, same_core(plain_groups)),
            weights_v,
            scalars=1,
            flops=4 * 10**9,
        )
        back = lax.ppermute(away, "frame", cores)
        return call(merge_kernel, results, scalars, attended, own, back, scalars=1, flops=10**8)

    def with_first_sum(
        scalars,
        part,
        far_parts,
        attended,
        attended_t,
        norms,
        values_v,
        values_t,
        other_frame,
        weights_v,
    ):
        other = lax.ppermute(part.astype(f16), "frame", halves).astype(f32)
        part = combined_of(part[None], other[None])
        return call(
            early_kernel,
            results,
            scalars,
            attended,
            norms,
            wired(part, near, near_groups),
            weights_v,
            scalars=1,
            flops=4 * 10**9,
        )

    combined, square = lax.cond(
        late,
        with_second_sum,
        with_first_sum,
        scalars,
        part,
        far_parts,
        attended,
        attended_t,
        norms,
        values_v,
        values_t,
        other_frame,
        weights_v,
    )
    columns = lax.axis_size("head")
    squares = lax.all_to_all(
        jnp.broadcast_to(square[:1], (columns, frame_len)),
        "head",
        split_axis=0,
        concat_axis=0,
        tiled=True,
    )
    (out,) = call(
        lambda *refs: final_kernel(*refs, features=width * columns),
        [((frame_len, width), bf16)],
        squares,
        combined,
        out_gain[None, :],
    )
    return out


def solution(mesh):
    in_specs = (
        P("frame", "head"),
        P("frame", "head"),
        P("frame", "head"),
        P("head", None, None),
        P("head", None, None),
        P("head", None, None),
        P("head"),
        P("head"),
        P("head"),
    )
    out_specs = P("frame", "head")
    return jax.shard_map(shards, mesh=mesh, in_specs=in_specs, out_specs=out_specs, check_vma=False)
```
